512 devices in a mesh: gx: 16 (over y, core), gy: 4 (over x), gz: 8 (over z).
Axes of the slice: x: 4, y: 8, z: 8, core: 2. Of those that a mesh axis runs over, the one named last changes fastest.
Arguments:
- right_side: float32 [64, 512, 512], P('gz', 'gx', 'gy'), may hold values from -6 to 6
- acoef: float32 [64, 512, 512], P('gz', 'gx', 'gy'), may hold values from 0.02 to 0.2
- beta: float32 [64, 512, 512], P('gz', 'gx', 'gy'), may hold values from 0.5 to 4
Outputs:
- solution: float32 [64, 512, 512], P('gz', 'gx', 'gy')
- residual: float32 [64, 512, 512], P('gz', 'gx', 'gy')
The draws below stay inside these ranges and needn't reach their ends.
All inputs are finite; a program needn't handle non-finite values.
Results may differ from the reference program's by a relative error of at most 0.0003.
Values sent between devices are 32-bit elements; how exact they have to be, the bound alone decides.
No kernel may reach another device: no remote copies, remote signals or barrier semaphores. Data moves between devices by JAX's collectives and lax.ppermute only.
A program may use at most 64 MiB of HBM per device.

```python
import math
import jax
import jax.numpy as jnp

LEVELS = 4
SWEEPS = 2
BOTTOM = 16
NZ = 64
NX = 512
NY = 512


def block_scale(key, extent, shards, smallest, top_value):
    def one(position, shards_of):
        draws = jax.random.uniform(jax.random.fold_in(jax.random.fold_in(key, 6), position), (shards_of,), jnp.float32, smallest / len(shards), top_value / len(shards))
        return jnp.repeat(jnp.exp(draws), extent[position] // shards_of).reshape((-1,) + (1,) * (len(extent) - position - 1))

    loudness = one(*shards[0])
    for cut in shards[1:]:
        loudness = loudness * one(*cut)
    return loudness


def gaussian(stream_key, shape, deviation, limit, shards=(), kind=jnp.bfloat16):
    values = jax.random.normal(stream_key, shape, jnp.float32) * deviation
    if len(shards) > 0:
        values = block_scale(stream_key, shape, shards, -0.22, 0.18) * values
    return jnp.clip(values, min=-limit, max=limit).astype(kind)


def setup_inputs(seed: int = 0) -> dict:
    streams_of = jax.random.split(jax.random.key(seed), 4)
    return {
        "right_side": gaussian(streams_of[0], (NZ, NX, NY), 1.0, 6.0, ((0, 8), (1, 16), (2, 4)), jnp.float32),
        "acoef": jnp.clip(jnp.exp(math.log(0.2) - 2.3025851 * jax.random.uniform(streams_of[1], (NZ, NX, NY), jnp.float32) ** block_scale(streams_of[1], (NZ, NX, NY), ((0, 8), (1, 16), (2, 4)), -0.2, 0.2)), 0.02, 0.2),
        "beta": jnp.clip(jnp.exp(math.log(4.0) - 2.0794415 * jax.random.uniform(streams_of[2], (NZ, NX, NY), jnp.float32) ** block_scale(streams_of[2], (NZ, NX, NY), ((0, 8), (1, 16), (2, 4)), -0.2, 0.2)), 0.5, 4.0),
    }


smooth_low = 0.3
bottom_low = 0.05
upper_bound = 2.0
face_scale = 1.0 / 6.0


def neighbours(padded):
    return [padded[:-2, 1:-1, 1:-1], padded[2:, 1:-1, 1:-1],
            padded[1:-1, :-2, 1:-1], padded[1:-1, 2:, 1:-1],
            padded[1:-1, 1:-1, :-2], padded[1:-1, 1:-1, 2:]]


def restrict(values):
    shape = values.shape
    return values.reshape(shape[0] // 2, 2, shape[1] // 2, 2, shape[2] // 2, 2).mean(axis=(1, 3, 5))


def prolong(values):
    return jnp.repeat(jnp.repeat(jnp.repeat(values, 2, axis=0), 2, axis=1), 2, axis=2)


def level_weights(acoef_level, beta_padded, grid_level):
    beta_inner = beta_padded[1:-1, 1:-1, 1:-1]
    scale = face_scale * 0.25 ** grid_level
    weights = [scale * 0.5 * (beta_inner + other) for other in neighbours(beta_padded)]
    diagonal = acoef_level
    for weight in weights:
        diagonal = diagonal + weight
    return weights, diagonal, 1.0 / diagonal


def operate(iterate, padded, weights, diagonal):
    result = diagonal * iterate
    for weight, other in zip(weights, neighbours(padded)):
        result = result - weight * other
    return result


def smooth(iterate, source, apply_level, inverse, sweeps, lower):
    centre = (upper_bound + lower) / 2.0
    half_width = (upper_bound - lower) / 2.0
    sigma_ratio = centre / half_width
    rho_prev = 1.0 / sigma_ratio
    if iterate is None:
        defect = source
    else:
        defect = source - apply_level(iterate)
    update = defect * inverse * (1.0 / centre)
    iterate = update if iterate is None else iterate + update
    for sweep_index in range(1, sweeps):
        defect = source - apply_level(iterate)
        rho_next = 1.0 / (2.0 * sigma_ratio - rho_prev)
        update = (rho_next * rho_prev) * update + (2.0 * rho_next / half_width) * (defect * inverse)
        rho_prev = rho_next
        iterate = iterate + update
    return iterate


def reference(right_side, acoef, beta):
    coarse_list = [(acoef, beta)]
    for grid_level in range(1, LEVELS):
        coarse_list.append((restrict(coarse_list[-1][0]), restrict(coarse_list[-1][1])))
    level_ops = []
    for grid_level in range(LEVELS):
        level_ops.append(level_weights(coarse_list[grid_level][0], jnp.pad(coarse_list[grid_level][1], 1), grid_level))

    def make_apply(grid_level):
        weights, diagonal, inverse = level_ops[grid_level]

        def apply_level(values):
            return operate(values, jnp.pad(values, 1), weights, diagonal)
        return apply_level

    def vcycle(source, grid_level):
        apply_level = make_apply(grid_level)
        inverse = level_ops[grid_level][2]
        if grid_level == LEVELS - 1:
            return smooth(None, source, apply_level, inverse, BOTTOM, bottom_low)
        iterate = smooth(None, source, apply_level, inverse, SWEEPS, smooth_low)
        defect = source - apply_level(iterate)
        iterate = iterate + prolong(vcycle(restrict(defect), grid_level + 1))
        return smooth(iterate, source, apply_level, inverse, SWEEPS, smooth_low)

    solution = vcycle(right_side, 0)
    residual = right_side - make_apply(0)(solution)
    return solution, residual
```

```python
import jax
import jax.numpy as jnp
from jax import lax
from jax.sharding import PartitionSpec as P

LEVELS = 4
SWEEPS = 2
BOTTOM = 16

smooth_low = 0.3
bottom_low = 0.05
upper_bound = 2.0
face_scale = 1.0 / 6.0


def chebyshev(steps, lower):
    centre = (upper_bound + lower) / 2.0
    half_width = (upper_bound - lower) / 2.0
    sigma = centre / half_width
    rho = 1.0 / sigma
    out = [(0.0, 1.0 / centre)]
    for _ in range(1, steps):
        rho_next = 1.0 / (2.0 * sigma - rho)
        out.append((rho_next * rho, 2.0 * rho_next / half_width))
        rho = rho_next
    return out


def halo(values, dim, axis, width):
    peers, length = lax.axis_size(axis), values.shape[dim]
    up = [(i, i + 1) for i in range(peers - 1)]
    down = [(j, i) for i, j in up]
    before = lax.ppermute(lax.slice_in_dim(values, length - width, length, axis=dim), axis, up)
    after = lax.ppermute(lax.slice_in_dim(values, 0, width, axis=dim), axis, down)
    return jnp.concatenate([before, values, after], axis=dim)


def lane_halo(values, axis, width):
    peers, length = lax.axis_size(axis), values.shape[-1]
    up = [(i, i + 1) for i in range(peers - 1)]
    down = [(j, i) for i, j in up]

    def send(part, pairs):
        moved = jnp.swapaxes(part, -1, -2)
        shape = moved.shape
        moved = lax.ppermute(moved.reshape(-1, shape[-1]), axis, pairs)
        return jnp.swapaxes(moved.reshape(shape), -1, -2)

    before = send(values[..., length - width :], up)
    after = send(values[..., :width], down)
    return jnp.concatenate([before, values, after], axis=-1)


def gather(values, dim, axis):
    peers = lax.axis_size(axis)
    copies = jnp.broadcast_to(values[None], (peers,) + values.shape)
    got = lax.all_to_all(copies, axis, 0, 0)
    got = jnp.moveaxis(got, 0, dim)
    shape = values.shape
    return got.reshape(shape[:dim] + (peers * shape[dim],) + shape[dim + 1 :])


def pair_matrix(size):
    return jnp.repeat(jnp.eye(size, dtype=jnp.float32), 2, axis=0)


def restrict(values):
    z, x, y = values.shape
    values = values.reshape(z // 2, 2, x, y)
    values = values[:, 0] + values[:, 1]
    values = jnp.einsum("zxy,yp->zxp", values, pair_matrix(y // 2) * 0.125, precision="highest")
    return jnp.einsum("xq,zxp->zqp", pair_matrix(x // 2), values, precision="highest")


def prolong(values):
    z, x, y = values.shape
    values = jnp.einsum("zxy,py->zxp", values, pair_matrix(y), precision="highest")
    values = jnp.einsum("qx,zxp->zqp", pair_matrix(x), values, precision="highest")
    return jnp.repeat(values, 2, axis=0)


def inner(values, by, z):
    if by == 0:
        return values
    return values[by:-by if z else None, by:-by, by:-by] if z else values[:, by:-by, by:-by]


def neighbours(values, z):
    if not z:
        values = jnp.pad(values, ((1, 1), (0, 0), (0, 0)))
    return [
        values[:-2, 1:-1, 1:-1],
        values[2:, 1:-1, 1:-1],
        values[1:-1, :-2, 1:-1],
        values[1:-1, 2:, 1:-1],
        values[1:-1, 1:-1, :-2],
        values[1:-1, 1:-1, 2:],
    ]


class Level:
    def __init__(self, source, acoef, beta, level, width, z):
        self.z, self.width = z, width
        scale = face_scale * 0.25**level * 0.5
        middle = inner(beta, 1, z)
        weights = [scale * (middle + other) for other in neighbours(beta, z)]
        diagonal = acoef
        for weight in weights:
            diagonal = diagonal + weight
        self.diagonal = diagonal
        self.inverse = jnp.where(middle > 0.0, 1.0 / diagonal, 0.0)
        self.weights = [weight * self.inverse for weight in weights]
        self.scaled = source * self.inverse

    def cut(self, values, to):
        return inner(values, self.width - to, self.z)

    def defect(self, iterate, at):
        result = self.cut(self.scaled, at) - inner(iterate, 1, self.z)
        for weight, other in zip(self.weights, neighbours(iterate, self.z)):
            result = result + self.cut(weight, at) * other
        return result

    def start(self):
        (_, first), (carry, gain) = chebyshev(SWEEPS, smooth_low)
        update = self.scaled * first
        at = self.width - 1
        update_in = inner(update, 1, self.z)
        return update_in + (carry * update_in + gain * self.defect(update, at))

    def residual(self, iterate, at):
        return self.cut(self.diagonal, at) * self.defect(iterate, at)

    def finish(self, iterate, at):
        (_, first), (carry, gain) = chebyshev(SWEEPS, smooth_low)
        update = first * self.defect(iterate, at + 1)
        iterate = inner(iterate, 1, self.z) + update
        update = carry * inner(update, 1, self.z) + gain * self.defect(iterate, at)
        return inner(iterate, 1, self.z) + update


def bottom(source, acoef, beta):
    pad = ((0, 0), (1, 1), (1, 1))
    grid = Level(source, acoef, jnp.pad(beta, pad), LEVELS - 1, 0, False)
    steps = chebyshev(BOTTOM, bottom_low)
    update = grid.scaled * steps[0][1]
    iterate = update
    for carry, gain in steps[1:]:
        update = carry * update + gain * grid.defect(jnp.pad(iterate, pad), 0)
        iterate = iterate + update
    return iterate


def on_device(right_side, acoef, beta):
    wide = jnp.stack([right_side, acoef, beta])
    wide = halo(wide, 1, "gz", 5)
    wide = halo(wide, 2, "gx", 5)
    wide = lane_halo(wide, "gy", 5)
    level0 = Level(inner(wide[0], 1, True), inner(wide[1], 1, True), wide[2], 0, 4, True)
    iterate0 = level0.start()
    coarse = restrict(level0.residual(inner(iterate0, 2, True), 0))

    wide = jnp.stack([coarse, restrict(acoef), restrict(beta)])
    wide = gather(wide, 1, "gz")
    wide = halo(wide, 2, "gx", 13)
    wide = lane_halo(wide, "gy", 13)
    source1, acoef1, beta1 = wide[0], wide[1], wide[2]
    level1 = Level(inner(source1, 1, False), inner(acoef1, 1, False), beta1, 1, 12, False)
    iterate1 = level1.start()
    source2 = restrict(level1.residual(iterate1, 10))
    acoef2 = restrict(inner(acoef1, 3, False))
    beta2 = restrict(inner(beta1, 1, False))

    level2 = Level(source2, acoef2, beta2, 2, 5, False)
    iterate2 = level2.start()
    source3 = restrict(level2.residual(inner(iterate2, 3, False), 0))
    wide = jnp.stack([source3, restrict(inner(acoef2, 5, False)), restrict(inner(beta2, 6, False))])
    wide = gather(wide, 2, "gx")
    wide = gather(wide, 3, "gy")
    error = bottom(wide[0], wide[1], wide[2])

    _, rows, columns = source3.shape
    error = jnp.pad(error, ((0, 0), (2, 2), (2, 2)))
    error = lax.dynamic_slice(
        error,
        (0, lax.axis_index("gx") * rows, lax.axis_index("gy") * columns),
        (error.shape[0], rows + 4, columns + 4),
    )
    iterate2 = level2.finish(iterate2 + prolong(error), 2)
    iterate1 = level1.finish(inner(iterate1, 7, False) + prolong(iterate2), 2)
    planes = coarse.shape[0]
    iterate1 = jnp.pad(iterate1, ((2, 2), (0, 0), (0, 0)))
    iterate1 = lax.dynamic_slice_in_dim(iterate1, lax.axis_index("gz") * planes, planes + 4, axis=0)
    iterate0 = iterate0 + inner(prolong(iterate1), 1, True)
    iterate0 = level0.finish(iterate0, 1)
    return inner(iterate0, 1, True), level0.residual(iterate0, 0)


def solution(mesh):
    spec = P("gz", "gx", "gy")
    return jax.shard_map(
        on_device, mesh=mesh, in_specs=(spec, spec, spec), out_specs=(spec, spec), check_vma=False
    )
```

```python
import functools

import jax
import jax.numpy as jnp
from jax import lax
from jax.experimental import pallas as pl
from jax.experimental.pallas import tpu as pltpu
from jax.sharding import PartitionSpec as P

LEVELS = 4
SWEEPS = 2
BOTTOM = 16

smooth_low = 0.3
bottom_low = 0.05
upper_bound = 2.0
face_scale = 1.0 / 6.0

F32 = jnp.float32
AXES = ("gx", "gy", "gz")
DEEP = 5


def chebyshev(steps, lower):
    centre = (upper_bound + lower) / 2.0
    half_width = (upper_bound - lower) / 2.0
    sigma = centre / half_width
    rho = 1.0 / sigma
    out = [(0.0, 1.0 / centre)]
    for _ in range(1, steps):
        rho_next = 1.0 / (2.0 * sigma - rho)
        out.append((rho_next * rho, 2.0 * rho_next / half_width))
        rho = rho_next
    return out


(_, FIRST), (CARRY, GAIN) = chebyshev(SWEEPS, smooth_low)


def roll(value, shift, axis):
    shift %= value.shape[axis]
    return pltpu.roll(value, shift, axis) if shift else value


def lane_of(shape):
    return lax.broadcasted_iota(jnp.int32, shape, 1)


def row_of(shape):
    return lax.broadcasted_iota(jnp.int32, shape, 0)


def sides(value):
    return [roll(value, 1, 0), roll(value, -1, 0), roll(value, 1, 1), roll(value, -1, 1)]


def scale_of(level):
    return face_scale * 0.25**level * 0.5


def coefficients(beta, below, above, acoef, level):
    weights = [scale_of(level) * (beta + other) for other in [below, above] + sides(beta)]
    diagonal = acoef
    for weight in weights:
        diagonal = diagonal + weight
    inside = beta > 0.0
    inverse = jnp.where(inside, 1.0 / jnp.where(inside, diagonal, 1.0), 0.0)
    return [weight * inverse for weight in weights], diagonal, inverse


def defect(scaled, weights, value, below, above):
    result = scaled - value
    for weight, other in zip(weights, [below, above] + sides(value)):
        result = result + weight * other
    return result


def dot(left, right):
    return jnp.dot(left, right, precision=lax.Precision.HIGHEST, preferred_element_type=F32)


def matrix(shape, rule, value=1.0):
    return jnp.where(rule(row_of(shape), lane_of(shape)), value, 0.0).astype(F32)


def copies(ref, value):
    for index in range(ref.shape[0]):
        ref[index] = value


def pack0(pos, f_ref, a_ref, b_ref, zb, za, xb, xa, whole, left, right):
    planes = f_ref.shape[0]
    has_before, has_after = pos[0] > 0, pos[0] < pos[3] - 1
    for index, ref in enumerate((f_ref, a_ref, b_ref)):
        whole[index, 0:DEEP, 0:32, :] = zb[index]
        whole[index, DEEP : DEEP + planes, 0:32, :] = ref[...]
        whole[index, DEEP + planes :, 0:32, :] = za[index]
        whole[index, :, 32:40, :] = jnp.where(has_after, xa[index], 0.0)
        whole[index, :, 40:48, :] = jnp.where(has_before, xb[index], 0.0)
    depth = planes + 2 * DEEP
    slot = lane_of((48, 128)) // 8
    for tile in range(left.shape[0]):
        low = high = jnp.zeros((48, 128), F32)
        for place in range(min(16, 3 * depth - 16 * tile)):
            index, plane = divmod(16 * tile + place, depth)
            value = whole[index, plane]
            low = jnp.where(slot == place, roll(value, 8 * place, 1), low)
            high = jnp.where(slot == place, roll(value, 8 * place + 8, 1), high)
        left[tile] = low
        right[tile] = high


def unpack0(whole, before, after, ext):
    depth = whole.shape[1]
    lane = lane_of((48, 128))
    for index in range(3):
        for plane in range(depth):
            tile, place = divmod(index * depth + plane, 16)
            ahead = jnp.where(lane < 8, roll(after[tile], -8 * place, 1), 0.0)
            ext[index, plane, :, 0:128] = whole[index, plane]
            ext[index, plane, :, 128:256] = jnp.where(lane >= 120, roll(before[tile], 120 - 8 * place, 1), ahead)


def prepare0(ext, weights, diagonal, scaled):
    @pl.loop(0, diagonal.shape[0])
    def _(plane):
        got, middle, inverse = coefficients(
            ext[2, plane + 1], ext[2, plane], ext[2, plane + 2], ext[1, plane + 1], 0
        )
        for index in range(6):
            weights[index, plane] = got[index]
        diagonal[plane] = middle
        scaled[plane] = ext[0, plane + 1] * inverse


def residual0(weights, diagonal, scaled, value, below, above, at):
    cut = lambda array: array[0:32, 0:128]
    result = scaled[at, 0:32, 0:128] - cut(value)
    for index, other in enumerate([below, above] + sides(value)):
        result = result + weights[index, at, 0:32, 0:128] * cut(other)
    return diagonal[at, 0:32, 0:128] * result


def down0(whole, before, after, iterate, message, ext, weights, diagonal, scaled, start, sums):
    unpack0(whole, before, after, ext)
    prepare0(ext, weights, diagonal, scaled)

    @pl.loop(0, start.shape[0])
    def _(plane):
        start[plane] = FIRST * scaled[plane]

    @pl.loop(0, iterate.shape[0])
    def _(plane):
        value = start[plane + 1]
        got = defect(
            scaled[plane + 1],
            [weights[index, plane + 1] for index in range(6)],
            value,
            start[plane],
            start[plane + 2],
        )
        iterate[plane] = value + (CARRY * value + GAIN * got)

    planes = whole.shape[1] - 2 * DEEP

    def left_over(plane):
        return residual0(
            weights, diagonal, scaled, iterate[plane + 3], iterate[plane + 2], iterate[plane + 4], plane + 4
        )

    half = planes // 2

    @pl.loop(0, half)
    def _(plane):
        sums[plane] = left_over(2 * plane) + left_over(2 * plane + 1)
        for index in (1, 2):
            low = whole[index, DEEP + 2 * plane, 0:32, :]
            sums[index * half + plane] = low + whole[index, DEEP + 2 * plane + 1, 0:32, :]

    count = 3 * half
    tall = [sums[plane, pl.ds(0, 16, stride=2), :] + sums[plane, pl.ds(1, 16, stride=2), :] for plane in range(count)]
    first = jnp.concatenate([value[0:8] for value in tall], axis=0)
    second = jnp.concatenate([value[8:16] for value in tall], axis=0)
    pair = matrix((128, 128), lambda row, lane: lane == row // 2, 0.125)
    other = matrix((128, 128), lambda row, lane: lane == row // 2 + 64, 0.125)
    copies(message, dot(first, pair) + dot(second, other))


def pack1(pos, own, xb, xa, whole, left, right):
    has_before, has_after = pos[0] > 0, pos[0] < pos[3] - 1
    lane = lane_of((8, 128))
    sources, rows = own.shape[0], own.shape[1]
    per = rows // 24
    depth = sources * per

    def spread(value):
        return jnp.where(lane < 64, value, 0.0), jnp.where(lane < 64, roll(value, 64, 1), 0.0)

    @pl.loop(0, sources)
    def _(source):
        for index in range(3):
            for plane in range(per):
                at = (index * per + plane) * 8
                to = index * depth + source * per + plane
                whole[to, 0:8, :], whole[to, 8:16, :] = spread(own[source, at : at + 8, :])
                value = jnp.where(has_after, xa[source, at : at + 8, :], 0.0)
                whole[to, 16:24, :], whole[to, 24:32, :] = spread(value)
                value = jnp.where(has_before, xb[source, at : at + 8, :], 0.0)
                whole[to, 32:40, :], whole[to, 40:48, :] = spread(value)

    slot = lane_of((48, 128)) // 16

    @pl.loop(0, left.shape[0])
    def _(tile):
        low = high = jnp.zeros((48, 128), F32)
        for place in range(8):
            value = whole[8 * tile + place]
            low = jnp.where(slot == place, roll(value, 16 * place, 1), low)
            high = jnp.where(slot == place, roll(value, 16 * place - 48, 1), high)
        left[tile] = low
        right[tile] = high


def pass_all(weights, scaled, value, out, count, combine):
    @pl.loop(0, count)
    def _(plane):
        middle = value[plane + 1]
        got = defect(
            scaled[plane],
            [weights[index, plane] for index in range(6)],
            middle,
            value[plane],
            value[plane + 2],
        )
        out(plane, combine(middle, got))


def prepare(ext, weights, diagonal, scaled, level, offset):
    @pl.loop(0, diagonal.shape[0])
    def _(plane):
        at = plane + offset
        got, middle, inverse = coefficients(ext[2, at], ext[2, at - 1], ext[2, at + 1], ext[1, at], level)
        for index in range(6):
            weights[index, plane] = got[index]
        diagonal[plane] = middle
        scaled[plane] = ext[0, at] * inverse


def down1(
    pos, whole, before, after, window1, window2, message,
    ext1, weights1, diagonal1, scaled1, start1, iterate1, sums1,
    ext2, weights2, diagonal2, scaled2, start2, iterate2, sums2, thin, thick,
):
    depth = whole.shape[0] // 3
    lane = lane_of((48, 128))
    for index in range(3):
        for end in (0, depth + 4):
            for plane in range(4):
                ext1[index, end + plane] = jnp.zeros((48, 128), F32)

    @pl.loop(0, before.shape[0])
    def _(tile):
        for place in range(8):
            at = 8 * tile + place
            index, plane = at // depth, lax.rem(at, depth)
            value = whole[at]
            value = jnp.where((lane >= 64) & (lane < 80), roll(after[tile], 64 - 16 * place, 1), value)
            value = jnp.where(lane >= 112, roll(before[tile], 112 - 16 * place, 1), value)
            ext1[index, plane + 4] = value

    prepare(ext1, weights1, diagonal1, scaled1, 1, 4)
    start1[0] = jnp.zeros((48, 128), F32)
    start1[depth + 1] = jnp.zeros((48, 128), F32)

    @pl.loop(0, depth)
    def _(plane):
        start1[plane + 1] = FIRST * scaled1[plane]

    for end in (0, depth + 4):
        for plane in range(4):
            iterate1[end + plane] = jnp.zeros((48, 128), F32)

    def put1(plane, value):
        iterate1[plane + 4] = value

    pass_all(weights1, scaled1, start1, put1, depth, lambda value, got: value + (CARRY * value + GAIN * got))

    half = depth // 2

    @pl.loop(0, half)
    def _(pair):
        total = None
        for plane in (2 * pair, 2 * pair + 1):
            got = diagonal1[plane] * defect(
                scaled1[plane],
                [weights1[index, plane] for index in range(6)],
                iterate1[plane + 4],
                iterate1[plane + 3],
                iterate1[plane + 5],
            )
            total = got if total is None else total + got
        sums1[pair] = total
        for index in (1, 2):
            sums1[index * half + pair] = ext1[index, 2 * pair + 4] + ext1[index, 2 * pair + 5]

    @pl.loop(0, 3 * half)
    def _(plane):
        thin[plane] = sums1[plane, pl.ds(0, 24, stride=2), :] + sums1[plane, pl.ds(1, 24, stride=2), :]

    def to_level2(row, lane):
        place = jnp.where(lane < 64, lane, lane - 128)
        source = lax.shift_right_arithmetic(jnp.where(row < 96, row, row - 128), 1)
        return (source == place) & ((row < 80) | (row >= 112))

    level2 = matrix((128, 128), to_level2, 0.125)
    for index in range(3):
        values = thin[index * half : (index + 1) * half].reshape(half * 24, 128)
        ext2[index, 4 : 4 + half] = dot(values, level2).reshape(half, 24, 128)
        for end in (0, half + 4):
            for plane in range(4):
                ext2[index, end + plane] = jnp.zeros((24, 128), F32)

    prepare(ext2, weights2, diagonal2, scaled2, 2, 4)
    start2[0] = jnp.zeros((24, 128), F32)
    start2[half + 1] = jnp.zeros((24, 128), F32)

    @pl.loop(0, half)
    def _(plane):
        start2[plane + 1] = FIRST * scaled2[plane]

    for end in (0, half + 4):
        for plane in range(4):
            iterate2[end + plane] = jnp.zeros((24, 128), F32)

    def put2(plane, value):
        iterate2[plane + 4] = value

    pass_all(weights2, scaled2, start2, put2, half, lambda value, got: value + (CARRY * value + GAIN * got))

    quarter = half // 2
    group = quarter // 2
    place2 = [
        matrix((128, 128), lambda row, lane, at=at: (row < 32) & (lane == row // 2 + 16 * at), 0.125)
        for at in range(6)
    ]
    for index in range(3):
        for plane in range(quarter):
            if index == 0:
                total = None
                for at in (2 * plane, 2 * plane + 1):
                    got = diagonal2[at] * defect(
                        scaled2[at],
                        [weights2[face, at] for face in range(6)],
                        iterate2[at + 4],
                        iterate2[at + 3],
                        iterate2[at + 5],
                    )
                    total = got if total is None else total + got
                total = total[0:8]
            else:
                total = ext2[index, 2 * plane + 4, 0:8, :] + ext2[index, 2 * plane + 5, 0:8, :]
            at = index * quarter + plane
            sums2[at] = total
            side, within = divmod(plane, group)
            thick[index * 2 + side, pl.ds(within, 4, stride=group), :] = (
                sums2[at, pl.ds(0, 4, stride=2), :] + sums2[at, pl.ds(1, 4, stride=2), :]
            )
    result = dot(thick[0], place2[0])
    for at in range(1, 6):
        result = result + dot(thick[at], place2[at])
    copies(message, result)

    at1, at2 = pos[2] * 4, pos[2] * 2
    for index in range(3):
        window1[index] = ext1[index, pl.ds(at1, 12)]
        window2[index] = ext2[index, pl.ds(at2, 10)]
    window1[3] = iterate1[pl.ds(at1, 12)]
    window2[3] = iterate2[pl.ds(at2, 10)]


def bottom(gathered, whole, weights, scaled, update, values):
    group = weights.shape[1]
    rows = weights.shape[2]
    for index in range(3):
        total = None
        lane = lane_of(gathered.shape[1:])
        for source in range(4):
            value = gathered[source]
            for side in range(2):
                to = 64 * side + 16 * source
                moved = roll(value, to - 16 * (2 * index + side), 1)
                moved = jnp.where((lane >= to) & (lane < to + 16), moved, 0.0)
                total = moved if total is None else total + moved
        whole[index] = total
    shape = (rows, 128)
    row, lane = row_of(shape), lane_of(shape)
    column = lax.rem(lane, 64)

    def plane_at(index, plane):
        return whole[index, pl.ds(plane, rows, stride=group), :]

    def around(get, plane):
        middle = get(plane)
        below = get(plane - 1) if plane else roll(get(group - 1), 64, 1)
        above = get(plane + 1) if plane < group - 1 else roll(get(0), 64, 1)
        return [below, above] + sides(middle)

    for plane in range(group):
        beta = plane_at(2, plane)
        masks = [
            (lane >= 64) if plane == 0 else None,
            (lane < 64) if plane == group - 1 else None,
            row > 0,
            row < rows - 1,
            column > 0,
            column < 63,
        ]
        near = around(lambda at: plane_at(2, at), plane)
        near = [other if mask is None else jnp.where(mask, other, 0.0) for other, mask in zip(near, masks)]
        faces = [scale_of(3) * (beta + other) for other in near]
        diagonal = plane_at(1, plane)
        for face in faces:
            diagonal = diagonal + face
        inverse = 1.0 / diagonal
        for index, (face, mask) in enumerate(zip(faces, masks)):
            face = face * inverse
            weights[index, plane] = face if mask is None else jnp.where(mask, face, 0.0)
        scaled[plane] = plane_at(0, plane) * inverse

    steps = chebyshev(BOTTOM, bottom_low)
    for plane in range(group):
        value = steps[0][1] * scaled[plane]
        update[plane] = value
        values[0, plane] = value
    for step, (carry, gain) in enumerate(steps[1:]):
        now, later = step % 2, (step + 1) % 2
        for plane in range(group):
            middle = values[now, plane]
            got = scaled[plane] - middle
            for index, other in enumerate(around(lambda at: values[now, at], plane)):
                got = got + weights[index, plane] * other
            moved = carry * update[plane] + gain * got
            update[plane] = moved
            values[later, plane] = middle + moved


def finish(ext, iterate, weights, diagonal, scaled, level, update, middle, put):
    count = iterate.shape[0]
    prepare(ext, weights, diagonal, scaled, level, 1)

    @pl.loop(0, count - 2)
    def _(plane):
        value = iterate[plane + 1]
        got = FIRST * defect(
            scaled[plane],
            [weights[index, plane] for index in range(6)],
            value,
            iterate[plane],
            iterate[plane + 2],
        )
        update[plane] = got
        middle[plane] = value + got

    @pl.loop(0, count - 4)
    def _(plane):
        value = middle[plane + 1]
        got = defect(
            scaled[plane + 1],
            [weights[index, plane + 1] for index in range(6)],
            value,
            middle[plane],
            middle[plane + 2],
        )
        put(plane, value + (CARRY * update[plane + 1] + GAIN * got))


def up(
    pos, gathered, window2, window1, whole0, before0, after0, iterate0, solved, left_over,
    whole3, weights3, scaled3, update3, values3,
    error2, value2, weights2, diagonal2, scaled2, update2, middle2, out2,
    tall1, value1, weights1, diagonal1, scaled1, update1, middle1, out1,
    tall0, ext0, value0, weights0, diagonal0, scaled0, update0, middle0, out0,
):
    bottom(gathered, whole3, weights3, scaled3, update3, values3)
    group, rows = weights3.shape[1], weights3.shape[2]
    at_x, at_y, at_z = 4 * pos[0], 16 * pos[1], pos[2]
    last = (BOTTOM - 1) % 2

    def rows_rule(row, lane):
        place = jnp.where(row < 16, row, row - 24)
        return lane == at_x + lax.shift_right_arithmetic(place, 1)

    pick = matrix((24, rows), rows_rule)
    for plane in range(group):
        got = dot(pick, values3[last, plane])
        for side in range(2):

            def lanes_rule(row, lane, side=side):
                place = jnp.where(lane < 64, lane, lane - 128)
                source = at_y + lax.shift_right_arithmetic(place, 1)
                return (row - 64 * side == source) & (source >= 0) & (source < 64) & ((lane < 40) | (lane >= 120))

            error2[side * group + plane + 2] = dot(got, matrix((128, 128), lanes_rule))
    for end in (0, 2 * group + 2):
        for plane in range(2):
            error2[end + plane] = jnp.zeros((24, 128), F32)

    for plane in range(10):
        value2[plane] = window2[3, plane] + error2[at_z + plane // 2]

    def put2(plane, value):
        out2[plane] = value

    finish(window2, value2, weights2, diagonal2, scaled2, 2, update2, middle2, put2)

    def to_level1(row, lane):
        place = jnp.where(lane < 96, lane, lane - 128)
        source = lax.shift_right_arithmetic(place, 1)
        return (jnp.where(row < 64, row, row - 128) == source) & ((lane < 80) | (lane >= 112))

    wide1 = matrix((128, 128), to_level1)
    for plane in range(6):
        tall1[plane, pl.ds(0, 24, stride=2), :] = out2[plane]
        tall1[plane, pl.ds(1, 24, stride=2), :] = out2[plane]
    spread = dot(tall1[...].reshape(6 * 48, 128), wide1).reshape(6, 48, 128)
    for plane in range(12):
        value1[plane] = window1[3, plane] + spread[plane // 2]

    def put1(plane, value):
        out1[plane] = value

    finish(window1, value1, weights1, diagonal1, scaled1, 1, update1, middle1, put1)

    def to_level0(row, lane):
        place = jnp.where(lane < 192, lane, lane - 256)
        source = lax.shift_right_arithmetic(place, 1)
        return (jnp.where(row < 96, row, row - 128) == source) & ((lane < 136) | (lane >= 248))

    wide0 = matrix((128, 256), to_level0)
    for plane in range(8):
        value = out1[plane]
        tall0[plane, pl.ds(0, 24, stride=2), :] = value[0:24]
        tall0[plane, pl.ds(1, 24, stride=2), :] = value[0:24]
        tall0[plane, pl.ds(40, 4, stride=2), :] = value[44:48]
        tall0[plane, pl.ds(41, 4, stride=2), :] = value[44:48]

    @pl.loop(0, 8)
    def _(plane):
        value = dot(tall0[plane], wide0)
        out0[2 * plane] = value
        out0[2 * plane + 1] = value

    @pl.loop(0, iterate0.shape[0])
    def _(plane):
        value0[plane] = iterate0[plane] + out0[plane + 1]

    unpack0(whole0, before0, after0, ext0)
    prepare0(ext0, weights0, diagonal0, scaled0)
    count = iterate0.shape[0]

    @pl.loop(0, count - 2)
    def _(plane):
        value = value0[plane + 1]
        got = FIRST * defect(
            scaled0[plane + 2],
            [weights0[index, plane + 2] for index in range(6)],
            value,
            value0[plane],
            value0[plane + 2],
        )
        update0[plane] = got
        middle0[plane] = value + got

    @pl.loop(0, count - 4)
    def _(plane):
        value = middle0[plane + 1]
        got = defect(
            scaled0[plane + 3],
            [weights0[index, plane + 3] for index in range(6)],
            value,
            middle0[plane],
            middle0[plane + 2],
        )
        out0[plane] = value + (CARRY * update0[plane + 1] + GAIN * got)

    @pl.loop(0, count - 6)
    def _(plane):
        value = out0[plane + 1]
        solved[plane] = value[0:32, 0:128]
        left_over[plane] = residual0(
            weights0, diagonal0, scaled0, value, out0[plane], out0[plane + 2], plane + 4
        )


def call(body, name, outs, scratch, pos, args):
    vmem = pl.BlockSpec(memory_space=pltpu.VMEM)
    smem = [pl.BlockSpec(memory_space=pltpu.SMEM)] if pos is not None else []
    operands = ([pos] if pos is not None else []) + list(args)
    return pl.pallas_call(
        body,
        name=name,
        out_shape=[jax.ShapeDtypeStruct(shape, F32) for shape in outs],
        in_specs=smem + [vmem] * len(args),
        out_specs=[vmem] * len(outs),
        scratch_shapes=[pltpu.VMEM(shape, F32) for shape in scratch],
        compiler_params=pltpu.CompilerParams(vmem_limit_bytes=40 * 2**20),
    )(*operands)


def exchange(up_values, down_values, axis, ring):
    peers = lax.axis_size(axis)
    up_pairs = [(i, (i + 1) % peers) for i in range(peers if ring else peers - 1)]
    down_pairs = [(j, i) for i, j in up_pairs]
    return lax.ppermute(up_values, axis, up_pairs), lax.ppermute(down_values, axis, down_pairs)


def coefficient_scratch(planes, rows, lanes):
    shape = (planes, rows, lanes)
    return [(6,) + shape, shape, shape]


def on_device(right_side, acoef, beta):
    ranks, turns, files = [lax.axis_size(axis) for axis in AXES]
    pos = jnp.stack([lax.axis_index(axis) for axis in AXES] + [jnp.int32(ranks)]).astype(jnp.int32)
    planes = right_side.shape[0]
    arrays = (right_side, acoef, beta)

    last = jnp.stack([value[planes - DEEP :] for value in arrays])
    first = jnp.stack([value[:DEEP] for value in arrays])
    zb, za = exchange(last, first, "gz", False)
    last = jnp.stack([jnp.concatenate([zb[i, :, 24:], arrays[i][:, 24:], za[i, :, 24:]]) for i in range(3)])
    first = jnp.stack([jnp.concatenate([zb[i, :, :8], arrays[i][:, :8], za[i, :, :8]]) for i in range(3)])
    xb, xa = exchange(last, first, "gx", True)
    depth = planes + 2 * DEEP
    tiles = -(-3 * depth // 16)
    whole0, left, right = call(
        pack0, "pack0", [(3, depth, 48, 128)] + [(tiles, 48, 128)] * 2, [], pos, arrays + (zb, za, xb, xa)
    )
    before0, after0 = exchange(right, left, "gy", False)
    plane0 = (48, 256)
    half = planes // 2
    iterate0, message = call(
        down0,
        "down0",
        [(depth - 4,) + plane0, (files, 3 * half * 8, 128)],
        [(3, depth) + plane0] + coefficient_scratch(depth - 2, *plane0) + [(depth - 2,) + plane0, (3 * half, 32, 128)],
        None,
        (whole0, before0, after0),
    )

    own = lax.all_to_all(message, "gz", 0, 0)
    xb, xa = exchange(own, own, "gx", True)
    depth1 = files * half
    tiles = 3 * depth1 // 8
    whole1, left, right = call(
        pack1, "pack1", [(3 * depth1, 48, 128)] + [(tiles, 48, 128)] * 2, [], pos, (own, xb, xa)
    )
    before1, after1 = exchange(right, left, "gy", False)
    plane1, plane2 = (48, 128), (24, 128)
    depth2 = depth1 // 2
    group = depth2 // 4
    window1, window2, message = call(
        down1,
        "down1",
        [(4, 12) + plane1, (4, 10) + plane2, (ranks, 4 * group, 128)],
        [(3, depth1 + 8) + plane1]
        + coefficient_scratch(depth1, *plane1)
        + [(depth1 + 2,) + plane1, (depth1 + 8,) + plane1, (3 * depth2,) + plane1, (3, depth2 + 8) + plane2]
        + coefficient_scratch(depth2, *plane2)
        + [(depth2 + 2,) + plane2, (depth2 + 8,) + plane2, (3 * depth2 // 2, 8, 128)]
        + [(3 * depth2,) + plane2, (6, 4 * group, 128)],
        pos,
        (whole1, before1, after1),
    )

    gathered = lax.all_to_all(message, "gx", 0, 0)
    gathered = gathered.reshape(1, ranks * 4 * group, 128)
    gathered = jnp.broadcast_to(gathered, (turns,) + gathered.shape[1:])
    gathered = lax.all_to_all(gathered, "gy", 0, 0)

    rows3 = 4 * ranks
    plane3 = (rows3, 128)
    solved, left_over = call(
        up,
        "up",
        [right_side.shape, right_side.shape],
        [(3, rows3 * group, 128), (6, group) + plane3, (group,) + plane3, (group,) + plane3, (2, group) + plane3]
        + [(2 * group + 4,) + plane2, (10,) + plane2]
        + coefficient_scratch(8, *plane2)
        + [(8,) + plane2, (8,) + plane2, (6,) + plane2, (6,) + plane1, (12,) + plane1]
        + coefficient_scratch(10, *plane1)
        + [(10,) + plane1, (10,) + plane1, (8,) + plane1, (8,) + plane1]
        + [(3, depth) + plane0, (depth - 4,) + plane0]
        + coefficient_scratch(depth - 2, *plane0)
        + [(depth - 6,) + plane0, (depth - 6,) + plane0, (depth - 2,) + plane0],
        pos,
        (gathered, window2, window1, whole0, before0, after0, iterate0),
    )
    return solved, left_over


def solution(mesh):
    spec = P("gz", "gx", "gy")
    return jax.shard_map(
        on_device, mesh=mesh, in_specs=(spec, spec, spec), out_specs=(spec, spec), check_vma=False
    )
```

```python
import functools

import jax
import jax.numpy as jnp
from jax import lax
from jax.experimental import pallas as pl
from jax.experimental.pallas import tpu as pltpu
from jax.sharding import PartitionSpec as P

LEVELS = 4
SWEEPS = 2
BOTTOM = 16

smooth_low = 0.3
bottom_low = 0.05
upper_bound = 2.0
face_scale = 1.0 / 6.0

F32 = jnp.float32
AXES = ("gx", "gy", "gz")
DEEP = 5


def chebyshev(steps, lower):
    centre = (upper_bound + lower) / 2.0
    half_width = (upper_bound - lower) / 2.0
    sigma = centre / half_width
    rho = 1.0 / sigma
    out = [(0.0, 1.0 / centre)]
    for _ in range(1, steps):
        rho_next = 1.0 / (2.0 * sigma - rho)
        out.append((rho_next * rho, 2.0 * rho_next / half_width))
        rho = rho_next
    return out


(_, FIRST), (CARRY, GAIN) = chebyshev(SWEEPS, smooth_low)


def roll(value, shift, axis):
    shift %= value.shape[axis]
    return pltpu.roll(value, shift, axis) if shift else value


def lane_of(shape):
    return lax.broadcasted_iota(jnp.int32, shape, 1)


def row_of(shape):
    return lax.broadcasted_iota(jnp.int32, shape, 0)


def sides(value):
    return [roll(value, 1, 0), roll(value, -1, 0), roll(value, 1, 1), roll(value, -1, 1)]


def scale_of(level):
    return face_scale * 0.25**level * 0.5


def coefficients(beta, below, above, acoef, level):
    weights = [scale_of(level) * (beta + other) for other in [below, above] + sides(beta)]
    diagonal = acoef
    for weight in weights:
        diagonal = diagonal + weight
    inside = beta > 0.0
    inverse = jnp.where(inside, 1.0 / jnp.where(inside, diagonal, 1.0), 0.0)
    return [weight * inverse for weight in weights], diagonal, inverse


def defect(scaled, weights, value, below, above):
    result = scaled - value
    for weight, other in zip(weights, [below, above] + sides(value)):
        result = result + weight * other
    return result


def dot(left, right):
    return jnp.dot(left, right, precision=lax.Precision.HIGHEST, preferred_element_type=F32)


def matrix(shape, rule, value=1.0):
    return jnp.where(rule(row_of(shape), lane_of(shape)), value, 0.0).astype(F32)


def copies(ref, value):
    for index in range(ref.shape[0]):
        ref[index] = value


def pack0(pos, f_ref, a_ref, b_ref, zb, za, xb, xa, whole, left, right):
    planes = f_ref.shape[0]
    has_before, has_after = pos[0] > 0, pos[0] < pos[3] - 1
    for index, ref in enumerate((f_ref, a_ref, b_ref)):
        whole[index, 0:DEEP, 0:32, :] = zb[index]
        whole[index, DEEP : DEEP + planes, 0:32, :] = ref[...]
        whole[index, DEEP + planes :, 0:32, :] = za[index]
        whole[index, :, 32:40, :] = jnp.where(has_after, xa[index], 0.0)
        whole[index, :, 40:48, :] = jnp.where(has_before, xb[index], 0.0)
    depth = planes + 2 * DEEP
    slot = lane_of((48, 128)) // 8
    for tile in range(left.shape[0]):
        low = high = jnp.zeros((48, 128), F32)
        for place in range(min(16, 3 * depth - 16 * tile)):
            index, plane = divmod(16 * tile + place, depth)
            value = whole[index, plane]
            low = jnp.where(slot == place, roll(value, 8 * place, 1), low)
            high = jnp.where(slot == place, roll(value, 8 * place + 8, 1), high)
        left[tile] = low
        right[tile] = high


def unpack0(whole, before, after, ext):
    depth = whole.shape[1]
    lane = lane_of((48, 128))
    for index in range(3):
        for plane in range(depth):
            tile, place = divmod(index * depth + plane, 16)
            ahead = jnp.where(lane < 8, roll(after[tile], -8 * place, 1), 0.0)
            ext[index, plane, :, 0:128] = whole[index, plane]
            ext[index, plane, :, 128:256] = jnp.where(lane >= 120, roll(before[tile], 120 - 8 * place, 1), ahead)


U0, U1, U2 = 4, 8, 16


def prepare0(ext, weights, diagonal, scaled):
    @pl.loop(0, diagonal.shape[0], unroll=U0)
    def _(plane):
        got, middle, inverse = coefficients(
            ext[2, plane + 1], ext[2, plane], ext[2, plane + 2], ext[1, plane + 1], 0
        )
        for index in range(6):
            weights[index, plane] = got[index]
        diagonal[plane] = middle
        scaled[plane] = ext[0, plane + 1] * inverse


def residual0(weights, diagonal, scaled, value, below, above, at):
    cut = lambda array: array[0:32, 0:128]
    result = scaled[at, 0:32, 0:128] - cut(value)
    for index, other in enumerate([below, above] + sides(value)):
        result = result + weights[index, at, 0:32, 0:128] * cut(other)
    return diagonal[at, 0:32, 0:128] * result


def down0(whole, before, after, iterate, message, ext, weights, diagonal, scaled, start, sums):
    unpack0(whole, before, after, ext)
    prepare0(ext, weights, diagonal, scaled)

    @pl.loop(0, start.shape[0])
    def _(plane):
        start[plane] = FIRST * scaled[plane]

    @pl.loop(0, iterate.shape[0], unroll=U0)
    def _(plane):
        value = start[plane + 1]
        got = defect(
            scaled[plane + 1],
            [weights[index, plane + 1] for index in range(6)],
            value,
            start[plane],
            start[plane + 2],
        )
        iterate[plane] = value + (CARRY * value + GAIN * got)

    planes = whole.shape[1] - 2 * DEEP

    def left_over(plane):
        return residual0(
            weights, diagonal, scaled, iterate[plane + 3], iterate[plane + 2], iterate[plane + 4], plane + 4
        )

    half = planes // 2

    @pl.loop(0, half, unroll=U0)
    def _(plane):
        sums[plane] = left_over(2 * plane) + left_over(2 * plane + 1)
        for index in (1, 2):
            low = whole[index, DEEP + 2 * plane, 0:32, :]
            sums[index * half + plane] = low + whole[index, DEEP + 2 * plane + 1, 0:32, :]

    count = 3 * half
    tall = [sums[plane, pl.ds(0, 16, stride=2), :] + sums[plane, pl.ds(1, 16, stride=2), :] for plane in range(count)]
    first = jnp.concatenate([value[0:8] for value in tall], axis=0)
    second = jnp.concatenate([value[8:16] for value in tall], axis=0)
    pair = matrix((128, 128), lambda row, lane: lane == row // 2, 0.125)
    other = matrix((128, 128), lambda row, lane: lane == row // 2 + 64, 0.125)
    copies(message, dot(first, pair) + dot(second, other))


def pack1(pos, own, xb, xa, whole, left, right):
    has_before, has_after = pos[0] > 0, pos[0] < pos[3] - 1
    lane = lane_of((8, 128))
    sources, rows = own.shape[0], own.shape[1]
    per = rows // 24
    depth = sources * per

    def spread(value):
        return jnp.where(lane < 64, value, 0.0), jnp.where(lane < 64, roll(value, 64, 1), 0.0)

    @pl.loop(0, sources)
    def _(source):
        for index in range(3):
            for plane in range(per):
                at = (index * per + plane) * 8
                to = index * depth + source * per + plane
                whole[to, 0:8, :], whole[to, 8:16, :] = spread(own[source, at : at + 8, :])
                value = jnp.where(has_after, xa[source, at : at + 8, :], 0.0)
                whole[to, 16:24, :], whole[to, 24:32, :] = spread(value)
                value = jnp.where(has_before, xb[source, at : at + 8, :], 0.0)
                whole[to, 32:40, :], whole[to, 40:48, :] = spread(value)

    slot = lane_of((48, 128)) // 16

    @pl.loop(0, left.shape[0])
    def _(tile):
        low = high = jnp.zeros((48, 128), F32)
        for place in range(8):
            value = whole[8 * tile + place]
            low = jnp.where(slot == place, roll(value, 16 * place, 1), low)
            high = jnp.where(slot == place, roll(value, 16 * place - 48, 1), high)
        left[tile] = low
        right[tile] = high


def pass_all(weights, scaled, value, out, count, combine, unroll):
    @pl.loop(0, count, unroll=unroll)
    def _(plane):
        middle = value[plane + 1]
        got = defect(
            scaled[plane],
            [weights[index, plane] for index in range(6)],
            middle,
            value[plane],
            value[plane + 2],
        )
        out(plane, combine(middle, got))


def prepare(ext, weights, diagonal, scaled, level, offset):
    @pl.loop(0, diagonal.shape[0], unroll=(U0, U1, U2)[level])
    def _(plane):
        at = plane + offset
        got, middle, inverse = coefficients(ext[2, at], ext[2, at - 1], ext[2, at + 1], ext[1, at], level)
        for index in range(6):
            weights[index, plane] = got[index]
        diagonal[plane] = middle
        scaled[plane] = ext[0, at] * inverse


def down1(
    pos, whole, before, after, window1, window2, message,
    ext1, weights1, diagonal1, scaled1, start1, iterate1, sums1,
    ext2, weights2, diagonal2, scaled2, start2, iterate2, sums2, thin, thick,
):
    depth = whole.shape[0] // 3
    lane = lane_of((48, 128))
    for index in range(3):
        for end in (0, depth + 4):
            for plane in range(4):
                ext1[index, end + plane] = jnp.zeros((48, 128), F32)

    @pl.loop(0, before.shape[0])
    def _(tile):
        for place in range(8):
            at = 8 * tile + place
            index, plane = at // depth, lax.rem(at, depth)
            value = whole[at]
            value = jnp.where((lane >= 64) & (lane < 80), roll(after[tile], 64 - 16 * place, 1), value)
            value = jnp.where(lane >= 112, roll(before[tile], 112 - 16 * place, 1), value)
            ext1[index, plane + 4] = value

    prepare(ext1, weights1, diagonal1, scaled1, 1, 4)
    start1[0] = jnp.zeros((48, 128), F32)
    start1[depth + 1] = jnp.zeros((48, 128), F32)

    @pl.loop(0, depth, unroll=U1)
    def _(plane):
        start1[plane + 1] = FIRST * scaled1[plane]

    for end in (0, depth + 4):
        for plane in range(4):
            iterate1[end + plane] = jnp.zeros((48, 128), F32)

    def put1(plane, value):
        iterate1[plane + 4] = value

    pass_all(weights1, scaled1, start1, put1, depth, lambda value, got: value + (CARRY * value + GAIN * got), U1)

    half = depth // 2

    @pl.loop(0, half, unroll=max(1, U1 // 2))
    def _(pair):
        total = None
        for plane in (2 * pair, 2 * pair + 1):
            got = diagonal1[plane] * defect(
                scaled1[plane],
                [weights1[index, plane] for index in range(6)],
                iterate1[plane + 4],
                iterate1[plane + 3],
                iterate1[plane + 5],
            )
            total = got if total is None else total + got
        sums1[pair] = total
        for index in (1, 2):
            sums1[index * half + pair] = ext1[index, 2 * pair + 4] + ext1[index, 2 * pair + 5]

    @pl.loop(0, 3 * half, unroll=8)
    def _(plane):
        thin[plane] = sums1[plane, pl.ds(0, 24, stride=2), :] + sums1[plane, pl.ds(1, 24, stride=2), :]

    def to_level2(row, lane):
        place = jnp.where(lane < 64, lane, lane - 128)
        source = lax.shift_right_arithmetic(jnp.where(row < 96, row, row - 128), 1)
        return (source == place) & ((row < 80) | (row >= 112))

    level2 = matrix((128, 128), to_level2, 0.125)
    for index in range(3):
        values = thin[index * half : (index + 1) * half].reshape(half * 24, 128)
        ext2[index, 4 : 4 + half] = dot(values, level2).reshape(half, 24, 128)
        for end in (0, half + 4):
            for plane in range(4):
                ext2[index, end + plane] = jnp.zeros((24, 128), F32)

    prepare(ext2, weights2, diagonal2, scaled2, 2, 4)
    start2[0] = jnp.zeros((24, 128), F32)
    start2[half + 1] = jnp.zeros((24, 128), F32)

    @pl.loop(0, half)
    def _(plane):
        start2[plane + 1] = FIRST * scaled2[plane]

    for end in (0, half + 4):
        for plane in range(4):
            iterate2[end + plane] = jnp.zeros((24, 128), F32)

    def put2(plane, value):
        iterate2[plane + 4] = value

    pass_all(weights2, scaled2, start2, put2, half, lambda value, got: value + (CARRY * value + GAIN * got), U2)

    quarter = half // 2
    group = quarter // 2
    place2 = [
        matrix((128, 128), lambda row, lane, at=at: (row < 32) & (lane == row // 2 + 16 * at), 0.125)
        for at in range(6)
    ]
    for index in range(3):
        for plane in range(quarter):
            if index == 0:
                total = None
                for at in (2 * plane, 2 * plane + 1):
                    got = diagonal2[at] * defect(
                        scaled2[at],
                        [weights2[face, at] for face in range(6)],
                        iterate2[at + 4],
                        iterate2[at + 3],
                        iterate2[at + 5],
                    )
                    total = got if total is None else total + got
                total = total[0:8]
            else:
                total = ext2[index, 2 * plane + 4, 0:8, :] + ext2[index, 2 * plane + 5, 0:8, :]
            at = index * quarter + plane
            sums2[at] = total
            side, within = divmod(plane, group)
            thick[index * 2 + side, pl.ds(within, 4, stride=group), :] = (
                sums2[at, pl.ds(0, 4, stride=2), :] + sums2[at, pl.ds(1, 4, stride=2), :]
            )
    result = dot(thick[0], place2[0])
    for at in range(1, 6):
        result = result + dot(thick[at], place2[at])
    copies(message, result)

    at1, at2 = pos[2] * 4, pos[2] * 2
    for index in range(3):
        window1[index] = ext1[index, pl.ds(at1, 12)]
        window2[index] = ext2[index, pl.ds(at2, 10)]
    window1[3] = iterate1[pl.ds(at1, 12)]
    window2[3] = iterate2[pl.ds(at2, 10)]


def bottom(gathered, whole, weights, scaled, update, values):
    group = weights.shape[1]
    rows = weights.shape[2]
    for index in range(3):
        total = None
        lane = lane_of(gathered.shape[1:])
        for source in range(4):
            value = gathered[source]
            for side in range(2):
                to = 64 * side + 16 * source
                moved = roll(value, to - 16 * (2 * index + side), 1)
                moved = jnp.where((lane >= to) & (lane < to + 16), moved, 0.0)
                total = moved if total is None else total + moved
        whole[index] = total
    shape = (rows, 128)
    row, lane = row_of(shape), lane_of(shape)
    column = lax.rem(lane, 64)

    def plane_at(index, plane):
        return whole[index, pl.ds(plane, rows, stride=group), :]

    def around(get, plane):
        middle = get(plane)
        below = get(plane - 1) if plane else roll(get(group - 1), 64, 1)
        above = get(plane + 1) if plane < group - 1 else roll(get(0), 64, 1)
        return [below, above] + sides(middle)

    for plane in range(group):
        beta = plane_at(2, plane)
        masks = [
            (lane >= 64) if plane == 0 else None,
            (lane < 64) if plane == group - 1 else None,
            row > 0,
            row < rows - 1,
            column > 0,
            column < 63,
        ]
        near = around(lambda at: plane_at(2, at), plane)
        near = [other if mask is None else jnp.where(mask, other, 0.0) for other, mask in zip(near, masks)]
        faces = [scale_of(3) * (beta + other) for other in near]
        diagonal = plane_at(1, plane)
        for face in faces:
            diagonal = diagonal + face
        inverse = 1.0 / diagonal
        for index, (face, mask) in enumerate(zip(faces, masks)):
            face = face * inverse
            weights[index, plane] = face if mask is None else jnp.where(mask, face, 0.0)
        scaled[plane] = plane_at(0, plane) * inverse

    steps = chebyshev(BOTTOM, bottom_low)
    for plane in range(group):
        value = steps[0][1] * scaled[plane]
        update[plane] = value
        values[0, plane] = value
    for step, (carry, gain) in enumerate(steps[1:]):
        now, later = step % 2, (step + 1) % 2
        for plane in range(group):
            middle = values[now, plane]
            got = scaled[plane] - middle
            for index, other in enumerate(around(lambda at: values[now, at], plane)):
                got = got + weights[index, plane] * other
            moved = carry * update[plane] + gain * got
            update[plane] = moved
            values[later, plane] = middle + moved


def finish(ext, iterate, weights, diagonal, scaled, level, update, middle, put):
    count = iterate.shape[0]
    prepare(ext, weights, diagonal, scaled, level, 1)

    @pl.loop(0, count - 2, unroll=(U0, U1, U2)[level])
    def _(plane):
        value = iterate[plane + 1]
        got = FIRST * defect(
            scaled[plane],
            [weights[index, plane] for index in range(6)],
            value,
            iterate[plane],
            iterate[plane + 2],
        )
        update[plane] = got
        middle[plane] = value + got

    @pl.loop(0, count - 4, unroll=(U0, U1, U2)[level])
    def _(plane):
        value = middle[plane + 1]
        got = defect(
            scaled[plane + 1],
            [weights[index, plane + 1] for index in range(6)],
            value,
            middle[plane],
            middle[plane + 2],
        )
        put(plane, value + (CARRY * update[plane + 1] + GAIN * got))


def up(
    pos, gathered, window2, window1, whole0, before0, after0, iterate0, solved, left_over,
    whole3, weights3, scaled3, update3, values3,
    error2, value2, weights2, diagonal2, scaled2, update2, middle2, out2,
    tall1, value1, weights1, diagonal1, scaled1, update1, middle1, out1,
    tall0, ext0, value0, weights0, diagonal0, scaled0, update0, middle0, out0,
):
    bottom(gathered, whole3, weights3, scaled3, update3, values3)
    group, rows = weights3.shape[1], weights3.shape[2]
    at_x, at_y, at_z = 4 * pos[0], 16 * pos[1], pos[2]
    last = (BOTTOM - 1) % 2

    def rows_rule(row, lane):
        place = jnp.where(row < 16, row, row - 24)
        return lane == at_x + lax.shift_right_arithmetic(place, 1)

    pick = matrix((24, rows), rows_rule)
    for plane in range(group):
        got = dot(pick, values3[last, plane])
        for side in range(2):

            def lanes_rule(row, lane, side=side):
                place = jnp.where(lane < 64, lane, lane - 128)
                source = at_y + lax.shift_right_arithmetic(place, 1)
                return (row - 64 * side == source) & (source >= 0) & (source < 64) & ((lane < 40) | (lane >= 120))

            error2[side * group + plane + 2] = dot(got, matrix((128, 128), lanes_rule))
    for end in (0, 2 * group + 2):
        for plane in range(2):
            error2[end + plane] = jnp.zeros((24, 128), F32)

    for plane in range(10):
        value2[plane] = window2[3, plane] + error2[at_z + plane // 2]

    def put2(plane, value):
        out2[plane] = value

    finish(window2, value2, weights2, diagonal2, scaled2, 2, update2, middle2, put2)

    def to_level1(row, lane):
        place = jnp.where(lane < 96, lane, lane - 128)
        source = lax.shift_right_arithmetic(place, 1)
        return (jnp.where(row < 64, row, row - 128) == source) & ((lane < 80) | (lane >= 112))

    wide1 = matrix((128, 128), to_level1)
    for plane in range(6):
        tall1[plane, pl.ds(0, 24, stride=2), :] = out2[plane]
        tall1[plane, pl.ds(1, 24, stride=2), :] = out2[plane]
    spread = dot(tall1[...].reshape(6 * 48, 128), wide1).reshape(6, 48, 128)
    for plane in range(12):
        value1[plane] = window1[3, plane] + spread[plane // 2]

    def put1(plane, value):
        out1[plane] = value

    finish(window1, value1, weights1, diagonal1, scaled1, 1, update1, middle1, put1)

    def to_level0(row, lane):
        place = jnp.where(lane < 192, lane, lane - 256)
        source = lax.shift_right_arithmetic(place, 1)
        return (jnp.where(row < 96, row, row - 128) == source) & ((lane < 136) | (lane >= 248))

    wide0 = matrix((128, 256), to_level0)
    for plane in range(8):
        value = out1[plane]
        tall0[plane, pl.ds(0, 24, stride=2), :] = value[0:24]
        tall0[plane, pl.ds(1, 24, stride=2), :] = value[0:24]
        tall0[plane, pl.ds(40, 4, stride=2), :] = value[44:48]
        tall0[plane, pl.ds(41, 4, stride=2), :] = value[44:48]

    @pl.loop(0, 8)
    def _(plane):
        value = dot(tall0[plane], wide0)
        out0[2 * plane] = value
        out0[2 * plane + 1] = value

    @pl.loop(0, iterate0.shape[0])
    def _(plane):
        value0[plane] = iterate0[plane] + out0[plane + 1]

    unpack0(whole0, before0, after0, ext0)
    prepare0(ext0, weights0, diagonal0, scaled0)
    count = iterate0.shape[0]

    @pl.loop(0, count - 2, unroll=U0)
    def _(plane):
        value = value0[plane + 1]
        got = FIRST * defect(
            scaled0[plane + 2],
            [weights0[index, plane + 2] for index in range(6)],
            value,
            value0[plane],
            value0[plane + 2],
        )
        update0[plane] = got
        middle0[plane] = value + got

    @pl.loop(0, count - 4, unroll=U0)
    def _(plane):
        value = middle0[plane + 1]
        got = defect(
            scaled0[plane + 3],
            [weights0[index, plane + 3] for index in range(6)],
            value,
            middle0[plane],
            middle0[plane + 2],
        )
        out0[plane] = value + (CARRY * update0[plane + 1] + GAIN * got)

    @pl.loop(0, count - 6, unroll=U0)
    def _(plane):
        value = out0[plane + 1]
        solved[plane] = value[0:32, 0:128]
        left_over[plane] = residual0(
            weights0, diagonal0, scaled0, value, out0[plane], out0[plane + 2], plane + 4
        )


def call(body, name, outs, scratch, pos, args):
    vmem = pl.BlockSpec(memory_space=pltpu.VMEM)
    smem = [pl.BlockSpec(memory_space=pltpu.SMEM)] if pos is not None else []
    operands = ([pos] if pos is not None else []) + list(args)
    return pl.pallas_call(
        body,
        name=name,
        out_shape=[jax.ShapeDtypeStruct(shape, F32) for shape in outs],
        in_specs=smem + [vmem] * len(args),
        out_specs=[vmem] * len(outs),
        scratch_shapes=[pltpu.VMEM(shape, F32) for shape in scratch],
        compiler_params=pltpu.CompilerParams(vmem_limit_bytes=40 * 2**20),
    )(*operands)


def exchange(up_values, down_values, axis, ring):
    peers = lax.axis_size(axis)
    up_pairs = [(i, (i + 1) % peers) for i in range(peers if ring else peers - 1)]
    down_pairs = [(j, i) for i, j in up_pairs]
    return lax.ppermute(up_values, axis, up_pairs), lax.ppermute(down_values, axis, down_pairs)


def coefficient_scratch(planes, rows, lanes):
    shape = (planes, rows, lanes)
    return [(6,) + shape, shape, shape]


def on_device(right_side, acoef, beta):
    ranks, turns, files = [lax.axis_size(axis) for axis in AXES]
    pos = jnp.stack([lax.axis_index(axis) for axis in AXES] + [jnp.int32(ranks)]).astype(jnp.int32)
    planes = right_side.shape[0]
    arrays = (right_side, acoef, beta)

    last = jnp.stack([value[planes - DEEP :] for value in arrays])
    first = jnp.stack([value[:DEEP] for value in arrays])
    zb, za = exchange(last, first, "gz", False)
    last = jnp.stack([jnp.concatenate([zb[i, :, 24:], arrays[i][:, 24:], za[i, :, 24:]]) for i in range(3)])
    first = jnp.stack([jnp.concatenate([zb[i, :, :8], arrays[i][:, :8], za[i, :, :8]]) for i in range(3)])
    xb, xa = exchange(last, first, "gx", True)
    depth = planes + 2 * DEEP
    tiles = -(-3 * depth // 16)
    whole0, left, right = call(
        pack0, "pack0", [(3, depth, 48, 128)] + [(tiles, 48, 128)] * 2, [], pos, arrays + (zb, za, xb, xa)
    )
    before0, after0 = exchange(right, left, "gy", False)
    plane0 = (48, 256)
    half = planes // 2
    iterate0, message = call(
        down0,
        "down0",
        [(depth - 4,) + plane0, (files, 3 * half * 8, 128)],
        [(3, depth) + plane0] + coefficient_scratch(depth - 2, *plane0) + [(depth - 2,) + plane0, (3 * half, 32, 128)],
        None,
        (whole0, before0, after0),
    )

    own = lax.all_to_all(message, "gz", 0, 0)
    xb, xa = exchange(own, own, "gx", True)
    depth1 = files * half
    tiles = 3 * depth1 // 8
    whole1, left, right = call(
        pack1, "pack1", [(3 * depth1, 48, 128)] + [(tiles, 48, 128)] * 2, [], pos, (own, xb, xa)
    )
    before1, after1 = exchange(right, left, "gy", False)
    plane1, plane2 = (48, 128), (24, 128)
    depth2 = depth1 // 2
    group = depth2 // 4
    window1, window2, message = call(
        down1,
        "down1",
        [(4, 12) + plane1, (4, 10) + plane2, (ranks, 4 * group, 128)],
        [(3, depth1 + 8) + plane1]
        + coefficient_scratch(depth1, *plane1)
        + [(depth1 + 2,) + plane1, (depth1 + 8,) + plane1, (3 * depth2,) + plane1, (3, depth2 + 8) + plane2]
        + coefficient_scratch(depth2, *plane2)
        + [(depth2 + 2,) + plane2, (depth2 + 8,) + plane2, (3 * depth2 // 2, 8, 128)]
        + [(3 * depth2,) + plane2, (6, 4 * group, 128)],
        pos,
        (whole1, before1, after1),
    )

    gathered = lax.all_to_all(message, "gx", 0, 0)
    gathered = gathered.reshape(1, ranks * 4 * group, 128)
    gathered = jnp.broadcast_to(gathered, (turns,) + gathered.shape[1:])
    gathered = lax.all_to_all(gathered, "gy", 0, 0)

    rows3 = 4 * ranks
    plane3 = (rows3, 128)
    solved, left_over = call(
        up,
        "up",
        [right_side.shape, right_side.shape],
        [(3, rows3 * group, 128), (6, group) + plane3, (group,) + plane3, (group,) + plane3, (2, group) + plane3]
        + [(2 * group + 4,) + plane2, (10,) + plane2]
        + coefficient_scratch(8, *plane2)
        + [(8,) + plane2, (8,) + plane2, (6,) + plane2, (6,) + plane1, (12,) + plane1]
        + coefficient_scratch(10, *plane1)
        + [(10,) + plane1, (10,) + plane1, (8,) + plane1, (8,) + plane1]
        + [(3, depth) + plane0, (depth - 4,) + plane0]
        + coefficient_scratch(depth - 2, *plane0)
        + [(depth - 6,) + plane0, (depth - 6,) + plane0, (depth - 2,) + plane0],
        pos,
        (gathered, window2, window1, whole0, before0, after0, iterate0),
    )
    return solved, left_over


def solution(mesh):
    spec = P("gz", "gx", "gy")
    return jax.shard_map(
        on_device, mesh=mesh, in_specs=(spec, spec, spec), out_specs=(spec, spec), check_vma=False
    )
```

```python
import functools

import jax
import jax.numpy as jnp
from jax import lax
from jax.experimental import pallas as pl
from jax.experimental.pallas import tpu as pltpu
from jax.sharding import PartitionSpec as P

LEVELS = 4
SWEEPS = 2
BOTTOM = 16

smooth_low = 0.3
bottom_low = 0.05
upper_bound = 2.0
face_scale = 1.0 / 6.0

F32 = jnp.float32
AXES = ("gx", "gy", "gz")
DEEP = 5


def chebyshev(steps, lower):
    centre = (upper_bound + lower) / 2.0
    half_width = (upper_bound - lower) / 2.0
    sigma = centre / half_width
    rho = 1.0 / sigma
    out = [(0.0, 1.0 / centre)]
    for _ in range(1, steps):
        rho_next = 1.0 / (2.0 * sigma - rho)
        out.append((rho_next * rho, 2.0 * rho_next / half_width))
        rho = rho_next
    return out


(_, FIRST), (CARRY, GAIN) = chebyshev(SWEEPS, smooth_low)


def roll(value, shift, axis):
    shift %= value.shape[axis]
    return pltpu.roll(value, shift, axis) if shift else value


def lane_of(shape):
    return lax.broadcasted_iota(jnp.int32, shape, 1)


def row_of(shape):
    return lax.broadcasted_iota(jnp.int32, shape, 0)


def sides(value):
    return [roll(value, 1, 0), roll(value, -1, 0), roll(value, 1, 1), roll(value, -1, 1)]


def scale_of(level):
    return face_scale * 0.25**level * 0.5


def coefficients(beta, below, above, acoef, level):
    weights = [scale_of(level) * (beta + other) for other in [below, above] + sides(beta)]
    diagonal = acoef
    for weight in weights:
        diagonal = diagonal + weight
    inside = beta > 0.0
    inverse = jnp.where(inside, 1.0 / jnp.where(inside, diagonal, 1.0), 0.0)
    return [weight * inverse for weight in weights], diagonal, inverse


def defect(scaled, weights, value, below, above):
    result = scaled - value
    for weight, other in zip(weights, [below, above] + sides(value)):
        result = result + weight * other
    return result


def dot(left, right):
    return jnp.dot(left, right, precision=lax.Precision.HIGHEST, preferred_element_type=F32)


def matrix(shape, rule, value=1.0):
    return jnp.where(rule(row_of(shape), lane_of(shape)), value, 0.0).astype(F32)


def copies(ref, value):
    for index in range(ref.shape[0]):
        ref[index] = value


def pack0(pos, f_ref, a_ref, b_ref, zb, za, xb, xa, whole, left, right):
    planes = f_ref.shape[0]
    has_before, has_after = pos[0] > 0, pos[0] < pos[3] - 1
    for index, ref in enumerate((f_ref, a_ref, b_ref)):
        whole[index, 0:DEEP, 0:32, :] = zb[index]
        whole[index, DEEP : DEEP + planes, 0:32, :] = ref[...]
        whole[index, DEEP + planes :, 0:32, :] = za[index]
        whole[index, :, 32:40, :] = jnp.where(has_after, xa[index], 0.0)
        whole[index, :, 40:48, :] = jnp.where(has_before, xb[index], 0.0)
    depth = planes + 2 * DEEP
    slot = lane_of((48, 128)) // 8
    for tile in range(left.shape[0]):
        low = high = jnp.zeros((48, 128), F32)
        for place in range(min(16, 3 * depth - 16 * tile)):
            index, plane = divmod(16 * tile + place, depth)
            value = whole[index, plane]
            low = jnp.where(slot == place, roll(value, 8 * place, 1), low)
            high = jnp.where(slot == place, roll(value, 8 * place + 8, 1), high)
        left[tile] = low
        right[tile] = high


def unpack0(whole, before, after, ext):
    depth = whole.shape[1]
    lane = lane_of((48, 128))
    for index in range(3):
        for plane in range(depth):
            tile, place = divmod(index * depth + plane, 16)
            ahead = jnp.where(lane < 8, roll(after[tile], -8 * place, 1), 0.0)
            ext[index, plane, :, 0:128] = whole[index, plane]
            ext[index, plane, :, 128:256] = jnp.where(lane >= 120, roll(before[tile], 120 - 8 * place, 1), ahead)


def planes_of(count, level, start=0):
    most = (7, 10, 16)[level]
    return pl.loop(start, start + count, unroll=max(n for n in range(1, most + 1) if count % n == 0))


def prepare0(ext, weights, diagonal, scaled):
    @planes_of(diagonal.shape[0], 0)
    def _(plane):
        got, middle, inverse = coefficients(
            ext[2, plane + 1], ext[2, plane], ext[2, plane + 2], ext[1, plane + 1], 0
        )
        for index in range(6):
            weights[index, plane] = got[index]
        diagonal[plane] = middle
        scaled[plane] = ext[0, plane + 1] * inverse


def residual0(weights, diagonal, scaled, value, below, above, at):
    cut = lambda array: array[0:32, 0:128]
    result = scaled[at, 0:32, 0:128] - cut(value)
    for index, other in enumerate([below, above] + sides(value)):
        result = result + weights[index, at, 0:32, 0:128] * cut(other)
    return diagonal[at, 0:32, 0:128] * result


def down0(whole, before, after, iterate, message, weights, diagonal, scaled, ext, start, sums):
    unpack0(whole, before, after, ext)
    prepare0(ext, weights, diagonal, scaled)

    @planes_of(start.shape[0], 0)
    def _(plane):
        start[plane] = FIRST * scaled[plane]

    @planes_of(iterate.shape[0], 0)
    def _(plane):
        value = start[plane + 1]
        got = defect(
            scaled[plane + 1],
            [weights[index, plane + 1] for index in range(6)],
            value,
            start[plane],
            start[plane + 2],
        )
        iterate[plane] = value + (CARRY * value + GAIN * got)

    planes = whole.shape[1] - 2 * DEEP

    def left_over(plane):
        return residual0(
            weights, diagonal, scaled, iterate[plane + 3], iterate[plane + 2], iterate[plane + 4], plane + 4
        )

    half = planes // 2

    @planes_of(half, 0)
    def _(plane):
        sums[plane] = left_over(2 * plane) + left_over(2 * plane + 1)
        for index in (1, 2):
            low = whole[index, DEEP + 2 * plane, 0:32, :]
            sums[index * half + plane] = low + whole[index, DEEP + 2 * plane + 1, 0:32, :]

    count = 3 * half
    tall = [sums[plane, pl.ds(0, 16, stride=2), :] + sums[plane, pl.ds(1, 16, stride=2), :] for plane in range(count)]
    first = jnp.concatenate([value[0:8] for value in tall], axis=0)
    second = jnp.concatenate([value[8:16] for value in tall], axis=0)
    pair = matrix((128, 128), lambda row, lane: lane == row // 2, 0.125)
    other = matrix((128, 128), lambda row, lane: lane == row // 2 + 64, 0.125)
    copies(message, dot(first, pair) + dot(second, other))


def pack1(pos, own, xb, xa, whole, left, right):
    has_before, has_after = pos[0] > 0, pos[0] < pos[3] - 1
    lane = lane_of((8, 128))
    sources, rows = own.shape[0], own.shape[1]
    per = rows // 24
    depth = sources * per

    def spread(value):
        return jnp.where(lane < 64, value, 0.0), jnp.where(lane < 64, roll(value, 64, 1), 0.0)

    @pl.loop(0, sources, unroll=2)
    def _(source):
        for index in range(3):
            for plane in range(per):
                at = (index * per + plane) * 8
                to = index * depth + source * per + plane
                whole[to, 0:8, :], whole[to, 8:16, :] = spread(own[source, at : at + 8, :])
                value = jnp.where(has_after, xa[source, at : at + 8, :], 0.0)
                whole[to, 16:24, :], whole[to, 24:32, :] = spread(value)
                value = jnp.where(has_before, xb[source, at : at + 8, :], 0.0)
                whole[to, 32:40, :], whole[to, 40:48, :] = spread(value)

    slot = lane_of((48, 128)) // 16

    @pl.loop(0, left.shape[0], unroll=2)
    def _(tile):
        low = high = jnp.zeros((48, 128), F32)
        for place in range(8):
            value = whole[8 * tile + place]
            low = jnp.where(slot == place, roll(value, 16 * place, 1), low)
            high = jnp.where(slot == place, roll(value, 16 * place - 48, 1), high)
        left[tile] = low
        right[tile] = high


def pass_all(weights, scaled, value, out, count, combine, level):
    @planes_of(count, level)
    def _(plane):
        middle = value[plane + 1]
        got = defect(
            scaled[plane + 4],
            [weights[index, plane + 4] for index in range(6)],
            middle,
            value[plane],
            value[plane + 2],
        )
        out(plane, combine(middle, got))


def prepare(ext, weights, diagonal, scaled, level):
    shape = scaled.shape[1:]
    count = scaled.shape[0] - 8
    for end in (0, count + 4):
        for plane in range(4):
            scaled[end + plane] = jnp.zeros(shape, F32)
            for index in range(6):
                weights[index, end + plane] = jnp.zeros(shape, F32)

    @planes_of(count, level, 4)
    def _(at):
        got, middle, inverse = coefficients(ext[2, at], ext[2, at - 1], ext[2, at + 1], ext[1, at], level)
        for index in range(6):
            weights[index, at] = got[index]
        diagonal[at] = middle
        scaled[at] = ext[0, at] * inverse


def down1(
    whole, before, after, message, weights1, scaled1, iterate1, weights2, scaled2, iterate2,
    ext1, diagonal1, start1, sums1, ext2, diagonal2, start2, sums2, thin, thick,
):
    depth = whole.shape[0] // 3
    lane = lane_of((48, 128))
    for index in range(3):
        for end in (0, depth + 4):
            for plane in range(4):
                ext1[index, end + plane] = jnp.zeros((48, 128), F32)

    @pl.loop(0, before.shape[0], unroll=2)
    def _(tile):
        for place in range(8):
            at = 8 * tile + place
            index, plane = at // depth, lax.rem(at, depth)
            value = whole[at]
            value = jnp.where((lane >= 64) & (lane < 80), roll(after[tile], 64 - 16 * place, 1), value)
            value = jnp.where(lane >= 112, roll(before[tile], 112 - 16 * place, 1), value)
            ext1[index, plane + 4] = value

    prepare(ext1, weights1, diagonal1, scaled1, 1)
    start1[0] = jnp.zeros((48, 128), F32)
    start1[depth + 1] = jnp.zeros((48, 128), F32)

    @planes_of(depth, 1)
    def _(plane):
        start1[plane + 1] = FIRST * scaled1[plane + 4]

    for end in (0, depth + 4):
        for plane in range(4):
            iterate1[end + plane] = jnp.zeros((48, 128), F32)

    def put1(plane, value):
        iterate1[plane + 4] = value

    pass_all(weights1, scaled1, start1, put1, depth, lambda value, got: value + (CARRY * value + GAIN * got), 1)

    half = depth // 2

    @planes_of(half, 1)
    def _(pair):
        total = None
        for plane in (2 * pair, 2 * pair + 1):
            got = diagonal1[plane + 4] * defect(
                scaled1[plane + 4],
                [weights1[index, plane + 4] for index in range(6)],
                iterate1[plane + 4],
                iterate1[plane + 3],
                iterate1[plane + 5],
            )
            total = got if total is None else total + got
        sums1[pair] = total
        for index in (1, 2):
            sums1[index * half + pair] = ext1[index, 2 * pair + 4] + ext1[index, 2 * pair + 5]

    @planes_of(3 * half, 1)
    def _(plane):
        thin[plane] = sums1[plane, pl.ds(0, 24, stride=2), :] + sums1[plane, pl.ds(1, 24, stride=2), :]

    def to_level2(row, lane):
        place = jnp.where(lane < 64, lane, lane - 128)
        source = lax.shift_right_arithmetic(jnp.where(row < 96, row, row - 128), 1)
        return (source == place) & ((row < 80) | (row >= 112))

    level2 = matrix((128, 128), to_level2, 0.125)
    for index in range(3):
        values = thin[index * half : (index + 1) * half].reshape(half * 24, 128)
        ext2[index, 4 : 4 + half] = dot(values, level2).reshape(half, 24, 128)
        for end in (0, half + 4):
            for plane in range(4):
                ext2[index, end + plane] = jnp.zeros((24, 128), F32)

    prepare(ext2, weights2, diagonal2, scaled2, 2)
    start2[0] = jnp.zeros((24, 128), F32)
    start2[half + 1] = jnp.zeros((24, 128), F32)

    @pl.loop(0, half)
    def _(plane):
        start2[plane + 1] = FIRST * scaled2[plane + 4]

    for end in (0, half + 4):
        for plane in range(4):
            iterate2[end + plane] = jnp.zeros((24, 128), F32)

    def put2(plane, value):
        iterate2[plane + 4] = value

    pass_all(weights2, scaled2, start2, put2, half, lambda value, got: value + (CARRY * value + GAIN * got), 2)

    quarter = half // 2
    group = quarter // 2
    place2 = [
        matrix((128, 128), lambda row, lane, at=at: (row < 32) & (lane == row // 2 + 16 * at), 0.125)
        for at in range(6)
    ]
    for index in range(3):
        for plane in range(quarter):
            if index == 0:
                total = None
                for at in (2 * plane, 2 * plane + 1):
                    got = diagonal2[at + 4] * defect(
                        scaled2[at + 4],
                        [weights2[face, at + 4] for face in range(6)],
                        iterate2[at + 4],
                        iterate2[at + 3],
                        iterate2[at + 5],
                    )
                    total = got if total is None else total + got
                total = total[0:8]
            else:
                total = ext2[index, 2 * plane + 4, 0:8, :] + ext2[index, 2 * plane + 5, 0:8, :]
            at = index * quarter + plane
            sums2[at] = total
            side, within = divmod(plane, group)
            thick[index * 2 + side, pl.ds(within, 4, stride=group), :] = (
                sums2[at, pl.ds(0, 4, stride=2), :] + sums2[at, pl.ds(1, 4, stride=2), :]
            )
    result = dot(thick[0], place2[0])
    for at in range(1, 6):
        result = result + dot(thick[at], place2[at])
    copies(message, result)


def bottom(gathered, whole, weights, scaled, update, values):
    group = weights.shape[1]
    rows = weights.shape[2]
    for index in range(3):
        total = None
        lane = lane_of(gathered.shape[1:])
        for source in range(4):
            value = gathered[source]
            for side in range(2):
                to = 64 * side + 16 * source
                moved = roll(value, to - 16 * (2 * index + side), 1)
                moved = jnp.where((lane >= to) & (lane < to + 16), moved, 0.0)
                total = moved if total is None else total + moved
        whole[index] = total
    shape = (rows, 128)
    row, lane = row_of(shape), lane_of(shape)
    column = lax.rem(lane, 64)

    def plane_at(index, plane):
        return whole[index, pl.ds(plane, rows, stride=group), :]

    def around(get, plane):
        middle = get(plane)
        below = get(plane - 1) if plane else roll(get(group - 1), 64, 1)
        above = get(plane + 1) if plane < group - 1 else roll(get(0), 64, 1)
        return [below, above] + sides(middle)

    for plane in range(group):
        beta = plane_at(2, plane)
        masks = [
            (lane >= 64) if plane == 0 else None,
            (lane < 64) if plane == group - 1 else None,
            row > 0,
            row < rows - 1,
            column > 0,
            column < 63,
        ]
        near = around(lambda at: plane_at(2, at), plane)
        near = [other if mask is None else jnp.where(mask, other, 0.0) for other, mask in zip(near, masks)]
        faces = [scale_of(3) * (beta + other) for other in near]
        diagonal = plane_at(1, plane)
        for face in faces:
            diagonal = diagonal + face
        inverse = 1.0 / diagonal
        for index, (face, mask) in enumerate(zip(faces, masks)):
            face = face * inverse
            weights[index, plane] = face if mask is None else jnp.where(mask, face, 0.0)
        scaled[plane] = plane_at(0, plane) * inverse

    steps = chebyshev(BOTTOM, bottom_low)
    for plane in range(group):
        value = steps[0][1] * scaled[plane]
        update[plane] = value
        values[0, plane] = value
    for step, (carry, gain) in enumerate(steps[1:]):
        now, later = step % 2, (step + 1) % 2
        for plane in range(group):
            middle = values[now, plane]
            got = scaled[plane] - middle
            for index, other in enumerate(around(lambda at: values[now, at], plane)):
                got = got + weights[index, plane] * other
            moved = carry * update[plane] + gain * got
            update[plane] = moved
            values[later, plane] = middle + moved


def finish(at, iterate, weights, scaled, level, update, middle, put):
    count = iterate.shape[0]

    @planes_of(count - 2, level)
    def _(plane):
        value = iterate[plane + 1]
        got = FIRST * defect(
            scaled[at + plane + 1],
            [weights[index, at + plane + 1] for index in range(6)],
            value,
            iterate[plane],
            iterate[plane + 2],
        )
        update[plane] = got
        middle[plane] = value + got

    @planes_of(count - 4, level)
    def _(plane):
        value = middle[plane + 1]
        got = defect(
            scaled[at + plane + 2],
            [weights[index, at + plane + 2] for index in range(6)],
            value,
            middle[plane],
            middle[plane + 2],
        )
        put(plane, value + (CARRY * update[plane + 1] + GAIN * got))


def up(
    pos, gathered, weights2, scaled2, iterate2, weights1, scaled1, iterate1,
    weights0, diagonal0, scaled0, iterate0, solved, left_over,
    whole3, weights3, scaled3, update3, values3,
    thin3, error2, value2, update2, middle2, out2,
    tall1, value1, update1, middle1, out1,
    tall0, value0, update0, middle0, out0,
):
    bottom(gathered, whole3, weights3, scaled3, update3, values3)
    group, rows = weights3.shape[1], weights3.shape[2]
    at_x, at_y, at_z = 4 * pos[0], 16 * pos[1], pos[2]
    last = (BOTTOM - 1) % 2

    lane = lane_of((8, 128))
    near = lax.rem(lane, 64)
    fits = ((near < 16) | ((near < 20) & (pos[1] < 3)) | ((near >= 60) & (pos[1] > 0))).astype(F32)
    first_row, last_row = (pos[0] > 0).astype(F32), (pos[0] < pos[3] - 1).astype(F32)
    low = row_of((8, 128)) < 4
    own = jnp.where(low, fits, fits * last_row)
    left = jnp.where(low, 0.0, fits * first_row)
    for plane in range(group):
        moved = pltpu.roll(values3[last, plane], lax.rem(rows - at_x, rows), 0)
        both = jnp.concatenate([moved[0:8], moved[rows - 8 :]], axis=0)
        both = pltpu.roll(both, lax.rem(128 - at_y, 128), 1)
        ahead, behind = both[0:8] * own, both[8:16] * left
        for start in (0, 1):
            thin3[plane, pl.ds(start, 8, stride=2), :] = ahead
            thin3[plane, pl.ds(16 + start, 4, stride=2), :] = behind[4:8]

    def to_level2(row, lane):
        side, within = lane // 128, lax.rem(lane, 128)
        place = jnp.where(within < 64, within, within - 128)
        source = jnp.where(side == 0, lax.rem(row, 128), lax.rem(row + 64, 128))
        source = jnp.where(source < 64, source, source - 128)
        return (source == lax.shift_right_arithmetic(place, 1)) & ((within < 40) | (within >= 120))

    spread = dot(thin3[...].reshape(group * 24, 128), matrix((128, 256), to_level2)).reshape(group, 24, 256)
    for plane in range(group):
        for side in range(2):
            error2[side * group + plane + 2] = spread[plane, :, 128 * side : 128 * side + 128]
    for end in (0, 2 * group + 2):
        for plane in range(2):
            error2[end + plane] = jnp.zeros((24, 128), F32)

    for plane in range(10):
        value2[plane] = iterate2[2 * at_z + plane] + error2[at_z + plane // 2]

    def put2(plane, value):
        out2[plane] = value

    finish(2 * at_z, value2, weights2, scaled2, 2, update2, middle2, put2)

    def to_level1(row, lane):
        place = jnp.where(lane < 96, lane, lane - 128)
        source = lax.shift_right_arithmetic(place, 1)
        return (jnp.where(row < 64, row, row - 128) == source) & ((lane < 80) | (lane >= 112))

    wide1 = matrix((128, 128), to_level1)
    for plane in range(6):
        tall1[plane, pl.ds(0, 24, stride=2), :] = out2[plane]
        tall1[plane, pl.ds(1, 24, stride=2), :] = out2[plane]
    spread = dot(tall1[...].reshape(6 * 48, 128), wide1).reshape(6, 48, 128)
    for plane in range(12):
        value1[plane] = iterate1[4 * at_z + plane] + spread[plane // 2]

    def put1(plane, value):
        out1[plane] = value

    finish(4 * at_z, value1, weights1, scaled1, 1, update1, middle1, put1)

    def to_level0(row, lane):
        place = jnp.where(lane < 192, lane, lane - 256)
        source = lax.shift_right_arithmetic(place, 1)
        return (jnp.where(row < 96, row, row - 128) == source) & ((lane < 136) | (lane >= 248))

    wide0 = matrix((128, 256), to_level0)
    for plane in range(8):
        value = out1[plane]
        tall0[plane, pl.ds(0, 24, stride=2), :] = value[0:24]
        tall0[plane, pl.ds(1, 24, stride=2), :] = value[0:24]
        tall0[plane, pl.ds(40, 4, stride=2), :] = value[44:48]
        tall0[plane, pl.ds(41, 4, stride=2), :] = value[44:48]

    @planes_of(8, 1)
    def _(plane):
        value = dot(tall0[plane], wide0)
        out0[2 * plane] = value
        out0[2 * plane + 1] = value

    @planes_of(iterate0.shape[0], 0)
    def _(plane):
        value0[plane] = iterate0[plane] + out0[plane + 1]

    count = iterate0.shape[0]

    @planes_of(count - 2, 0)
    def _(plane):
        value = value0[plane + 1]
        got = FIRST * defect(
            scaled0[plane + 2],
            [weights0[index, plane + 2] for index in range(6)],
            value,
            value0[plane],
            value0[plane + 2],
        )
        update0[plane] = got
        middle0[plane] = value + got

    @planes_of(count - 4, 0)
    def _(plane):
        value = middle0[plane + 1]
        got = defect(
            scaled0[plane + 3],
            [weights0[index, plane + 3] for index in range(6)],
            value,
            middle0[plane],
            middle0[plane + 2],
        )
        out0[plane] = value + (CARRY * update0[plane + 1] + GAIN * got)

    @planes_of(count - 6, 0)
    def _(plane):
        value = out0[plane + 1]
        solved[plane] = value[0:32, 0:128]
        left_over[plane] = residual0(
            weights0, diagonal0, scaled0, value, out0[plane], out0[plane + 2], plane + 4
        )


def call(body, name, outs, scratch, pos, args):
    vmem = pl.BlockSpec(memory_space=pltpu.VMEM)
    smem = [pl.BlockSpec(memory_space=pltpu.SMEM)] if pos is not None else []
    operands = ([pos] if pos is not None else []) + list(args)
    return pl.pallas_call(
        body,
        name=name,
        out_shape=[jax.ShapeDtypeStruct(shape, F32) for shape in outs],
        in_specs=smem + [vmem] * len(args),
        out_specs=[vmem] * len(outs),
        scratch_shapes=[pltpu.VMEM(shape, F32) for shape in scratch],
        compiler_params=pltpu.CompilerParams(vmem_limit_bytes=32 * 2**20),
    )(*operands)


def exchange(up_values, down_values, axis, ring):
    peers = lax.axis_size(axis)
    up_pairs = [(i, (i + 1) % peers) for i in range(peers if ring else peers - 1)]
    down_pairs = [(j, i) for i, j in up_pairs]
    return lax.ppermute(up_values, axis, up_pairs), lax.ppermute(down_values, axis, down_pairs)


def on_device(right_side, acoef, beta):
    ranks, turns, files = [lax.axis_size(axis) for axis in AXES]
    pos = jnp.stack([lax.axis_index(axis) for axis in AXES] + [jnp.int32(ranks)]).astype(jnp.int32)
    planes = right_side.shape[0]
    arrays = (right_side, acoef, beta)

    last = jnp.stack([value[planes - DEEP :] for value in arrays])
    first = jnp.stack([value[:DEEP] for value in arrays])
    zb, za = exchange(last, first, "gz", False)
    last = jnp.stack([jnp.concatenate([zb[i, :, 24:], arrays[i][:, 24:], za[i, :, 24:]]) for i in range(3)])
    first = jnp.stack([jnp.concatenate([zb[i, :, :8], arrays[i][:, :8], za[i, :, :8]]) for i in range(3)])
    xb, xa = exchange(last, first, "gx", True)
    depth = planes + 2 * DEEP
    tiles = -(-3 * depth // 16)
    whole0, left, right = call(
        pack0, "pack0", [(3, depth, 48, 128)] + [(tiles, 48, 128)] * 2, [], pos, arrays + (zb, za, xb, xa)
    )
    before0, after0 = exchange(right, left, "gy", False)
    plane0 = (48, 256)
    half = planes // 2
    iterate0, message, weights0, diagonal0, scaled0 = call(
        down0,
        "down0",
        [(depth - 4,) + plane0, (files, 3 * half * 8, 128), (6, depth - 2) + plane0] + [(depth - 2,) + plane0] * 2,
        [(3, depth) + plane0, (depth - 2,) + plane0, (3 * half, 32, 128)],
        None,
        (whole0, before0, after0),
    )

    own = lax.all_to_all(message, "gz", 0, 0)
    xb, xa = exchange(own, own, "gx", True)
    depth1 = files * half
    tiles = 3 * depth1 // 8
    whole1, left, right = call(
        pack1, "pack1", [(3 * depth1, 48, 128)] + [(tiles, 48, 128)] * 2, [], pos, (own, xb, xa)
    )
    before1, after1 = exchange(right, left, "gy", False)
    plane1, plane2 = (48, 128), (24, 128)
    depth2 = depth1 // 2
    group = depth2 // 4
    tall1, tall2 = (depth1 + 8,) + plane1, (depth2 + 8,) + plane2
    message, weights1, scaled1, iterate1, weights2, scaled2, iterate2 = call(
        down1,
        "down1",
        [(ranks, 4 * group, 128), (6,) + tall1, tall1, tall1, (6,) + tall2, tall2, tall2],
        [(3,) + tall1, tall1, (depth1 + 2,) + plane1, (3 * depth2,) + plane1]
        + [(3,) + tall2, tall2, (depth2 + 2,) + plane2, (3 * depth2 // 2, 8, 128)]
        + [(3 * depth2,) + plane2, (6, 4 * group, 128)],
        None,
        (whole1, before1, after1),
    )

    gathered = lax.all_to_all(message, "gx", 0, 0)
    gathered = gathered.reshape(1, ranks * 4 * group, 128)
    gathered = jnp.broadcast_to(gathered, (turns,) + gathered.shape[1:])
    gathered = lax.all_to_all(gathered, "gy", 0, 0)

    rows3 = 4 * ranks
    plane3 = (rows3, 128)
    solved, left_over = call(
        up,
        "up",
        [right_side.shape, right_side.shape],
        [(3, rows3 * group, 128), (6, group) + plane3, (group,) + plane3, (group,) + plane3, (2, group) + plane3]
        + [(group,) + plane2, (2 * group + 4,) + plane2, (10,) + plane2, (8,) + plane2, (8,) + plane2, (6,) + plane2]
        + [(6,) + plane1, (12,) + plane1, (10,) + plane1, (10,) + plane1, (8,) + plane1]
        + [(8,) + plane1, (depth - 4,) + plane0, (depth - 6,) + plane0, (depth - 6,) + plane0, (depth - 2,) + plane0],
        pos,
        (gathered, weights2, scaled2, iterate2, weights1, scaled1, iterate1)
        + (weights0, diagonal0, scaled0, iterate0),
    )
    return solved, left_over


def solution(mesh):
    spec = P("gz", "gx", "gy")
    return jax.shard_map(
        on_device, mesh=mesh, in_specs=(spec, spec, spec), out_specs=(spec, spec), check_vma=False
    )
```

```python
import functools

import jax
import jax.numpy as jnp
from jax import lax
from jax.experimental import pallas as pl
from jax.experimental.pallas import tpu as pltpu
from jax.sharding import PartitionSpec as P

LEVELS = 4
SWEEPS = 2
BOTTOM = 16

smooth_low = 0.3
bottom_low = 0.05
upper_bound = 2.0
face_scale = 1.0 / 6.0

F32 = jnp.float32
AXES = ("gx", "gy", "gz")
DEEP = 5


def chebyshev(steps, lower):
    centre = (upper_bound + lower) / 2.0
    half_width = (upper_bound - lower) / 2.0
    sigma = centre / half_width
    rho = 1.0 / sigma
    out = [(0.0, 1.0 / centre)]
    for _ in range(1, steps):
        rho_next = 1.0 / (2.0 * sigma - rho)
        out.append((rho_next * rho, 2.0 * rho_next / half_width))
        rho = rho_next
    return out


(_, FIRST), (CARRY, GAIN) = chebyshev(SWEEPS, smooth_low)


def roll(value, shift, axis):
    shift %= value.shape[axis]
    return pltpu.roll(value, shift, axis) if shift else value


def lane_of(shape):
    return lax.broadcasted_iota(jnp.int32, shape, 1)


def row_of(shape):
    return lax.broadcasted_iota(jnp.int32, shape, 0)


def sides(value):
    return [roll(value, 1, 0), roll(value, -1, 0), roll(value, 1, 1), roll(value, -1, 1)]


def scale_of(level):
    return face_scale * 0.25**level * 0.5


def coefficients(beta, below, above, acoef, level):
    weights = [scale_of(level) * (beta + other) for other in [below, above] + sides(beta)]
    diagonal = acoef
    for weight in weights:
        diagonal = diagonal + weight
    inside = beta > 0.0
    inverse = jnp.where(inside, 1.0 / jnp.where(inside, diagonal, 1.0), 0.0)
    return [weight * inverse for weight in weights], diagonal, inverse


def defect(scaled, weights, value, below, above):
    result = scaled - value
    for weight, other in zip(weights, [below, above] + sides(value)):
        result = result + weight * other
    return result


def dot(left, right):
    return jnp.dot(left, right, precision=lax.Precision.HIGHEST, preferred_element_type=F32)


def matrix(shape, rule, value=1.0):
    return jnp.where(rule(row_of(shape), lane_of(shape)), value, 0.0).astype(F32)


def copies(ref, value):
    for index in range(ref.shape[0]):
        ref[index] = value


def slices(depth):
    wide, narrow = [], []
    for index, reach in enumerate((DEEP - 2, DEEP - 2, DEEP - 3)):
        for plane in range(depth):
            (wide if reach <= plane < depth - reach else narrow).append((index, plane))
    return wide, narrow


def slots(depth):
    wide, narrow = slices(depth)
    out = [(index, plane, at // 4, 32 * (at % 4), 32) for at, (index, plane) in enumerate(wide)]
    first = -(-len(wide) // 4)
    return out + [(index, plane, first + at // 16, 8 * (at % 16), 8) for at, (index, plane) in enumerate(narrow)]


def packz(f_ref, a_ref, b_ref, last, first):
    for index, ref in enumerate((f_ref, a_ref, b_ref)):
        last[index] = ref[ref.shape[0] - DEEP :]
        first[index] = ref[:DEEP]


def pack0(pos, f_ref, a_ref, b_ref, zb, za, xb, xa, whole, left, right):
    planes = f_ref.shape[0]
    has_before, has_after = pos[0] > 0, pos[0] < pos[3] - 1
    for index, ref in enumerate((f_ref, a_ref, b_ref)):
        whole[index, 0:DEEP, 0:32, :] = zb[index]
        whole[index, DEEP : DEEP + planes, 0:32, :] = ref[...]
        whole[index, DEEP + planes :, 0:32, :] = za[index]
        whole[index, :, 32:40, :] = jnp.where(has_after, xa[index], 0.0)
        whole[index, :, 40:48, :] = jnp.where(has_before, xb[index], 0.0)
    lane = lane_of((48, 128))
    low, high = {}, {}
    for index, plane, tile, to, lanes in slots(planes + 2 * DEEP):
        value = whole[index, plane]
        here = (lane >= to) & (lane < to + lanes)
        zero = jnp.zeros((48, 128), F32)
        low[tile] = jnp.where(here, roll(value, to, 1), low.get(tile, zero))
        high[tile] = jnp.where(here, roll(value, to + lanes, 1), high.get(tile, zero))
    for tile in low:
        left[tile] = low[tile]
        right[tile] = high[tile]


def unpack0(whole, before, after, ext):
    lane = lane_of((48, 128))
    for index, plane, tile, to, lanes in slots(whole.shape[1]):
        ahead = jnp.where(lane < lanes, roll(after[tile], -to, 1), 0.0)
        ext[index, plane, :, 0:128] = whole[index, plane]
        ext[index, plane, :, 128:256] = jnp.where(lane >= 128 - lanes, roll(before[tile], -lanes - to, 1), ahead)


def planes_of(count, level, start=0):
    most = (7, 10, 16)[level]
    return pl.loop(start, start + count, unroll=max(n for n in range(1, most + 1) if count % n == 0))


def prepare0(ext, weights, diagonal, scaled):
    @planes_of(diagonal.shape[0], 0)
    def _(plane):
        got, middle, inverse = coefficients(
            ext[2, plane + 1], ext[2, plane], ext[2, plane + 2], ext[1, plane + 1], 0
        )
        for index in range(6):
            weights[index, plane] = got[index]
        diagonal[plane] = middle
        scaled[plane] = ext[0, plane + 1] * inverse


def residual0(weights, diagonal, scaled, value, below, above, at, lanes):
    cut = lambda array: array[0:32, 0:lanes]
    result = scaled[at, 0:32, 0:lanes] - cut(value)
    for index, other in enumerate([below, above] + sides(value)):
        result = result + weights[index, at, 0:32, 0:lanes] * cut(other)
    return diagonal[at, 0:32, 0:lanes] * result


def down0(whole, before, after, iterate, message, weights, diagonal, scaled, ext, start, sums):
    unpack0(whole, before, after, ext)
    prepare0(ext, weights, diagonal, scaled)

    @planes_of(start.shape[0], 0)
    def _(plane):
        start[plane] = FIRST * scaled[plane]

    @planes_of(iterate.shape[0], 0)
    def _(plane):
        value = start[plane + 1]
        got = defect(
            scaled[plane + 1],
            [weights[index, plane + 1] for index in range(6)],
            value,
            start[plane],
            start[plane + 2],
        )
        iterate[plane] = value + (CARRY * value + GAIN * got)

    planes = whole.shape[1] - 2 * DEEP

    def left_over(plane):
        return residual0(
            weights, diagonal, scaled, iterate[plane + 3], iterate[plane + 2], iterate[plane + 4], plane + 4, 256
        )

    half = planes // 2

    @planes_of(half, 0)
    def _(plane):
        pairs = [left_over(2 * plane) + left_over(2 * plane + 1)]
        for index in (1, 2):
            low = ext[index, DEEP + 2 * plane, 0:32, :]
            pairs.append(low + ext[index, DEEP + 2 * plane + 1, 0:32, :])
        for index, value in enumerate(pairs):
            sums[0, index * half + plane] = value[:, 0:128]
            sums[1, index * half + plane] = value[:, 128:256]

    def rows_of(side, places):
        tall = [
            sums[side, place, pl.ds(0, 16, stride=2), :] + sums[side, place, pl.ds(1, 16, stride=2), :]
            for place in places
        ]
        return jnp.concatenate(tall, axis=0)

    even = matrix((128, 128), lambda row, lane: lane == row // 2, 0.125)
    odd = matrix((128, 128), lambda row, lane: lane == row // 2 + 64, 0.125)
    middle = dot(rows_of(0, range(0, 3 * half, 2)), even) + dot(rows_of(0, range(1, 3 * half, 2)), odd)
    ends = None
    for plane in range(half):

        def rule(row, lane, to=32 * plane):
            ahead = (row < 32) & (lane == to + row // 2)
            return ahead | ((row >= 96) & (lane == to + 16 + (row - 96) // 2))

        got = dot(rows_of(1, range(plane, 3 * half, half)), matrix((128, 128), rule, 0.125))
        ends = got if ends is None else ends + got
    copies(message, jnp.concatenate([middle, ends], axis=0))


def unpack1(pos, own, xb, xa, ext):
    has_before, has_after = pos[0] > 0, pos[0] < pos[3] - 1
    lane = lane_of((16, 128))
    per = own.shape[1] // 36

    @pl.loop(0, own.shape[0], unroll=2)
    def _(source):
        for block, (ref, there) in enumerate(((own, None), (xa, has_after), (xb, has_before))):
            for index in range(3):
                ends = ref[source, 96 + 16 * index : 112 + 16 * index, :]
                for plane in range(per):
                    at = (2 * index + plane // 2) * 16
                    value = roll(ref[source, at : at + 16, :], 64 * (plane % 2), 1)
                    value = jnp.where(lane < 80, jnp.where(lane < 64, value, roll(ends, 64 - 32 * plane, 1)), 0.0)
                    value = jnp.where(lane >= 112, roll(ends, 96 - 32 * plane, 1), value)
                    if there is not None:
                        value = jnp.where(there, value, 0.0)
                    ext[index, 4 + source * per + plane, 16 * block : 16 * block + 16, :] = value


def pass_all(weights, scaled, value, out, count, combine, level):
    @planes_of(count, level)
    def _(plane):
        middle = value[plane + 1]
        got = defect(
            scaled[plane + 4],
            [weights[index, plane + 4] for index in range(6)],
            middle,
            value[plane],
            value[plane + 2],
        )
        out(plane, combine(middle, got))


def prepare(ext, weights, diagonal, scaled, level):
    shape = scaled.shape[1:]
    count = scaled.shape[0] - 8
    for end in (0, count + 4):
        for plane in range(4):
            scaled[end + plane] = jnp.zeros(shape, F32)
            for index in range(6):
                weights[index, end + plane] = jnp.zeros(shape, F32)

    @planes_of(count, level, 4)
    def _(at):
        got, middle, inverse = coefficients(ext[2, at], ext[2, at - 1], ext[2, at + 1], ext[1, at], level)
        for index in range(6):
            weights[index, at] = got[index]
        diagonal[at] = middle
        scaled[at] = ext[0, at] * inverse


def down1(
    pos, own, xb, xa, message, weights1, scaled1, iterate1, weights2, scaled2, iterate2,
    ext1, diagonal1, start1, sums1, ext2, diagonal2, start2, sums2, thin, thick,
):
    depth = scaled1.shape[0] - 8
    for index in range(3):
        for end in (0, depth + 4):
            for plane in range(4):
                ext1[index, end + plane] = jnp.zeros((48, 128), F32)

    unpack1(pos, own, xb, xa, ext1)
    prepare(ext1, weights1, diagonal1, scaled1, 1)
    start1[0] = jnp.zeros((48, 128), F32)
    start1[depth + 1] = jnp.zeros((48, 128), F32)

    @planes_of(depth, 1)
    def _(plane):
        start1[plane + 1] = FIRST * scaled1[plane + 4]

    for end in (0, depth + 4):
        for plane in range(4):
            iterate1[end + plane] = jnp.zeros((48, 128), F32)

    def put1(plane, value):
        iterate1[plane + 4] = value

    pass_all(weights1, scaled1, start1, put1, depth, lambda value, got: value + (CARRY * value + GAIN * got), 1)

    half = depth // 2

    @planes_of(half, 1)
    def _(pair):
        total = None
        for plane in (2 * pair, 2 * pair + 1):
            got = diagonal1[plane + 4] * defect(
                scaled1[plane + 4],
                [weights1[index, plane + 4] for index in range(6)],
                iterate1[plane + 4],
                iterate1[plane + 3],
                iterate1[plane + 5],
            )
            total = got if total is None else total + got
        sums1[pair] = total
        for index in (1, 2):
            sums1[index * half + pair] = ext1[index, 2 * pair + 4] + ext1[index, 2 * pair + 5]

    @planes_of(3 * half, 1)
    def _(plane):
        thin[plane] = sums1[plane, pl.ds(0, 24, stride=2), :] + sums1[plane, pl.ds(1, 24, stride=2), :]

    def to_level2(row, lane):
        place = jnp.where(lane < 64, lane, lane - 128)
        source = lax.shift_right_arithmetic(jnp.where(row < 96, row, row - 128), 1)
        return (source == place) & ((row < 80) | (row >= 112))

    level2 = matrix((128, 128), to_level2, 0.125)
    for index in range(3):
        values = thin[index * half : (index + 1) * half].reshape(half * 24, 128)
        ext2[index, 4 : 4 + half] = dot(values, level2).reshape(half, 24, 128)
        for end in (0, half + 4):
            for plane in range(4):
                ext2[index, end + plane] = jnp.zeros((24, 128), F32)

    prepare(ext2, weights2, diagonal2, scaled2, 2)
    start2[0] = jnp.zeros((24, 128), F32)
    start2[half + 1] = jnp.zeros((24, 128), F32)

    @pl.loop(0, half)
    def _(plane):
        start2[plane + 1] = FIRST * scaled2[plane + 4]

    for end in (0, half + 4):
        for plane in range(4):
            iterate2[end + plane] = jnp.zeros((24, 128), F32)

    def put2(plane, value):
        iterate2[plane + 4] = value

    pass_all(weights2, scaled2, start2, put2, half, lambda value, got: value + (CARRY * value + GAIN * got), 2)

    quarter = half // 2
    group = quarter // 2
    place2 = [
        matrix((128, 128), lambda row, lane, at=at: (row < 32) & (lane == row // 2 + 16 * at), 0.125)
        for at in range(6)
    ]
    for index in range(3):
        for plane in range(quarter):
            if index == 0:
                total = None
                for at in (2 * plane, 2 * plane + 1):
                    got = diagonal2[at + 4] * defect(
                        scaled2[at + 4],
                        [weights2[face, at + 4] for face in range(6)],
                        iterate2[at + 4],
                        iterate2[at + 3],
                        iterate2[at + 5],
                    )
                    total = got if total is None else total + got
                total = total[0:8]
            else:
                total = ext2[index, 2 * plane + 4, 0:8, :] + ext2[index, 2 * plane + 5, 0:8, :]
            at = index * quarter + plane
            sums2[at] = total
            side, within = divmod(plane, group)
            thick[index * 2 + side, pl.ds(within, 4, stride=group), :] = (
                sums2[at, pl.ds(0, 4, stride=2), :] + sums2[at, pl.ds(1, 4, stride=2), :]
            )
    result = dot(thick[0], place2[0])
    for at in range(1, 6):
        result = result + dot(thick[at], place2[at])
    copies(message, result)


def bottom(gathered, whole, weights, scaled, update, values):
    group = weights.shape[1]
    rows = weights.shape[2]
    for index in range(3):
        total = None
        lane = lane_of(gathered.shape[1:])
        for source in range(4):
            value = gathered[source]
            for side in range(2):
                to = 64 * side + 16 * source
                moved = roll(value, to - 16 * (2 * index + side), 1)
                moved = jnp.where((lane >= to) & (lane < to + 16), moved, 0.0)
                total = moved if total is None else total + moved
        whole[index] = total
    shape = (rows, 128)
    row, lane = row_of(shape), lane_of(shape)
    column = lax.rem(lane, 64)

    def plane_at(index, plane):
        return whole[index, pl.ds(plane, rows, stride=group), :]

    def around(get, plane):
        middle = get(plane)
        below = get(plane - 1) if plane else roll(get(group - 1), 64, 1)
        above = get(plane + 1) if plane < group - 1 else roll(get(0), 64, 1)
        return [below, above] + sides(middle)

    for plane in range(group):
        beta = plane_at(2, plane)
        masks = [
            (lane >= 64) if plane == 0 else None,
            (lane < 64) if plane == group - 1 else None,
            row > 0,
            row < rows - 1,
            column > 0,
            column < 63,
        ]
        near = around(lambda at: plane_at(2, at), plane)
        near = [other if mask is None else jnp.where(mask, other, 0.0) for other, mask in zip(near, masks)]
        faces = [scale_of(3) * (beta + other) for other in near]
        diagonal = plane_at(1, plane)
        for face in faces:
            diagonal = diagonal + face
        inverse = 1.0 / diagonal
        for index, (face, mask) in enumerate(zip(faces, masks)):
            face = face * inverse
            weights[index, plane] = face if mask is None else jnp.where(mask, face, 0.0)
        scaled[plane] = plane_at(0, plane) * inverse

    steps = chebyshev(BOTTOM, bottom_low)
    for plane in range(group):
        value = steps[0][1] * scaled[plane]
        update[plane] = value
        values[0, plane] = value
    for step, (carry, gain) in enumerate(steps[1:]):
        now, later = step % 2, (step + 1) % 2
        for plane in range(group):
            middle = values[now, plane]
            got = scaled[plane] - middle
            for index, other in enumerate(around(lambda at: values[now, at], plane)):
                got = got + weights[index, plane] * other
            moved = carry * update[plane] + gain * got
            update[plane] = moved
            values[later, plane] = middle + moved


def finish(at, iterate, weights, scaled, level, update, middle, put):
    count = iterate.shape[0]

    @planes_of(count - 2, level)
    def _(plane):
        value = iterate[plane + 1]
        got = FIRST * defect(
            scaled[at + plane + 1],
            [weights[index, at + plane + 1] for index in range(6)],
            value,
            iterate[plane],
            iterate[plane + 2],
        )
        update[plane] = got
        middle[plane] = value + got

    @planes_of(count - 4, level)
    def _(plane):
        value = middle[plane + 1]
        got = defect(
            scaled[at + plane + 2],
            [weights[index, at + plane + 2] for index in range(6)],
            value,
            middle[plane],
            middle[plane + 2],
        )
        put(plane, value + (CARRY * update[plane + 1] + GAIN * got))


def up(
    pos, gathered, weights2, scaled2, iterate2, weights1, scaled1, iterate1,
    weights0, diagonal0, scaled0, iterate0, solved, left_over,
    whole3, weights3, scaled3, update3, values3,
    thin3, error2, value2, update2, middle2, out2,
    tall1, value1, update1, middle1, out1,
    tall0, value0, update0, middle0, out0,
):
    bottom(gathered, whole3, weights3, scaled3, update3, values3)
    group, rows = weights3.shape[1], weights3.shape[2]
    at_x, at_y, at_z = 4 * pos[0], 16 * pos[1], pos[2]
    last = (BOTTOM - 1) % 2

    lane = lane_of((8, 128))
    near = lax.rem(lane, 64)
    fits = ((near < 16) | ((near < 20) & (pos[1] < 3)) | ((near >= 60) & (pos[1] > 0))).astype(F32)
    first_row, last_row = (pos[0] > 0).astype(F32), (pos[0] < pos[3] - 1).astype(F32)
    low = row_of((8, 128)) < 4
    own = jnp.where(low, fits, fits * last_row)
    left = jnp.where(low, 0.0, fits * first_row)
    for plane in range(group):
        moved = pltpu.roll(values3[last, plane], lax.rem(rows - at_x, rows), 0)
        both = jnp.concatenate([moved[0:8], moved[rows - 8 :]], axis=0)
        both = pltpu.roll(both, lax.rem(128 - at_y, 128), 1)
        ahead, behind = both[0:8] * own, both[8:16] * left
        for start in (0, 1):
            thin3[plane, pl.ds(start, 8, stride=2), :] = ahead
            thin3[plane, pl.ds(16 + start, 4, stride=2), :] = behind[4:8]

    def to_level2(row, lane):
        side, within = lane // 128, lax.rem(lane, 128)
        place = jnp.where(within < 64, within, within - 128)
        source = jnp.where(side == 0, lax.rem(row, 128), lax.rem(row + 64, 128))
        source = jnp.where(source < 64, source, source - 128)
        return (source == lax.shift_right_arithmetic(place, 1)) & ((within < 40) | (within >= 120))

    spread = dot(thin3[...].reshape(group * 24, 128), matrix((128, 256), to_level2)).reshape(group, 24, 256)
    for plane in range(group):
        for side in range(2):
            error2[side * group + plane + 2] = spread[plane, :, 128 * side : 128 * side + 128]
    for end in (0, 2 * group + 2):
        for plane in range(2):
            error2[end + plane] = jnp.zeros((24, 128), F32)

    for plane in range(10):
        value2[plane] = iterate2[2 * at_z + plane] + error2[at_z + plane // 2]

    def put2(plane, value):
        out2[plane] = value

    finish(2 * at_z, value2, weights2, scaled2, 2, update2, middle2, put2)

    def to_level1(row, lane):
        place = jnp.where(lane < 96, lane, lane - 128)
        source = lax.shift_right_arithmetic(place, 1)
        return (jnp.where(row < 64, row, row - 128) == source) & ((lane < 80) | (lane >= 112))

    wide1 = matrix((128, 128), to_level1)
    for plane in range(6):
        tall1[plane, pl.ds(0, 24, stride=2), :] = out2[plane]
        tall1[plane, pl.ds(1, 24, stride=2), :] = out2[plane]
    spread = dot(tall1[...].reshape(6 * 48, 128), wide1).reshape(6, 48, 128)
    for plane in range(12):
        value1[plane] = iterate1[4 * at_z + plane] + spread[plane // 2]

    def put1(plane, value):
        out1[plane] = value

    finish(4 * at_z, value1, weights1, scaled1, 1, update1, middle1, put1)

    def to_level0(row, lane):
        place = jnp.where(lane < 192, lane, lane - 256)
        source = lax.shift_right_arithmetic(place, 1)
        return (jnp.where(row < 96, row, row - 128) == source) & ((lane < 136) | (lane >= 248))

    wide0 = matrix((128, 256), to_level0)
    for plane in range(8):
        value = out1[plane]
        tall0[plane, pl.ds(0, 24, stride=2), :] = value[0:24]
        tall0[plane, pl.ds(1, 24, stride=2), :] = value[0:24]
        tall0[plane, pl.ds(40, 4, stride=2), :] = value[44:48]
        tall0[plane, pl.ds(41, 4, stride=2), :] = value[44:48]

    @planes_of(8, 1)
    def _(plane):
        value = dot(tall0[plane], wide0)
        out0[2 * plane] = value
        out0[2 * plane + 1] = value

    @planes_of(iterate0.shape[0], 0)
    def _(plane):
        value0[plane] = iterate0[plane] + out0[plane + 1]

    count = iterate0.shape[0]

    @planes_of(count - 2, 0)
    def _(plane):
        value = value0[plane + 1]
        got = FIRST * defect(
            scaled0[plane + 2],
            [weights0[index, plane + 2] for index in range(6)],
            value,
            value0[plane],
            value0[plane + 2],
        )
        update0[plane] = got
        middle0[plane] = value + got

    @planes_of(count - 4, 0)
    def _(plane):
        value = middle0[plane + 1]
        got = defect(
            scaled0[plane + 3],
            [weights0[index, plane + 3] for index in range(6)],
            value,
            middle0[plane],
            middle0[plane + 2],
        )
        out0[plane] = value + (CARRY * update0[plane + 1] + GAIN * got)

    @planes_of(count - 6, 0)
    def _(plane):
        value = out0[plane + 1]
        solved[plane] = value[0:32, 0:128]
        left_over[plane] = residual0(
            weights0, diagonal0, scaled0, value, out0[plane], out0[plane + 2], plane + 4, 128
        )


def call(body, name, outs, scratch, pos, args):
    vmem = pl.BlockSpec(memory_space=pltpu.VMEM)
    smem = [pl.BlockSpec(memory_space=pltpu.SMEM)] if pos is not None else []
    operands = ([pos] if pos is not None else []) + list(args)
    return pl.pallas_call(
        body,
        name=name,
        out_shape=[jax.ShapeDtypeStruct(shape, F32) for shape in outs],
        in_specs=smem + [vmem] * len(args),
        out_specs=[vmem] * len(outs),
        scratch_shapes=[pltpu.VMEM(shape, F32) for shape in scratch],
        compiler_params=pltpu.CompilerParams(vmem_limit_bytes=32 * 2**20),
    )(*operands)


def exchange(up_values, down_values, axis, ring):
    peers = lax.axis_size(axis)
    up_pairs = [(i, (i + 1) % peers) for i in range(peers if ring else peers - 1)]
    down_pairs = [(j, i) for i, j in up_pairs]
    return lax.ppermute(up_values, axis, up_pairs), lax.ppermute(down_values, axis, down_pairs)


def on_device(right_side, acoef, beta):
    ranks, turns, files = [lax.axis_size(axis) for axis in AXES]
    pos = jnp.stack([lax.axis_index(axis) for axis in AXES] + [jnp.int32(ranks)]).astype(jnp.int32)
    planes = right_side.shape[0]
    arrays = (right_side, acoef, beta)

    shape = (3, DEEP) + right_side.shape[1:]
    last, first = call(packz, "packz", [shape, shape], [], None, arrays)
    zb, za = exchange(last, first, "gz", False)
    last = jnp.stack([jnp.concatenate([zb[i, :, 24:], arrays[i][:, 24:], za[i, :, 24:]]) for i in range(3)])
    first = jnp.stack([jnp.concatenate([zb[i, :, :8], arrays[i][:, :8], za[i, :, :8]]) for i in range(3)])
    xb, xa = exchange(last, first, "gx", True)
    depth = planes + 2 * DEEP
    tiles = max(tile for _, _, tile, _, _ in slots(depth)) + 1
    whole0, left, right = call(
        pack0, "pack0", [(3, depth, 48, 128)] + [(tiles, 48, 128)] * 2, [], pos, arrays + (zb, za, xb, xa)
    )
    before0, after0 = exchange(right, left, "gy", False)
    plane0 = (48, 256)
    half = planes // 2
    iterate0, message, weights0, diagonal0, scaled0 = call(
        down0,
        "down0",
        [(depth - 4,) + plane0, (files, 36 * half, 128), (6, depth - 2) + plane0] + [(depth - 2,) + plane0] * 2,
        [(3, depth) + plane0, (depth - 2,) + plane0, (2, 3 * half, 32, 128)],
        None,
        (whole0, before0, after0),
    )

    own = lax.all_to_all(message, "gz", 0, 0)
    xb, xa = exchange(own, own, "gx", True)
    depth1 = files * half
    plane1, plane2 = (48, 128), (24, 128)
    depth2 = depth1 // 2
    group = depth2 // 4
    tall1, tall2 = (depth1 + 8,) + plane1, (depth2 + 8,) + plane2
    message, weights1, scaled1, iterate1, weights2, scaled2, iterate2 = call(
        down1,
        "down1",
        [(ranks, 4 * group, 128), (6,) + tall1, tall1, tall1, (6,) + tall2, tall2, tall2],
        [(3,) + tall1, tall1, (depth1 + 2,) + plane1, (3 * depth2,) + plane1]
        + [(3,) + tall2, tall2, (depth2 + 2,) + plane2, (3 * depth2 // 2, 8, 128)]
        + [(3 * depth2,) + plane2, (6, 4 * group, 128)],
        pos,
        (own, xb, xa),
    )

    gathered = lax.all_to_all(message, "gx", 0, 0)
    gathered = gathered.reshape(1, ranks * 4 * group, 128)
    gathered = jnp.broadcast_to(gathered, (turns,) + gathered.shape[1:])
    gathered = lax.all_to_all(gathered, "gy", 0, 0)

    rows3 = 4 * ranks
    plane3 = (rows3, 128)
    solved, left_over = call(
        up,
        "up",
        [right_side.shape, right_side.shape],
        [(3, rows3 * group, 128), (6, group) + plane3, (group,) + plane3, (group,) + plane3, (2, group) + plane3]
        + [(group,) + plane2, (2 * group + 4,) + plane2, (10,) + plane2, (8,) + plane2, (8,) + plane2, (6,) + plane2]
        + [(6,) + plane1, (12,) + plane1, (10,) + plane1, (10,) + plane1, (8,) + plane1]
        + [(8,) + plane1, (depth - 4,) + plane0, (depth - 6,) + plane0, (depth - 6,) + plane0, (depth - 2,) + plane0],
        pos,
        (gathered, weights2, scaled2, iterate2, weights1, scaled1, iterate1)
        + (weights0, diagonal0, scaled0, iterate0),
    )
    return solved, left_over


def solution(mesh):
    spec = P("gz", "gx", "gy")
    return jax.shard_map(
        on_device, mesh=mesh, in_specs=(spec, spec, spec), out_specs=(spec, spec), check_vma=False
    )
```

```python
import functools

import jax
import jax.numpy as jnp
from jax import lax
from jax.experimental import pallas as pl
from jax.experimental.pallas import tpu as pltpu
from jax.sharding import PartitionSpec as P

LEVELS = 4
SWEEPS = 2
BOTTOM = 16

smooth_low = 0.3
bottom_low = 0.05
upper_bound = 2.0
face_scale = 1.0 / 6.0

F32 = jnp.float32
AXES = ("gx", "gy", "gz")
REACH = (4, 4, 5)
DEEP = 5


def chebyshev(steps, lower):
    centre = (upper_bound + lower) / 2.0
    half_width = (upper_bound - lower) / 2.0
    sigma = centre / half_width
    rho = 1.0 / sigma
    out = [(0.0, 1.0 / centre)]
    for _ in range(1, steps):
        rho_next = 1.0 / (2.0 * sigma - rho)
        out.append((rho_next * rho, 2.0 * rho_next / half_width))
        rho = rho_next
    return out


(_, FIRST), (CARRY, GAIN) = chebyshev(SWEEPS, smooth_low)


def roll(value, shift, axis):
    shift %= value.shape[axis]
    return pltpu.roll(value, shift, axis) if shift else value


def lane_of(shape):
    return lax.broadcasted_iota(jnp.int32, shape, 1)


def row_of(shape):
    return lax.broadcasted_iota(jnp.int32, shape, 0)


def sides(value):
    return [roll(value, 1, 0), roll(value, -1, 0), roll(value, 1, 1), roll(value, -1, 1)]


def scale_of(level):
    return face_scale * 0.25**level * 0.5


def coefficients(beta, below, above, acoef, level):
    weights = [scale_of(level) * (beta + other) for other in [below, above] + sides(beta)]
    diagonal = acoef
    for weight in weights:
        diagonal = diagonal + weight
    inside = beta > 0.0
    inverse = jnp.where(inside, 1.0 / jnp.where(inside, diagonal, 1.0), 0.0)
    return [weight * inverse for weight in weights], diagonal, inverse


def defect(scaled, weights, value, below, above):
    result = scaled - value
    for weight, other in zip(weights, [below, above] + sides(value)):
        result = result + weight * other
    return result


def dot(left, right):
    return jnp.dot(left, right, precision=lax.Precision.HIGHEST, preferred_element_type=F32)


def matrix(shape, rule, value=1.0):
    return jnp.where(rule(row_of(shape), lane_of(shape)), value, 0.0).astype(F32)


def copies(ref, value):
    for index in range(ref.shape[0]):
        ref[index] = value


def away(plane, depth):
    return max(DEEP - plane, plane - (depth - 1 - DEEP), 0)


def slots(depth):
    wide, narrow = [], []
    for index, reach in enumerate(REACH):
        for plane in range(depth):
            if away(plane, depth) < reach:
                (wide if away(plane, depth) <= reach - 2 else narrow).append((index, plane))
    out = [(index, plane, at // 4, 32 * (at % 4), 32) for at, (index, plane) in enumerate(wide)]
    first = -(-len(wide) // 4)
    return out + [(index, plane, first + at // 16, 8 * (at % 16), 8) for at, (index, plane) in enumerate(narrow)]


def packx(own, zb, za, last, first):
    planes, at = own.shape[1], 0
    for index, reach in enumerate(REACH):
        for value in (zb[index, DEEP - reach + 1 :], own[index], za[index, : reach - 1]):
            last[at : at + value.shape[0]] = value[:, 24:]
            first[at : at + value.shape[0]] = value[:, :8]
            at += value.shape[0]


def pack0(pos, own, zb, za, xb, xa, whole, left, right):
    planes = own.shape[1]
    depth = planes + 2 * DEEP
    has_before, has_after = pos[0] > 0, pos[0] < pos[3] - 1
    at_x = 0
    for index, reach in enumerate(REACH):
        for plane in range(DEEP - reach):
            for end in (plane, depth - 1 - plane):
                whole[index, end] = jnp.zeros((48, 128), F32)
        whole[index, DEEP - reach : DEEP, 0:32, :] = zb[index, DEEP - reach :]
        whole[index, DEEP : DEEP + planes, 0:32, :] = own[index]
        whole[index, DEEP + planes : DEEP + planes + reach, 0:32, :] = za[index, :reach]
        for plane in (DEEP - reach, DEEP + planes + reach - 1):
            whole[index, plane, 32:48, :] = jnp.zeros((16, 128), F32)
        inner, count = DEEP - reach + 1, planes + 2 * reach - 2
        whole[index, inner : inner + count, 32:40, :] = jnp.where(has_after, xa[at_x : at_x + count], 0.0)
        whole[index, inner : inner + count, 40:48, :] = jnp.where(has_before, xb[at_x : at_x + count], 0.0)
        at_x += count
    lane = lane_of((40, 128))
    four = row_of((8, 128)) < 4
    low, high = {}, {}
    for index, plane, tile, to, lanes in slots(depth):
        ends = jnp.where(four, whole[index, plane, 32:40, :], whole[index, plane, 40:48, :])
        value = jnp.concatenate([whole[index, plane, 0:32, :], ends], axis=0)
        here = (lane >= to) & (lane < to + lanes)
        zero = jnp.zeros((40, 128), F32)
        low[tile] = jnp.where(here, roll(value, to, 1), low.get(tile, zero))
        high[tile] = jnp.where(here, roll(value, to + lanes, 1), high.get(tile, zero))
    for tile in low:
        left[tile] = low[tile]
        right[tile] = high[tile]


def unpack0(whole, before, after, ext):
    depth = whole.shape[1]
    ext[:, :, :, 0:128] = whole[...]
    lane = lane_of((40, 128))
    there = {(index, plane): rest for index, plane, *rest in slots(depth)}
    for index in range(3):
        for plane in range(depth):
            if (index, plane) not in there:
                ext[index, plane, :, 128:256] = jnp.zeros((48, 128), F32)
                continue
            tile, to, lanes = there[index, plane]
            ahead = jnp.where(lane < lanes, roll(after[tile], -to, 1), 0.0)
            value = jnp.where(lane >= 128 - lanes, roll(before[tile], -lanes - to, 1), ahead)
            ext[index, plane, 0:40, 128:256] = value
            ext[index, plane, 40:48, 128:256] = value[32:40]


def planes_of(count, level, start=0):
    most = (7, 10, 16)[level]
    return pl.loop(start, start + count, unroll=max(n for n in range(1, most + 1) if count % n == 0))


def prepare0(ext, weights, diagonal, scaled):
    @planes_of(diagonal.shape[0], 0)
    def _(plane):
        got, middle, inverse = coefficients(
            ext[2, plane + 1], ext[2, plane], ext[2, plane + 2], ext[1, plane + 1], 0
        )
        for index in range(6):
            weights[index, plane] = got[index]
        diagonal[plane] = middle
        scaled[plane] = ext[0, plane + 1] * inverse


def residual0(weights, diagonal, scaled, value, below, above, at, lanes):
    cut = lambda array: array[0:32, 0:lanes]
    result = scaled[at, 0:32, 0:lanes] - cut(value)
    for index, other in enumerate([below, above] + sides(value)):
        result = result + weights[index, at, 0:32, 0:lanes] * cut(other)
    return diagonal[at, 0:32, 0:lanes] * result


def down0(whole, before, after, iterate, message, weights, diagonal, scaled, ext, start, sums):
    unpack0(whole, before, after, ext)
    prepare0(ext, weights, diagonal, scaled)

    @planes_of(start.shape[0], 0)
    def _(plane):
        start[plane] = FIRST * scaled[plane]

    @planes_of(iterate.shape[0], 0)
    def _(plane):
        value = start[plane + 1]
        got = defect(
            scaled[plane + 1],
            [weights[index, plane + 1] for index in range(6)],
            value,
            start[plane],
            start[plane + 2],
        )
        iterate[plane] = value + (CARRY * value + GAIN * got)

    planes = whole.shape[1] - 2 * DEEP

    def left_over(plane):
        return residual0(
            weights, diagonal, scaled, iterate[plane + 3], iterate[plane + 2], iterate[plane + 4], plane + 4, 256
        )

    half = planes // 2

    @planes_of(half, 0)
    def _(plane):
        pairs = [left_over(2 * plane) + left_over(2 * plane + 1)]
        for index in (1, 2):
            low = ext[index, DEEP + 2 * plane, 0:32, :]
            pairs.append(low + ext[index, DEEP + 2 * plane + 1, 0:32, :])
        for index, value in enumerate(pairs):
            sums[0, index * half + plane] = value[:, 0:128]
            sums[1, index * half + plane] = value[:, 128:256]

    def rows_of(side, places):
        tall = [
            sums[side, place, pl.ds(0, 16, stride=2), :] + sums[side, place, pl.ds(1, 16, stride=2), :]
            for place in places
        ]
        return jnp.concatenate(tall, axis=0)

    even = matrix((128, 128), lambda row, lane: lane == row // 2, 0.125)
    odd = matrix((128, 128), lambda row, lane: lane == row // 2 + 64, 0.125)
    middle = dot(rows_of(0, range(0, 3 * half, 2)), even) + dot(rows_of(0, range(1, 3 * half, 2)), odd)
    ends = None
    for plane in range(half):

        def rule(row, lane, to=32 * plane):
            ahead = (row < 32) & (lane == to + row // 2)
            return ahead | ((row >= 96) & (lane == to + 16 + (row - 96) // 2))

        got = dot(rows_of(1, range(plane, 3 * half, half)), matrix((128, 128), rule, 0.125))
        ends = got if ends is None else ends + got
    copies(message, jnp.concatenate([middle, ends], axis=0))


def unpack1(pos, own, xb, xa, ext):
    has_before, has_after = pos[0] > 0, pos[0] < pos[3] - 1
    lane = lane_of((16, 128))
    per = own.shape[1] // 36

    @pl.loop(0, own.shape[0], unroll=2)
    def _(source):
        for block, (ref, there) in enumerate(((own, None), (xa, has_after), (xb, has_before))):
            for index in range(3):
                ends = ref[source, 96 + 16 * index : 112 + 16 * index, :]
                for plane in range(per):
                    at = (2 * index + plane // 2) * 16
                    value = roll(ref[source, at : at + 16, :], 64 * (plane % 2), 1)
                    value = jnp.where(lane < 80, jnp.where(lane < 64, value, roll(ends, 64 - 32 * plane, 1)), 0.0)
                    value = jnp.where(lane >= 112, roll(ends, 96 - 32 * plane, 1), value)
                    if there is not None:
                        value = jnp.where(there, value, 0.0)
                    ext[index, 4 + source * per + plane, 16 * block : 16 * block + 16, :] = value


def pass_all(weights, scaled, value, out, count, combine, level):
    @planes_of(count, level)
    def _(plane):
        middle = value[plane + 1]
        got = defect(
            scaled[plane + 4],
            [weights[index, plane + 4] for index in range(6)],
            middle,
            value[plane],
            value[plane + 2],
        )
        out(plane, combine(middle, got))


def prepare(ext, weights, diagonal, scaled, level):
    shape = scaled.shape[1:]
    count = scaled.shape[0] - 8
    for end in (0, count + 4):
        for plane in range(4):
            scaled[end + plane] = jnp.zeros(shape, F32)
            for index in range(6):
                weights[index, end + plane] = jnp.zeros(shape, F32)

    @planes_of(count, level, 4)
    def _(at):
        got, middle, inverse = coefficients(ext[2, at], ext[2, at - 1], ext[2, at + 1], ext[1, at], level)
        for index in range(6):
            weights[index, at] = got[index]
        diagonal[at] = middle
        scaled[at] = ext[0, at] * inverse


def down1(
    pos, own, xb, xa, message, weights1, scaled1, iterate1, weights2, scaled2, iterate2,
    ext1, diagonal1, start1, sums1, ext2, diagonal2, start2, sums2, thin, thick,
):
    depth = scaled1.shape[0] - 8
    for index in range(3):
        for end in (0, depth + 4):
            for plane in range(4):
                ext1[index, end + plane] = jnp.zeros((48, 128), F32)

    unpack1(pos, own, xb, xa, ext1)
    prepare(ext1, weights1, diagonal1, scaled1, 1)
    start1[0] = jnp.zeros((48, 128), F32)
    start1[depth + 1] = jnp.zeros((48, 128), F32)

    @planes_of(depth, 1)
    def _(plane):
        start1[plane + 1] = FIRST * scaled1[plane + 4]

    for end in (0, depth + 4):
        for plane in range(4):
            iterate1[end + plane] = jnp.zeros((48, 128), F32)

    def put1(plane, value):
        iterate1[plane + 4] = value

    pass_all(weights1, scaled1, start1, put1, depth, lambda value, got: value + (CARRY * value + GAIN * got), 1)

    half = depth // 2

    @planes_of(half, 1)
    def _(pair):
        total = None
        for plane in (2 * pair, 2 * pair + 1):
            got = diagonal1[plane + 4] * defect(
                scaled1[plane + 4],
                [weights1[index, plane + 4] for index in range(6)],
                iterate1[plane + 4],
                iterate1[plane + 3],
                iterate1[plane + 5],
            )
            total = got if total is None else total + got
        sums1[pair] = total
        for index in (1, 2):
            sums1[index * half + pair] = ext1[index, 2 * pair + 4] + ext1[index, 2 * pair + 5]

    @planes_of(3 * half, 1)
    def _(plane):
        thin[plane] = sums1[plane, pl.ds(0, 24, stride=2), :] + sums1[plane, pl.ds(1, 24, stride=2), :]

    def to_level2(row, lane):
        place = jnp.where(lane < 64, lane, lane - 128)
        source = lax.shift_right_arithmetic(jnp.where(row < 96, row, row - 128), 1)
        return (source == place) & ((row < 80) | (row >= 112))

    level2 = matrix((128, 128), to_level2, 0.125)
    for index in range(3):
        values = thin[index * half : (index + 1) * half].reshape(half * 24, 128)
        ext2[index, 4 : 4 + half] = dot(values, level2).reshape(half, 24, 128)
        for end in (0, half + 4):
            for plane in range(4):
                ext2[index, end + plane] = jnp.zeros((24, 128), F32)

    prepare(ext2, weights2, diagonal2, scaled2, 2)
    start2[0] = jnp.zeros((24, 128), F32)
    start2[half + 1] = jnp.zeros((24, 128), F32)

    @pl.loop(0, half)
    def _(plane):
        start2[plane + 1] = FIRST * scaled2[plane + 4]

    for end in (0, half + 4):
        for plane in range(4):
            iterate2[end + plane] = jnp.zeros((24, 128), F32)

    def put2(plane, value):
        iterate2[plane + 4] = value

    pass_all(weights2, scaled2, start2, put2, half, lambda value, got: value + (CARRY * value + GAIN * got), 2)

    quarter = half // 2
    group = quarter // 2
    place2 = [
        matrix((128, 128), lambda row, lane, at=at: (row < 32) & (lane == row // 2 + 16 * at), 0.125)
        for at in range(6)
    ]
    for index in range(3):
        for plane in range(quarter):
            if index == 0:
                total = None
                for at in (2 * plane, 2 * plane + 1):
                    got = diagonal2[at + 4] * defect(
                        scaled2[at + 4],
                        [weights2[face, at + 4] for face in range(6)],
                        iterate2[at + 4],
                        iterate2[at + 3],
                        iterate2[at + 5],
                    )
                    total = got if total is None else total + got
                total = total[0:8]
            else:
                total = ext2[index, 2 * plane + 4, 0:8, :] + ext2[index, 2 * plane + 5, 0:8, :]
            at = index * quarter + plane
            sums2[at] = total
            side, within = divmod(plane, group)
            thick[index * 2 + side, pl.ds(within, 4, stride=group), :] = (
                sums2[at, pl.ds(0, 4, stride=2), :] + sums2[at, pl.ds(1, 4, stride=2), :]
            )
    result = dot(thick[0], place2[0])
    for at in range(1, 6):
        result = result + dot(thick[at], place2[at])
    copies(message, result)


def bottom(gathered, whole, weights, scaled, update, values):
    group = weights.shape[1]
    rows = weights.shape[2]
    for index in range(3):
        total = None
        lane = lane_of(gathered.shape[1:])
        for source in range(4):
            value = gathered[source]
            for side in range(2):
                to = 64 * side + 16 * source
                moved = roll(value, to - 16 * (2 * index + side), 1)
                moved = jnp.where((lane >= to) & (lane < to + 16), moved, 0.0)
                total = moved if total is None else total + moved
        whole[index] = total
    shape = (rows, 128)
    row, lane = row_of(shape), lane_of(shape)
    column = lax.rem(lane, 64)

    def plane_at(index, plane):
        return whole[index, pl.ds(plane, rows, stride=group), :]

    def around(get, plane):
        middle = get(plane)
        below = get(plane - 1) if plane else roll(get(group - 1), 64, 1)
        above = get(plane + 1) if plane < group - 1 else roll(get(0), 64, 1)
        return [below, above] + sides(middle)

    for plane in range(group):
        beta = plane_at(2, plane)
        masks = [
            (lane >= 64) if plane == 0 else None,
            (lane < 64) if plane == group - 1 else None,
            row > 0,
            row < rows - 1,
            column > 0,
            column < 63,
        ]
        near = around(lambda at: plane_at(2, at), plane)
        near = [other if mask is None else jnp.where(mask, other, 0.0) for other, mask in zip(near, masks)]
        faces = [scale_of(3) * (beta + other) for other in near]
        diagonal = plane_at(1, plane)
        for face in faces:
            diagonal = diagonal + face
        inverse = 1.0 / diagonal
        for index, (face, mask) in enumerate(zip(faces, masks)):
            face = face * inverse
            weights[index, plane] = face if mask is None else jnp.where(mask, face, 0.0)
        scaled[plane] = plane_at(0, plane) * inverse

    steps = chebyshev(BOTTOM, bottom_low)
    for plane in range(group):
        value = steps[0][1] * scaled[plane]
        update[plane] = value
        values[0, plane] = value
    for step, (carry, gain) in enumerate(steps[1:]):
        now, later = step % 2, (step + 1) % 2
        for plane in range(group):
            middle = values[now, plane]
            got = scaled[plane] - middle
            for index, other in enumerate(around(lambda at: values[now, at], plane)):
                got = got + weights[index, plane] * other
            moved = carry * update[plane] + gain * got
            update[plane] = moved
            values[later, plane] = middle + moved


def finish(at, iterate, weights, scaled, level, update, middle, put):
    count = iterate.shape[0]

    @planes_of(count - 2, level)
    def _(plane):
        value = iterate[plane + 1]
        got = FIRST * defect(
            scaled[at + plane + 1],
            [weights[index, at + plane + 1] for index in range(6)],
            value,
            iterate[plane],
            iterate[plane + 2],
        )
        update[plane] = got
        middle[plane] = value + got

    @planes_of(count - 4, level)
    def _(plane):
        value = middle[plane + 1]
        got = defect(
            scaled[at + plane + 2],
            [weights[index, at + plane + 2] for index in range(6)],
            value,
            middle[plane],
            middle[plane + 2],
        )
        put(plane, value + (CARRY * update[plane + 1] + GAIN * got))


def up(
    pos, gathered, weights2, scaled2, iterate2, weights1, scaled1, iterate1,
    weights0, diagonal0, scaled0, iterate0, solved, left_over,
    whole3, weights3, scaled3, update3, values3,
    thin3, error2, value2, update2, middle2, out2,
    tall1, value1, update1, middle1, out1,
    tall0, value0, update0, middle0, out0,
):
    bottom(gathered, whole3, weights3, scaled3, update3, values3)
    group, rows = weights3.shape[1], weights3.shape[2]
    at_x, at_y, at_z = 4 * pos[0], 16 * pos[1], pos[2]
    last = (BOTTOM - 1) % 2

    lane = lane_of((8, 128))
    near = lax.rem(lane, 64)
    fits = ((near < 16) | ((near < 20) & (pos[1] < 3)) | ((near >= 60) & (pos[1] > 0))).astype(F32)
    first_row, last_row = (pos[0] > 0).astype(F32), (pos[0] < pos[3] - 1).astype(F32)
    low = row_of((8, 128)) < 4
    own = jnp.where(low, fits, fits * last_row)
    left = jnp.where(low, 0.0, fits * first_row)
    for plane in range(group):
        moved = pltpu.roll(values3[last, plane], lax.rem(rows - at_x, rows), 0)
        both = jnp.concatenate([moved[0:8], moved[rows - 8 :]], axis=0)
        both = pltpu.roll(both, lax.rem(128 - at_y, 128), 1)
        ahead, behind = both[0:8] * own, both[8:16] * left
        for start in (0, 1):
            thin3[plane, pl.ds(start, 8, stride=2), :] = ahead
            thin3[plane, pl.ds(16 + start, 4, stride=2), :] = behind[4:8]

    def to_level2(row, lane):
        side, within = lane // 128, lax.rem(lane, 128)
        place = jnp.where(within < 64, within, within - 128)
        source = jnp.where(side == 0, lax.rem(row, 128), lax.rem(row + 64, 128))
        source = jnp.where(source < 64, source, source - 128)
        return (source == lax.shift_right_arithmetic(place, 1)) & ((within < 40) | (within >= 120))

    spread = dot(thin3[...].reshape(group * 24, 128), matrix((128, 256), to_level2)).reshape(group, 24, 256)
    for plane in range(group):
        for side in range(2):
            error2[side * group + plane + 2] = spread[plane, :, 128 * side : 128 * side + 128]
    for end in (0, 2 * group + 2):
        for plane in range(2):
            error2[end + plane] = jnp.zeros((24, 128), F32)

    for plane in range(10):
        value2[plane] = iterate2[2 * at_z + plane] + error2[at_z + plane // 2]

    def put2(plane, value):
        out2[plane] = value

    finish(2 * at_z, value2, weights2, scaled2, 2, update2, middle2, put2)

    def to_level1(row, lane):
        place = jnp.where(lane < 96, lane, lane - 128)
        source = lax.shift_right_arithmetic(place, 1)
        return (jnp.where(row < 64, row, row - 128) == source) & ((lane < 80) | (lane >= 112))

    wide1 = matrix((128, 128), to_level1)
    for plane in range(6):
        tall1[plane, pl.ds(0, 24, stride=2), :] = out2[plane]
        tall1[plane, pl.ds(1, 24, stride=2), :] = out2[plane]
    spread = dot(tall1[...].reshape(6 * 48, 128), wide1).reshape(6, 48, 128)
    for plane in range(12):
        value1[plane] = iterate1[4 * at_z + plane] + spread[plane // 2]

    def put1(plane, value):
        out1[plane] = value

    finish(4 * at_z, value1, weights1, scaled1, 1, update1, middle1, put1)

    def to_level0(row, lane):
        place = jnp.where(lane < 192, lane, lane - 256)
        source = lax.shift_right_arithmetic(place, 1)
        return (jnp.where(row < 96, row, row - 128) == source) & ((lane < 136) | (lane >= 248))

    wide0 = matrix((128, 256), to_level0)
    for plane in range(8):
        value = out1[plane]
        tall0[plane, pl.ds(0, 24, stride=2), :] = value[0:24]
        tall0[plane, pl.ds(1, 24, stride=2), :] = value[0:24]
        tall0[plane, pl.ds(40, 4, stride=2), :] = value[44:48]
        tall0[plane, pl.ds(41, 4, stride=2), :] = value[44:48]

    @planes_of(8, 1)
    def _(plane):
        value = dot(tall0[plane], wide0)
        out0[2 * plane] = value
        out0[2 * plane + 1] = value

    @planes_of(iterate0.shape[0], 0)
    def _(plane):
        value0[plane] = iterate0[plane] + out0[plane + 1]

    count = iterate0.shape[0]

    @planes_of(count - 2, 0)
    def _(plane):
        value = value0[plane + 1]
        got = FIRST * defect(
            scaled0[plane + 2],
            [weights0[index, plane + 2] for index in range(6)],
            value,
            value0[plane],
            value0[plane + 2],
        )
        update0[plane] = got
        middle0[plane] = value + got

    @planes_of(count - 4, 0)
    def _(plane):
        value = middle0[plane + 1]
        got = defect(
            scaled0[plane + 3],
            [weights0[index, plane + 3] for index in range(6)],
            value,
            middle0[plane],
            middle0[plane + 2],
        )
        out0[plane] = value + (CARRY * update0[plane + 1] + GAIN * got)

    @planes_of(count - 6, 0)
    def _(plane):
        value = out0[plane + 1]
        solved[plane] = value[0:32, 0:128]
        left_over[plane] = residual0(
            weights0, diagonal0, scaled0, value, out0[plane], out0[plane + 2], plane + 4, 128
        )


def call(body, name, outs, scratch, pos, args):
    vmem = pl.BlockSpec(memory_space=pltpu.VMEM)
    smem = [pl.BlockSpec(memory_space=pltpu.SMEM)] if pos is not None else []
    operands = ([pos] if pos is not None else []) + list(args)
    return pl.pallas_call(
        body,
        name=name,
        out_shape=[jax.ShapeDtypeStruct(shape, F32) for shape in outs],
        in_specs=smem + [vmem] * len(args),
        out_specs=[vmem] * len(outs),
        scratch_shapes=[pltpu.VMEM(shape, F32) for shape in scratch],
        compiler_params=pltpu.CompilerParams(vmem_limit_bytes=32 * 2**20),
    )(*operands)


def exchange(up_values, down_values, axis, ring):
    peers = lax.axis_size(axis)
    up_pairs = [(i, (i + 1) % peers) for i in range(peers if ring else peers - 1)]
    down_pairs = [(j, i) for i, j in up_pairs]
    return lax.ppermute(up_values, axis, up_pairs), lax.ppermute(down_values, axis, down_pairs)


def on_device(right_side, acoef, beta):
    ranks, turns, files = [lax.axis_size(axis) for axis in AXES]
    pos = jnp.stack([lax.axis_index(axis) for axis in AXES] + [jnp.int32(ranks)]).astype(jnp.int32)
    planes = right_side.shape[0]
    arrays = (right_side, acoef, beta)

    last = jnp.stack([value[planes - DEEP :] for value in arrays])
    first = jnp.stack([value[:DEEP] for value in arrays])
    zb, za = exchange(last, first, "gz", False)
    own = jnp.stack(arrays)
    shape = (sum(planes + 2 * reach - 2 for reach in REACH), 8, 128)
    last, first = call(packx, "packx", [shape, shape], [], None, (own, zb, za))
    xb, xa = exchange(last, first, "gx", True)
    depth = planes + 2 * DEEP
    tiles = max(tile for _, _, tile, _, _ in slots(depth)) + 1
    whole0, left, right = call(
        pack0, "pack0", [(3, depth, 48, 128)] + [(tiles, 40, 128)] * 2, [], pos, (own, zb, za, xb, xa)
    )
    before0, after0 = exchange(right, left, "gy", False)
    plane0 = (48, 256)
    half = planes // 2
    iterate0, message, weights0, diagonal0, scaled0 = call(
        down0,
        "down0",
        [(depth - 4,) + plane0, (files, 36 * half, 128), (6, depth - 2) + plane0] + [(depth - 2,) + plane0] * 2,
        [(3, depth) + plane0, (depth - 2,) + plane0, (2, 3 * half, 32, 128)],
        None,
        (whole0, before0, after0),
    )

    whole1 = lax.all_to_all(message, "gz", 0, 0)
    xb, xa = exchange(whole1, whole1, "gx", True)
    depth1 = files * half
    plane1, plane2 = (48, 128), (24, 128)
    depth2 = depth1 // 2
    group = depth2 // 4
    tall1, tall2 = (depth1 + 8,) + plane1, (depth2 + 8,) + plane2
    message, weights1, scaled1, iterate1, weights2, scaled2, iterate2 = call(
        down1,
        "down1",
        [(ranks, 4 * group, 128), (6,) + tall1, tall1, tall1, (6,) + tall2, tall2, tall2],
        [(3,) + tall1, tall1, (depth1 + 2,) + plane1, (3 * depth2,) + plane1]
        + [(3,) + tall2, tall2, (depth2 + 2,) + plane2, (3 * depth2 // 2, 8, 128)]
        + [(3 * depth2,) + plane2, (6, 4 * group, 128)],
        pos,
        (whole1, xb, xa),
    )

    gathered = lax.all_to_all(message, "gx", 0, 0)
    gathered = gathered.reshape(1, ranks * 4 * group, 128)
    gathered = jnp.broadcast_to(gathered, (turns,) + gathered.shape[1:])
    gathered = lax.all_to_all(gathered, "gy", 0, 0)

    rows3 = 4 * ranks
    plane3 = (rows3, 128)
    solved, left_over = call(
        up,
        "up",
        [right_side.shape, right_side.shape],
        [(3, rows3 * group, 128), (6, group) + plane3, (group,) + plane3, (group,) + plane3, (2, group) + plane3]
        + [(group,) + plane2, (2 * group + 4,) + plane2, (10,) + plane2, (8,) + plane2, (8,) + plane2, (6,) + plane2]
        + [(6,) + plane1, (12,) + plane1, (10,) + plane1, (10,) + plane1, (8,) + plane1]
        + [(8,) + plane1, (depth - 4,) + plane0, (depth - 6,) + plane0, (depth - 6,) + plane0, (depth - 2,) + plane0],
        pos,
        (gathered, weights2, scaled2, iterate2, weights1, scaled1, iterate1)
        + (weights0, diagonal0, scaled0, iterate0),
    )
    return solved, left_over


def solution(mesh):
    spec = P("gz", "gx", "gy")
    return jax.shard_map(
        on_device, mesh=mesh, in_specs=(spec, spec, spec), out_specs=(spec, spec), check_vma=False
    )
```

```python
import functools

import jax
import jax.numpy as jnp
from jax import lax
from jax.experimental import pallas as pl
from jax.experimental.pallas import tpu as pltpu
from jax.sharding import PartitionSpec as P

LEVELS = 4
SWEEPS = 2
BOTTOM = 16

smooth_low = 0.3
bottom_low = 0.05
upper_bound = 2.0
face_scale = 1.0 / 6.0

F32 = jnp.float32
AXES = ("gx", "gy", "gz")
REACH = (4, 4, 5)
DEEP = 5


def chebyshev(steps, lower):
    centre = (upper_bound + lower) / 2.0
    half_width = (upper_bound - lower) / 2.0
    sigma = centre / half_width
    rho = 1.0 / sigma
    out = [(0.0, 1.0 / centre)]
    for _ in range(1, steps):
        rho_next = 1.0 / (2.0 * sigma - rho)
        out.append((rho_next * rho, 2.0 * rho_next / half_width))
        rho = rho_next
    return out


(_, FIRST), (CARRY, GAIN) = chebyshev(SWEEPS, smooth_low)


def roll(value, shift, axis):
    shift %= value.shape[axis]
    return pltpu.roll(value, shift, axis) if shift else value


def lane_of(shape):
    return lax.broadcasted_iota(jnp.int32, shape, 1)


def row_of(shape):
    return lax.broadcasted_iota(jnp.int32, shape, 0)


def sides(value):
    return [roll(value, 1, 0), roll(value, -1, 0), roll(value, 1, 1), roll(value, -1, 1)]


def scale_of(level):
    return face_scale * 0.25**level * 0.5


def coefficients(beta, below, above, acoef, level):
    weights = [scale_of(level) * (beta + other) for other in [below, above] + sides(beta)]
    diagonal = acoef
    for weight in weights:
        diagonal = diagonal + weight
    inside = beta > 0.0
    inverse = jnp.where(inside, 1.0 / jnp.where(inside, diagonal, 1.0), 0.0)
    return [weight * inverse for weight in weights], diagonal, inverse


def defect(scaled, weights, value, below, above):
    result = scaled - value
    for weight, other in zip(weights, [below, above] + sides(value)):
        result = result + weight * other
    return result


def dot(left, right):
    return jnp.dot(left, right, precision=lax.Precision.HIGHEST, preferred_element_type=F32)


def matrix(shape, rule, value=1.0):
    return jnp.where(rule(row_of(shape), lane_of(shape)), value, 0.0).astype(F32)


def copies(ref, value):
    for index in range(ref.shape[0]):
        ref[index] = value


def away(plane, depth):
    return max(DEEP - plane, plane - (depth - 1 - DEEP), 0)


def slots(depth):
    wide, narrow = [], []
    for index, reach in enumerate(REACH):
        for plane in range(depth):
            if away(plane, depth) < reach:
                (wide if away(plane, depth) <= reach - 2 else narrow).append((index, plane))
    out = [(index, plane, at // 4, 32 * (at % 4), 32) for at, (index, plane) in enumerate(wide)]
    first = -(-len(wide) // 4)
    return out + [(index, plane, first + at // 16, 8 * (at % 16), 8) for at, (index, plane) in enumerate(narrow)]


def masked(pos, xb, xa, index):
    before = jnp.where(pos[0] > 0, xb[index], 0.0)
    return before, jnp.where(pos[0] < pos[3] - 1, xa[index], 0.0)


def packz(pos, own, xb, xa, last, first):
    planes, at = own.shape[1], 0
    four = lax.broadcasted_iota(jnp.int32, xb.shape[1:], 1) < 4
    for index, reach in enumerate(REACH):
        before, after = masked(pos, xb, xa, index)
        ends = jnp.where(four, after, before)
        last[at : at + reach, 0:32, :] = own[index, planes - reach :]
        last[at : at + reach, 32:40, :] = ends[planes - reach :]
        first[at : at + reach, 0:32, :] = own[index, :reach]
        first[at : at + reach, 32:40, :] = ends[:reach]
        at += reach


def pack0(pos, own, xb, xa, zb, za, whole, left, right):
    planes = own.shape[1]
    depth = planes + 2 * DEEP
    at = 0
    for index, reach in enumerate(REACH):
        for plane in range(DEEP - reach):
            for end in (plane, depth - 1 - plane):
                whole[index, end] = jnp.zeros((48, 128), F32)
        for ref, start in ((zb, DEEP - reach), (za, DEEP + planes)):
            whole[index, start : start + reach, 0:40, :] = ref[at : at + reach]
            whole[index, start : start + reach, 40:48, :] = ref[at : at + reach, 32:40, :]
        before, after = masked(pos, xb, xa, index)
        whole[index, DEEP : DEEP + planes, 0:32, :] = own[index]
        whole[index, DEEP : DEEP + planes, 32:40, :] = after
        whole[index, DEEP : DEEP + planes, 40:48, :] = before
        at += reach
    lane = lane_of((40, 128))
    four = row_of((8, 128)) < 4
    low, high = {}, {}
    for index, plane, tile, to, lanes in slots(depth):
        ends = jnp.where(four, whole[index, plane, 32:40, :], whole[index, plane, 40:48, :])
        value = jnp.concatenate([whole[index, plane, 0:32, :], ends], axis=0)
        here = (lane >= to) & (lane < to + lanes)
        zero = jnp.zeros((40, 128), F32)
        low[tile] = jnp.where(here, roll(value, to, 1), low.get(tile, zero))
        high[tile] = jnp.where(here, roll(value, to + lanes, 1), high.get(tile, zero))
    for tile in low:
        left[tile] = low[tile]
        right[tile] = high[tile]


def unpack0(whole, before, after, ext):
    depth = whole.shape[1]
    ext[:, :, :, 0:128] = whole[...]
    lane = lane_of((40, 128))
    there = {(index, plane): rest for index, plane, *rest in slots(depth)}
    for index in range(3):
        for plane in range(depth):
            if (index, plane) not in there:
                ext[index, plane, :, 128:256] = jnp.zeros((48, 128), F32)
                continue
            tile, to, lanes = there[index, plane]
            ahead = jnp.where(lane < lanes, roll(after[tile], -to, 1), 0.0)
            value = jnp.where(lane >= 128 - lanes, roll(before[tile], -lanes - to, 1), ahead)
            ext[index, plane, 0:40, 128:256] = value
            ext[index, plane, 40:48, 128:256] = value[32:40]


def planes_of(count, level, start=0):
    most = (7, 10, 16)[level]
    return pl.loop(start, start + count, unroll=max(n for n in range(1, most + 1) if count % n == 0))


def prepare0(ext, weights, diagonal, scaled):
    @planes_of(diagonal.shape[0], 0)
    def _(plane):
        got, middle, inverse = coefficients(
            ext[2, plane + 1], ext[2, plane], ext[2, plane + 2], ext[1, plane + 1], 0
        )
        for index in range(6):
            weights[index, plane] = got[index]
        diagonal[plane] = middle
        scaled[plane] = ext[0, plane + 1] * inverse


def residual0(weights, diagonal, scaled, value, below, above, at, lanes):
    cut = lambda array: array[0:32, 0:lanes]
    result = scaled[at, 0:32, 0:lanes] - cut(value)
    for index, other in enumerate([below, above] + sides(value)):
        result = result + weights[index, at, 0:32, 0:lanes] * cut(other)
    return diagonal[at, 0:32, 0:lanes] * result


def down0(whole, before, after, iterate, message, weights, diagonal, scaled, ext, start, sums):
    unpack0(whole, before, after, ext)
    prepare0(ext, weights, diagonal, scaled)

    @planes_of(start.shape[0], 0)
    def _(plane):
        start[plane] = FIRST * scaled[plane]

    @planes_of(iterate.shape[0], 0)
    def _(plane):
        value = start[plane + 1]
        got = defect(
            scaled[plane + 1],
            [weights[index, plane + 1] for index in range(6)],
            value,
            start[plane],
            start[plane + 2],
        )
        iterate[plane] = value + (CARRY * value + GAIN * got)

    planes = whole.shape[1] - 2 * DEEP

    def left_over(plane):
        return residual0(
            weights, diagonal, scaled, iterate[plane + 3], iterate[plane + 2], iterate[plane + 4], plane + 4, 256
        )

    half = planes // 2

    @planes_of(half, 0)
    def _(plane):
        pairs = [left_over(2 * plane) + left_over(2 * plane + 1)]
        for index in (1, 2):
            low = ext[index, DEEP + 2 * plane, 0:32, :]
            pairs.append(low + ext[index, DEEP + 2 * plane + 1, 0:32, :])
        for index, value in enumerate(pairs):
            sums[0, index * half + plane] = value[:, 0:128]
            sums[1, index * half + plane] = value[:, 128:256]

    def rows_of(side, places):
        tall = [
            sums[side, place, pl.ds(0, 16, stride=2), :] + sums[side, place, pl.ds(1, 16, stride=2), :]
            for place in places
        ]
        return jnp.concatenate(tall, axis=0)

    even = matrix((128, 128), lambda row, lane: lane == row // 2, 0.125)
    odd = matrix((128, 128), lambda row, lane: lane == row // 2 + 64, 0.125)
    middle = dot(rows_of(0, range(0, 3 * half, 2)), even) + dot(rows_of(0, range(1, 3 * half, 2)), odd)
    ends = None
    for plane in range(half):

        def rule(row, lane, to=32 * plane):
            ahead = (row < 32) & (lane == to + row // 2)
            return ahead | ((row >= 96) & (lane == to + 16 + (row - 96) // 2))

        got = dot(rows_of(1, range(plane, 3 * half, half)), matrix((128, 128), rule, 0.125))
        ends = got if ends is None else ends + got
    copies(message, jnp.concatenate([middle, ends], axis=0))


def unpack1(pos, own, xb, xa, ext):
    has_before, has_after = pos[0] > 0, pos[0] < pos[3] - 1
    lane = lane_of((16, 128))
    per = own.shape[1] // 36

    @pl.loop(0, own.shape[0], unroll=2)
    def _(source):
        for block, (ref, there) in enumerate(((own, None), (xa, has_after), (xb, has_before))):
            for index in range(3):
                ends = ref[source, 96 + 16 * index : 112 + 16 * index, :]
                for plane in range(per):
                    at = (2 * index + plane // 2) * 16
                    value = roll(ref[source, at : at + 16, :], 64 * (plane % 2), 1)
                    value = jnp.where(lane < 80, jnp.where(lane < 64, value, roll(ends, 64 - 32 * plane, 1)), 0.0)
                    value = jnp.where(lane >= 112, roll(ends, 96 - 32 * plane, 1), value)
                    if there is not None:
                        value = jnp.where(there, value, 0.0)
                    ext[index, 4 + source * per + plane, 16 * block : 16 * block + 16, :] = value


def pass_all(weights, scaled, value, out, count, combine, level):
    @planes_of(count, level)
    def _(plane):
        middle = value[plane + 1]
        got = defect(
            scaled[plane + 4],
            [weights[index, plane + 4] for index in range(6)],
            middle,
            value[plane],
            value[plane + 2],
        )
        out(plane, combine(middle, got))


def prepare(ext, weights, diagonal, scaled, level):
    shape = scaled.shape[1:]
    count = scaled.shape[0] - 8
    for end in (0, count + 4):
        for plane in range(4):
            scaled[end + plane] = jnp.zeros(shape, F32)
            for index in range(6):
                weights[index, end + plane] = jnp.zeros(shape, F32)

    @planes_of(count, level, 4)
    def _(at):
        got, middle, inverse = coefficients(ext[2, at], ext[2, at - 1], ext[2, at + 1], ext[1, at], level)
        for index in range(6):
            weights[index, at] = got[index]
        diagonal[at] = middle
        scaled[at] = ext[0, at] * inverse


def down1(
    pos, own, xb, xa, message, weights1, scaled1, iterate1, weights2, scaled2, iterate2,
    ext1, diagonal1, start1, sums1, ext2, diagonal2, start2, sums2, thin, thick,
):
    depth = scaled1.shape[0] - 8
    for index in range(3):
        for end in (0, depth + 4):
            for plane in range(4):
                ext1[index, end + plane] = jnp.zeros((48, 128), F32)

    unpack1(pos, own, xb, xa, ext1)
    prepare(ext1, weights1, diagonal1, scaled1, 1)
    start1[0] = jnp.zeros((48, 128), F32)
    start1[depth + 1] = jnp.zeros((48, 128), F32)

    @planes_of(depth, 1)
    def _(plane):
        start1[plane + 1] = FIRST * scaled1[plane + 4]

    for end in (0, depth + 4):
        for plane in range(4):
            iterate1[end + plane] = jnp.zeros((48, 128), F32)

    def put1(plane, value):
        iterate1[plane + 4] = value

    pass_all(weights1, scaled1, start1, put1, depth, lambda value, got: value + (CARRY * value + GAIN * got), 1)

    half = depth // 2

    @planes_of(half, 1)
    def _(pair):
        total = None
        for plane in (2 * pair, 2 * pair + 1):
            got = diagonal1[plane + 4] * defect(
                scaled1[plane + 4],
                [weights1[index, plane + 4] for index in range(6)],
                iterate1[plane + 4],
                iterate1[plane + 3],
                iterate1[plane + 5],
            )
            total = got if total is None else total + got
        sums1[pair] = total
        for index in (1, 2):
            sums1[index * half + pair] = ext1[index, 2 * pair + 4] + ext1[index, 2 * pair + 5]

    @planes_of(3 * half, 1)
    def _(plane):
        thin[plane] = sums1[plane, pl.ds(0, 24, stride=2), :] + sums1[plane, pl.ds(1, 24, stride=2), :]

    def to_level2(row, lane):
        place = jnp.where(lane < 64, lane, lane - 128)
        source = lax.shift_right_arithmetic(jnp.where(row < 96, row, row - 128), 1)
        return (source == place) & ((row < 80) | (row >= 112))

    level2 = matrix((128, 128), to_level2, 0.125)
    for index in range(3):
        values = thin[index * half : (index + 1) * half].reshape(half * 24, 128)
        ext2[index, 4 : 4 + half] = dot(values, level2).reshape(half, 24, 128)
        for end in (0, half + 4):
            for plane in range(4):
                ext2[index, end + plane] = jnp.zeros((24, 128), F32)

    prepare(ext2, weights2, diagonal2, scaled2, 2)
    start2[0] = jnp.zeros((24, 128), F32)
    start2[half + 1] = jnp.zeros((24, 128), F32)

    @pl.loop(0, half)
    def _(plane):
        start2[plane + 1] = FIRST * scaled2[plane + 4]

    for end in (0, half + 4):
        for plane in range(4):
            iterate2[end + plane] = jnp.zeros((24, 128), F32)

    def put2(plane, value):
        iterate2[plane + 4] = value

    pass_all(weights2, scaled2, start2, put2, half, lambda value, got: value + (CARRY * value + GAIN * got), 2)

    quarter = half // 2
    group = quarter // 2
    place2 = []
    for at in range(6):
        to = 64 * (at % 2) + 16 * lax.rem(pos[1] + at // 2, 4)
        place2.append(matrix((128, 128), lambda row, lane, to=to: (row < 32) & (lane == row // 2 + to), 0.125))
    for index in range(3):
        for plane in range(quarter):
            if index == 0:
                total = None
                for at in (2 * plane, 2 * plane + 1):
                    got = diagonal2[at + 4] * defect(
                        scaled2[at + 4],
                        [weights2[face, at + 4] for face in range(6)],
                        iterate2[at + 4],
                        iterate2[at + 3],
                        iterate2[at + 5],
                    )
                    total = got if total is None else total + got
                total = total[0:8]
            else:
                total = ext2[index, 2 * plane + 4, 0:8, :] + ext2[index, 2 * plane + 5, 0:8, :]
            at = index * quarter + plane
            sums2[at] = total
            side, within = divmod(plane, group)
            thick[index * 2 + side, pl.ds(within, 4, stride=group), :] = (
                sums2[at, pl.ds(0, 4, stride=2), :] + sums2[at, pl.ds(1, 4, stride=2), :]
            )
    result = dot(thick[0], place2[0])
    for at in range(1, 6):
        result = result + dot(thick[at], place2[at])
    copies(message, result)


def bottom(gathered, whole, weights, scaled, update, values):
    group = weights.shape[1]
    rows = weights.shape[2]
    place = lax.rem(lane_of(gathered.shape[1:]) // 16, 4)
    for index in range(3):
        total = gathered[0]
        for source in range(1, 4):
            total = jnp.where(place == (source + index) % 4, gathered[source], total)
        if index:
            total = jnp.where(place + index < 4, roll(total, -16 * index, 1), roll(total, 64 - 16 * index, 1))
        whole[index] = total
    shape = (rows, 128)
    row, lane = row_of(shape), lane_of(shape)
    column = lax.rem(lane, 64)

    def plane_at(index, plane):
        return whole[index, pl.ds(plane, rows, stride=group), :]

    def around(get, plane):
        middle = get(plane)
        below = get(plane - 1) if plane else roll(get(group - 1), 64, 1)
        above = get(plane + 1) if plane < group - 1 else roll(get(0), 64, 1)
        return [below, above] + sides(middle)

    for plane in range(group):
        beta = plane_at(2, plane)
        masks = [
            (lane >= 64) if plane == 0 else None,
            (lane < 64) if plane == group - 1 else None,
            row > 0,
            row < rows - 1,
            column > 0,
            column < 63,
        ]
        near = around(lambda at: plane_at(2, at), plane)
        near = [other if mask is None else jnp.where(mask, other, 0.0) for other, mask in zip(near, masks)]
        faces = [scale_of(3) * (beta + other) for other in near]
        diagonal = plane_at(1, plane)
        for face in faces:
            diagonal = diagonal + face
        inverse = 1.0 / diagonal
        for index, (face, mask) in enumerate(zip(faces, masks)):
            face = face * inverse
            weights[index, plane] = face if mask is None else jnp.where(mask, face, 0.0)
        scaled[plane] = plane_at(0, plane) * inverse

    steps = chebyshev(BOTTOM, bottom_low)
    for plane in range(group):
        value = steps[0][1] * scaled[plane]
        update[plane] = value
        values[0, plane] = value
    for step, (carry, gain) in enumerate(steps[1:]):
        now, later = step % 2, (step + 1) % 2
        for plane in range(group):
            middle = values[now, plane]
            got = scaled[plane] - middle
            for index, other in enumerate(around(lambda at: values[now, at], plane)):
                got = got + weights[index, plane] * other
            moved = carry * update[plane] + gain * got
            update[plane] = moved
            values[later, plane] = middle + moved


def finish(at, iterate, weights, scaled, level, update, middle, put):
    count = iterate.shape[0]

    @planes_of(count - 2, level)
    def _(plane):
        value = iterate[plane + 1]
        got = FIRST * defect(
            scaled[at + plane + 1],
            [weights[index, at + plane + 1] for index in range(6)],
            value,
            iterate[plane],
            iterate[plane + 2],
        )
        update[plane] = got
        middle[plane] = value + got

    @planes_of(count - 4, level)
    def _(plane):
        value = middle[plane + 1]
        got = defect(
            scaled[at + plane + 2],
            [weights[index, at + plane + 2] for index in range(6)],
            value,
            middle[plane],
            middle[plane + 2],
        )
        put(plane, value + (CARRY * update[plane + 1] + GAIN * got))


def up(
    pos, gathered, weights2, scaled2, iterate2, weights1, scaled1, iterate1,
    weights0, diagonal0, scaled0, iterate0, solved, left_over,
    whole3, weights3, scaled3, update3, values3,
    thin3, error2, value2, update2, middle2, out2,
    tall1, value1, update1, middle1, out1,
    tall0, value0, update0, middle0, out0,
):
    bottom(gathered, whole3, weights3, scaled3, update3, values3)
    group, rows = weights3.shape[1], weights3.shape[2]
    at_x, at_y, at_z = 4 * pos[0], 16 * pos[1], pos[2]
    last = (BOTTOM - 1) % 2

    lane = lane_of((8, 128))
    near = lax.rem(lane, 64)
    fits = ((near < 16) | ((near < 20) & (pos[1] < 3)) | ((near >= 60) & (pos[1] > 0))).astype(F32)
    first_row, last_row = (pos[0] > 0).astype(F32), (pos[0] < pos[3] - 1).astype(F32)
    low = row_of((8, 128)) < 4
    own = jnp.where(low, fits, fits * last_row)
    left = jnp.where(low, 0.0, fits * first_row)
    for plane in range(group):
        moved = pltpu.roll(values3[last, plane], lax.rem(rows - at_x, rows), 0)
        both = jnp.concatenate([moved[0:8], moved[rows - 8 :]], axis=0)
        both = pltpu.roll(both, lax.rem(128 - at_y, 128), 1)
        ahead, behind = both[0:8] * own, both[8:16] * left
        for start in (0, 1):
            thin3[plane, pl.ds(start, 8, stride=2), :] = ahead
            thin3[plane, pl.ds(16 + start, 4, stride=2), :] = behind[4:8]

    def to_level2(row, lane):
        side, within = lane // 128, lax.rem(lane, 128)
        place = jnp.where(within < 64, within, within - 128)
        source = jnp.where(side == 0, lax.rem(row, 128), lax.rem(row + 64, 128))
        source = jnp.where(source < 64, source, source - 128)
        return (source == lax.shift_right_arithmetic(place, 1)) & ((within < 40) | (within >= 120))

    spread = dot(thin3[...].reshape(group * 24, 128), matrix((128, 256), to_level2)).reshape(group, 24, 256)
    for plane in range(group):
        for side in range(2):
            error2[side * group + plane + 2] = spread[plane, :, 128 * side : 128 * side + 128]
    for end in (0, 2 * group + 2):
        for plane in range(2):
            error2[end + plane] = jnp.zeros((24, 128), F32)

    for plane in range(10):
        value2[plane] = iterate2[2 * at_z + plane] + error2[at_z + plane // 2]

    def put2(plane, value):
        out2[plane] = value

    finish(2 * at_z, value2, weights2, scaled2, 2, update2, middle2, put2)

    def to_level1(row, lane):
        place = jnp.where(lane < 96, lane, lane - 128)
        source = lax.shift_right_arithmetic(place, 1)
        return (jnp.where(row < 64, row, row - 128) == source) & ((lane < 80) | (lane >= 112))

    wide1 = matrix((128, 128), to_level1)
    for plane in range(6):
        tall1[plane, pl.ds(0, 24, stride=2), :] = out2[plane]
        tall1[plane, pl.ds(1, 24, stride=2), :] = out2[plane]
    spread = dot(tall1[...].reshape(6 * 48, 128), wide1).reshape(6, 48, 128)
    for plane in range(12):
        value1[plane] = iterate1[4 * at_z + plane] + spread[plane // 2]

    def put1(plane, value):
        out1[plane] = value

    finish(4 * at_z, value1, weights1, scaled1, 1, update1, middle1, put1)

    def to_level0(row, lane):
        place = jnp.where(lane < 192, lane, lane - 256)
        source = lax.shift_right_arithmetic(place, 1)
        return (jnp.where(row < 96, row, row - 128) == source) & ((lane < 136) | (lane >= 248))

    wide0 = matrix((128, 256), to_level0)
    for plane in range(8):
        value = out1[plane]
        tall0[plane, pl.ds(0, 24, stride=2), :] = value[0:24]
        tall0[plane, pl.ds(1, 24, stride=2), :] = value[0:24]
        tall0[plane, pl.ds(40, 4, stride=2), :] = value[44:48]
        tall0[plane, pl.ds(41, 4, stride=2), :] = value[44:48]

    @planes_of(8, 1)
    def _(plane):
        value = dot(tall0[plane], wide0)
        out0[2 * plane] = value
        out0[2 * plane + 1] = value

    @planes_of(iterate0.shape[0], 0)
    def _(plane):
        value0[plane] = iterate0[plane] + out0[plane + 1]

    count = iterate0.shape[0]

    @planes_of(count - 2, 0)
    def _(plane):
        value = value0[plane + 1]
        got = FIRST * defect(
            scaled0[plane + 2],
            [weights0[index, plane + 2] for index in range(6)],
            value,
            value0[plane],
            value0[plane + 2],
        )
        update0[plane] = got
        middle0[plane] = value + got

    @planes_of(count - 4, 0)
    def _(plane):
        value = middle0[plane + 1]
        got = defect(
            scaled0[plane + 3],
            [weights0[index, plane + 3] for index in range(6)],
            value,
            middle0[plane],
            middle0[plane + 2],
        )
        out0[plane] = value + (CARRY * update0[plane + 1] + GAIN * got)

    @planes_of(count - 6, 0)
    def _(plane):
        value = out0[plane + 1]
        solved[plane] = value[0:32, 0:128]
        left_over[plane] = residual0(
            weights0, diagonal0, scaled0, value, out0[plane], out0[plane + 2], plane + 4, 128
        )


def call(body, name, outs, scratch, pos, args):
    vmem = pl.BlockSpec(memory_space=pltpu.VMEM)
    smem = [pl.BlockSpec(memory_space=pltpu.SMEM)] if pos is not None else []
    operands = ([pos] if pos is not None else []) + list(args)
    return pl.pallas_call(
        body,
        name=name,
        out_shape=[jax.ShapeDtypeStruct(shape, F32) for shape in outs],
        in_specs=smem + [vmem] * len(args),
        out_specs=[vmem] * len(outs),
        scratch_shapes=[pltpu.VMEM(shape, F32) for shape in scratch],
        compiler_params=pltpu.CompilerParams(vmem_limit_bytes=32 * 2**20),
    )(*operands)


def exchange(up_values, down_values, axis, ring):
    peers = lax.axis_size(axis)
    up_pairs = [(i, (i + 1) % peers) for i in range(peers if ring else peers - 1)]
    down_pairs = [(j, i) for i, j in up_pairs]
    return lax.ppermute(up_values, axis, up_pairs), lax.ppermute(down_values, axis, down_pairs)


def on_device(right_side, acoef, beta):
    ranks, turns, files = [lax.axis_size(axis) for axis in AXES]
    pos = jnp.stack([lax.axis_index(axis) for axis in AXES] + [jnp.int32(ranks)]).astype(jnp.int32)
    planes = right_side.shape[0]
    arrays = (right_side, acoef, beta)

    last = jnp.stack([value[:, 24:] for value in arrays])
    first = jnp.stack([value[:, :8] for value in arrays])
    xb, xa = exchange(last, first, "gx", True)
    own = jnp.stack(arrays)
    last, first = call(packz, "packz", [(sum(REACH), 40, 128)] * 2, [], pos, (own, xb, xa))
    zb, za = exchange(last, first, "gz", False)
    depth = planes + 2 * DEEP
    tiles = max(tile for _, _, tile, _, _ in slots(depth)) + 1
    whole0, left, right = call(
        pack0, "pack0", [(3, depth, 48, 128)] + [(tiles, 40, 128)] * 2, [], pos, (own, xb, xa, zb, za)
    )
    before0, after0 = exchange(right, left, "gy", False)
    plane0 = (48, 256)
    half = planes // 2
    iterate0, message, weights0, diagonal0, scaled0 = call(
        down0,
        "down0",
        [(depth - 4,) + plane0, (files, 36 * half, 128), (6, depth - 2) + plane0] + [(depth - 2,) + plane0] * 2,
        [(3, depth) + plane0, (depth - 2,) + plane0, (2, 3 * half, 32, 128)],
        None,
        (whole0, before0, after0),
    )

    whole1 = lax.all_to_all(message, "gz", 0, 0)
    xb, xa = exchange(whole1, whole1, "gx", True)
    depth1 = files * half
    plane1, plane2 = (48, 128), (24, 128)
    depth2 = depth1 // 2
    group = depth2 // 4
    tall1, tall2 = (depth1 + 8,) + plane1, (depth2 + 8,) + plane2
    message, weights1, scaled1, iterate1, weights2, scaled2, iterate2 = call(
        down1,
        "down1",
        [(ranks, 4 * group, 128), (6,) + tall1, tall1, tall1, (6,) + tall2, tall2, tall2],
        [(3,) + tall1, tall1, (depth1 + 2,) + plane1, (3 * depth2,) + plane1]
        + [(3,) + tall2, tall2, (depth2 + 2,) + plane2, (3 * depth2 // 2, 8, 128)]
        + [(3 * depth2,) + plane2, (6, 4 * group, 128)],
        pos,
        (whole1, xb, xa),
    )

    gathered = lax.all_to_all(message, "gx", 0, 0)
    gathered = gathered.reshape(1, ranks * 4 * group, 128)
    gathered = jnp.broadcast_to(gathered, (turns,) + gathered.shape[1:])
    gathered = lax.all_to_all(gathered, "gy", 0, 0)

    rows3 = 4 * ranks
    plane3 = (rows3, 128)
    solved, left_over = call(
        up,
        "up",
        [right_side.shape, right_side.shape],
        [(3, rows3 * group, 128), (6, group) + plane3, (group,) + plane3, (group,) + plane3, (2, group) + plane3]
        + [(group,) + plane2, (2 * group + 4,) + plane2, (10,) + plane2, (8,) + plane2, (8,) + plane2, (6,) + plane2]
        + [(6,) + plane1, (12,) + plane1, (10,) + plane1, (10,) + plane1, (8,) + plane1]
        + [(8,) + plane1, (depth - 4,) + plane0, (depth - 6,) + plane0, (depth - 6,) + plane0, (depth - 2,) + plane0],
        pos,
        (gathered, weights2, scaled2, iterate2, weights1, scaled1, iterate1)
        + (weights0, diagonal0, scaled0, iterate0),
    )
    return solved, left_over


def solution(mesh):
    spec = P("gz", "gx", "gy")
    return jax.shard_map(
        on_device, mesh=mesh, in_specs=(spec, spec, spec), out_specs=(spec, spec), check_vma=False
    )
```

```python
import functools

import jax
import jax.numpy as jnp
from jax import lax
from jax.experimental import pallas as pl
from jax.experimental.pallas import tpu as pltpu
from jax.sharding import PartitionSpec as P

LEVELS = 4
SWEEPS = 2
BOTTOM = 16

smooth_low = 0.3
bottom_low = 0.05
upper_bound = 2.0
face_scale = 1.0 / 6.0

F32 = jnp.float32
AXES = ("gx", "gy", "gz")
REACH = (4, 4, 5)
DEEP = 5


def chebyshev(steps, lower):
    centre = (upper_bound + lower) / 2.0
    half_width = (upper_bound - lower) / 2.0
    sigma = centre / half_width
    rho = 1.0 / sigma
    out = [(0.0, 1.0 / centre)]
    for _ in range(1, steps):
        rho_next = 1.0 / (2.0 * sigma - rho)
        out.append((rho_next * rho, 2.0 * rho_next / half_width))
        rho = rho_next
    return out


(_, FIRST), (CARRY, GAIN) = chebyshev(SWEEPS, smooth_low)


def roll(value, shift, axis):
    shift %= value.shape[axis]
    return pltpu.roll(value, shift, axis) if shift else value


def lane_of(shape):
    return lax.broadcasted_iota(jnp.int32, shape, 1)


def row_of(shape):
    return lax.broadcasted_iota(jnp.int32, shape, 0)


def sides(value):
    return [roll(value, 1, 0), roll(value, -1, 0), roll(value, 1, 1), roll(value, -1, 1)]


def scale_of(level):
    return face_scale * 0.25**level * 0.5


def coefficients(beta, below, above, acoef, level):
    weights = [scale_of(level) * (beta + other) for other in [below, above] + sides(beta)]
    diagonal = acoef
    for weight in weights:
        diagonal = diagonal + weight
    inside = beta > 0.0
    inverse = jnp.where(inside, 1.0 / jnp.where(inside, diagonal, 1.0), 0.0)
    return [weight * inverse for weight in weights], diagonal, inverse


def defect(scaled, weights, value, below, above):
    result = scaled - value
    for weight, other in zip(weights, [below, above] + sides(value)):
        result = result + weight * other
    return result


def dot(left, right):
    right = right.astype(jnp.bfloat16)
    high = left.astype(jnp.bfloat16)
    rest = left - high.astype(F32)
    middle = rest.astype(jnp.bfloat16)
    low = (rest - middle.astype(F32)).astype(jnp.bfloat16)
    total = jnp.dot(low, right, preferred_element_type=F32)
    total = total + jnp.dot(middle, right, preferred_element_type=F32)
    return total + jnp.dot(high, right, preferred_element_type=F32)


def matrix(shape, rule, value=1.0):
    return jnp.where(rule(row_of(shape), lane_of(shape)), value, 0.0).astype(F32)


def copies(ref, value):
    for index in range(ref.shape[0]):
        ref[index] = value


def away(plane, depth):
    return max(DEEP - plane, plane - (depth - 1 - DEEP), 0)


def slots(depth):
    wide, narrow = [], []
    for index, reach in enumerate(REACH):
        for plane in range(depth):
            if away(plane, depth) < reach:
                (wide if away(plane, depth) <= reach - 2 else narrow).append((index, plane))
    out = [(index, plane, at // 4, 32 * (at % 4), 32) for at, (index, plane) in enumerate(wide)]
    first = -(-len(wide) // 4)
    return out + [(index, plane, first + at // 16, 8 * (at % 16), 8) for at, (index, plane) in enumerate(narrow)]


def masked(pos, xb, xa, index):
    before = jnp.where(pos[0] > 0, xb[index], 0.0)
    return before, jnp.where(pos[0] < pos[3] - 1, xa[index], 0.0)


def packz(pos, own, xb, xa, last, first):
    planes, at = own.shape[1], 0
    four = lax.broadcasted_iota(jnp.int32, xb.shape[1:], 1) < 4
    for index, reach in enumerate(REACH):
        before, after = masked(pos, xb, xa, index)
        ends = jnp.where(four, after, before)
        last[at : at + reach, 0:32, :] = own[index, planes - reach :]
        last[at : at + reach, 32:40, :] = ends[planes - reach :]
        first[at : at + reach, 0:32, :] = own[index, :reach]
        first[at : at + reach, 32:40, :] = ends[:reach]
        at += reach


def pack0(pos, own, xb, xa, zb, za, whole, left, right):
    planes = own.shape[1]
    depth = planes + 2 * DEEP
    at = 0
    for index, reach in enumerate(REACH):
        for plane in range(DEEP - reach):
            for end in (plane, depth - 1 - plane):
                whole[index, end] = jnp.zeros((48, 128), F32)
        for ref, start in ((zb, DEEP - reach), (za, DEEP + planes)):
            whole[index, start : start + reach, 0:40, :] = ref[at : at + reach]
            whole[index, start : start + reach, 40:48, :] = ref[at : at + reach, 32:40, :]
        before, after = masked(pos, xb, xa, index)
        whole[index, DEEP : DEEP + planes, 0:32, :] = own[index]
        whole[index, DEEP : DEEP + planes, 32:40, :] = after
        whole[index, DEEP : DEEP + planes, 40:48, :] = before
        at += reach
    lane = lane_of((40, 128))
    four = row_of((8, 128)) < 4
    low, high = {}, {}
    for index, plane, tile, to, lanes in slots(depth):
        ends = jnp.where(four, whole[index, plane, 32:40, :], whole[index, plane, 40:48, :])
        value = jnp.concatenate([whole[index, plane, 0:32, :], ends], axis=0)
        here = (lane >= to) & (lane < to + lanes)
        zero = jnp.zeros((40, 128), F32)
        low[tile] = jnp.where(here, roll(value, to, 1), low.get(tile, zero))
        high[tile] = jnp.where(here, roll(value, to + lanes, 1), high.get(tile, zero))
    for tile in low:
        left[tile] = low[tile]
        right[tile] = high[tile]


def unpack0(whole, before, after, ext, wanted):
    lane = lane_of((40, 128))
    there = {(index, plane): rest for index, plane, *rest in slots(whole.shape[1])}
    for index, plane in wanted:
        ext[index, plane, :, 0:128] = whole[index, plane]
        if (index, plane) not in there:
            ext[index, plane, :, 128:256] = jnp.zeros((48, 128), F32)
            continue
        tile, to, lanes = there[index, plane]
        ahead = jnp.where(lane < lanes, roll(after[tile], -to, 1), 0.0)
        value = jnp.where(lane >= 128 - lanes, roll(before[tile], -lanes - to, 1), ahead)
        ext[index, plane, 0:40, 128:256] = value
        ext[index, plane, 40:48, 128:256] = value[32:40]


def planes_of(count, level, start=0):
    most = (12, 32, 16)[level]
    return pl.loop(start, start + count, unroll=max(n for n in range(1, most + 1) if count % n == 0))


def coefficients0(ext, plane):
    got, middle, inverse = coefficients(ext[2, plane], ext[2, plane - 1], ext[2, plane + 1], ext[1, plane], 0)
    return got, middle, ext[0, plane] * inverse


def first_sweeps(weights, scaled, below, middle, above):
    value = FIRST * middle
    return value + (CARRY * value + GAIN * defect(scaled, weights, value, FIRST * below, FIRST * above))


def residual0(weights, diagonal, scaled, value, below, above, at, lanes):
    cut = lambda array: array[0:32, 0:lanes]
    result = scaled[at, 0:32, 0:lanes] - cut(value)
    for index, other in enumerate([below, above] + sides(value)):
        result = result + weights[index, at, 0:32, 0:lanes] * cut(other)
    return diagonal[at, 0:32, 0:lanes] * result


def down0(whole, before, after, iterate, message, weights, diagonal, scaled, ext, sums):
    depth = whole.shape[1]
    wanted = [(index, plane) for index in range(2) for plane in range(3, depth - 3)]
    unpack0(whole, before, after, ext, wanted + [(2, plane) for plane in range(2, depth - 2)])

    @planes_of(diagonal.shape[0], 0)
    def _(plane):
        got, diagonal[plane], scaled[plane] = coefficients0(ext, plane + 3)
        for index in range(6):
            weights[index, plane] = got[index]

    @planes_of(iterate.shape[0], 0)
    def _(plane):
        faces = [weights[index, plane + 1] for index in range(6)]
        iterate[plane] = first_sweeps(faces, scaled[plane + 1], scaled[plane], scaled[plane + 1], scaled[plane + 2])

    planes = whole.shape[1] - 2 * DEEP

    def left_over(plane):
        return residual0(
            weights, diagonal, scaled, iterate[plane + 1], iterate[plane], iterate[plane + 2], plane + 2, 256
        )

    half = planes // 2

    @planes_of(half, 0)
    def _(plane):
        pairs = [left_over(2 * plane) + left_over(2 * plane + 1)]
        for index in (1, 2):
            low = ext[index, DEEP + 2 * plane, 0:32, :]
            pairs.append(low + ext[index, DEEP + 2 * plane + 1, 0:32, :])
        for index, value in enumerate(pairs):
            sums[0, index * half + plane] = value[:, 0:128]
            sums[1, index * half + plane] = value[:, 128:256]

    def rows_of(side, places):
        tall = [
            sums[side, place, pl.ds(0, 16, stride=2), :] + sums[side, place, pl.ds(1, 16, stride=2), :]
            for place in places
        ]
        return jnp.concatenate(tall, axis=0)

    even = matrix((128, 128), lambda row, lane: lane == row // 2, 0.125)
    odd = matrix((128, 128), lambda row, lane: lane == row // 2 + 64, 0.125)
    middle = dot(rows_of(0, range(0, 3 * half, 2)), even) + dot(rows_of(0, range(1, 3 * half, 2)), odd)
    ends = None
    for plane in range(half):

        def rule(row, lane, to=32 * plane):
            ahead = (row < 32) & (lane == to + row // 2)
            return ahead | ((row >= 96) & (lane == to + 16 + (row - 96) // 2))

        got = dot(rows_of(1, range(plane, 3 * half, half)), matrix((128, 128), rule, 0.125))
        ends = got if ends is None else ends + got
    copies(message, jnp.concatenate([middle, ends], axis=0))


def rest0(whole, before, after, weights, scaled, later, outer, ext):
    depth = whole.shape[1]
    ends = ((1, 2), (depth - 2, depth - 3))
    wanted = [(index, plane) for index in range(2) for end in ends for plane in end]
    unpack0(whole, before, after, ext, wanted + [(2, p) for p in (0, 1, 2, 3, depth - 4, depth - 3, depth - 2, depth - 1)])
    count = scaled.shape[0]
    for side, (far, near) in enumerate(ends):
        at, beside = (0, 1) if side == 0 else (count - 1, count - 2)
        farthest = coefficients0(ext, far)[2]
        faces, _, middle = coefficients0(ext, near)
        around = (farthest, scaled[at]) if side == 0 else (scaled[at], farthest)
        outer[3 * side] = first_sweeps(faces, middle, around[0], middle, around[1])
        faces = [weights[index, at] for index in range(6)]
        around = (middle, scaled[beside]) if side == 0 else (scaled[beside], middle)
        outer[1 + side] = first_sweeps(faces, scaled[at], around[0], scaled[at], around[1])


def unpack1(ref, there, put):
    lane = lane_of((16, 128))
    per = ref.shape[1] // 36

    @pl.loop(0, ref.shape[0], unroll=ref.shape[0])
    def _(source):
        for index in range(3):
            ends = ref[source, 96 + 16 * index : 112 + 16 * index, :]
            for plane in range(per):
                at = (2 * index + plane // 2) * 16
                value = roll(ref[source, at : at + 16, :], 64 * (plane % 2), 1)
                value = jnp.where(lane < 80, jnp.where(lane < 64, value, roll(ends, 64 - 32 * plane, 1)), 0.0)
                value = jnp.where(lane >= 112, roll(ends, 96 - 32 * plane, 1), value)
                if there is not None:
                    value = jnp.where(there, value, 0.0)
                put(index, source * per + plane, value)


def pass_all(weights, scaled, value, out, count, combine, level):
    @planes_of(count, level)
    def _(plane):
        middle = value[plane + 1]
        got = defect(
            scaled[plane + 4],
            [weights[index, plane + 4] for index in range(6)],
            middle,
            value[plane],
            value[plane + 2],
        )
        out(plane, combine(middle, got))


def prepare(ext, weights, diagonal, scaled, level):
    shape = scaled.shape[1:]
    count = scaled.shape[0] - 8
    for end in (0, count + 4):
        for plane in range(4):
            scaled[end + plane] = jnp.zeros(shape, F32)
            for index in range(6):
                weights[index, end + plane] = jnp.zeros(shape, F32)

    @planes_of(count, level, 4)
    def _(at):
        got, middle, inverse = coefficients(ext[2, at], ext[2, at - 1], ext[2, at + 1], ext[1, at], level)
        for index in range(6):
            weights[index, at] = got[index]
        diagonal[at] = middle
        scaled[at] = ext[0, at] * inverse


def down1(
    pos, own, xb, xa, message, weights1, scaled1, iterate1, weights2, scaled2, iterate2,
    ext1, diagonal1, start1, sums1, ext2, diagonal2, start2, sums2, thin, thick,
):
    depth = scaled1.shape[0] - 8
    for index in range(3):
        for end in (0, depth + 4):
            for plane in range(4):
                ext1[index, end + plane] = jnp.zeros((48, 128), F32)

    for start, ref, there in ((0, own, None), (16, xa, pos[0] < pos[3] - 1), (32, xb, pos[0] > 0)):

        def put(index, plane, value, start=start):
            ext1[index, plane + 4, start : start + 16, :] = value

        unpack1(ref, there, put)
    prepare(ext1, weights1, diagonal1, scaled1, 1)
    start1[0] = jnp.zeros((48, 128), F32)
    start1[depth + 1] = jnp.zeros((48, 128), F32)

    @planes_of(depth, 1)
    def _(plane):
        start1[plane + 1] = FIRST * scaled1[plane + 4]

    for end in (0, depth + 4):
        for plane in range(4):
            iterate1[end + plane] = jnp.zeros((48, 128), F32)

    def put1(plane, value):
        iterate1[plane + 4] = value

    pass_all(weights1, scaled1, start1, put1, depth, lambda value, got: value + (CARRY * value + GAIN * got), 1)

    half = depth // 2

    @planes_of(half, 1)
    def _(pair):
        total = None
        for plane in (2 * pair, 2 * pair + 1):
            got = diagonal1[plane + 4] * defect(
                scaled1[plane + 4],
                [weights1[index, plane + 4] for index in range(6)],
                iterate1[plane + 4],
                iterate1[plane + 3],
                iterate1[plane + 5],
            )
            total = got if total is None else total + got
        sums1[pair] = total
        for index in (1, 2):
            sums1[index * half + pair] = ext1[index, 2 * pair + 4] + ext1[index, 2 * pair + 5]

    @planes_of(3 * half, 1)
    def _(plane):
        thin[plane] = sums1[plane, pl.ds(0, 24, stride=2), :] + sums1[plane, pl.ds(1, 24, stride=2), :]

    def to_level2(row, lane):
        place = jnp.where(lane < 64, lane, lane - 128)
        source = lax.shift_right_arithmetic(jnp.where(row < 96, row, row - 128), 1)
        return (source == place) & ((row < 80) | (row >= 112))

    level2 = matrix((128, 128), to_level2, 0.125)
    for index in range(3):
        values = thin[index * half : (index + 1) * half].reshape(half * 24, 128)
        ext2[index, 4 : 4 + half] = dot(values, level2).reshape(half, 24, 128)
        for end in (0, half + 4):
            for plane in range(4):
                ext2[index, end + plane] = jnp.zeros((24, 128), F32)

    prepare(ext2, weights2, diagonal2, scaled2, 2)
    start2[0] = jnp.zeros((24, 128), F32)
    start2[half + 1] = jnp.zeros((24, 128), F32)

    @pl.loop(0, half)
    def _(plane):
        start2[plane + 1] = FIRST * scaled2[plane + 4]

    for end in (0, half + 4):
        for plane in range(4):
            iterate2[end + plane] = jnp.zeros((24, 128), F32)

    def put2(plane, value):
        iterate2[plane + 4] = value

    pass_all(weights2, scaled2, start2, put2, half, lambda value, got: value + (CARRY * value + GAIN * got), 2)

    quarter = half // 2
    group = quarter // 2
    place2 = []
    for at in range(6):
        to = 64 * (at % 2) + 16 * lax.rem(pos[1] + at // 2, 4)
        place2.append(matrix((128, 128), lambda row, lane, to=to: (row < 32) & (lane == row // 2 + to), 0.125))
    for index in range(3):
        for plane in range(quarter):
            if index == 0:
                total = None
                for at in (2 * plane, 2 * plane + 1):
                    got = diagonal2[at + 4] * defect(
                        scaled2[at + 4],
                        [weights2[face, at + 4] for face in range(6)],
                        iterate2[at + 4],
                        iterate2[at + 3],
                        iterate2[at + 5],
                    )
                    total = got if total is None else total + got
                total = total[0:8]
            else:
                total = ext2[index, 2 * plane + 4, 0:8, :] + ext2[index, 2 * plane + 5, 0:8, :]
            at = index * quarter + plane
            sums2[at] = total
            side, within = divmod(plane, group)
            thick[index * 2 + side, pl.ds(within, 4, stride=group), :] = (
                sums2[at, pl.ds(0, 4, stride=2), :] + sums2[at, pl.ds(1, 4, stride=2), :]
            )
    result = dot(thick[0], place2[0])
    for at in range(1, 6):
        result = result + dot(thick[at], place2[at])
    copies(message, result)


def bottom(gathered, whole, weights, scaled, update, values):
    group = weights.shape[1]
    rows = weights.shape[2]
    place = lax.rem(lane_of(gathered.shape[1:]) // 16, 4)
    for index in range(3):
        total = gathered[0]
        for source in range(1, 4):
            total = jnp.where(place == (source + index) % 4, gathered[source], total)
        if index:
            total = jnp.where(place + index < 4, roll(total, -16 * index, 1), roll(total, 64 - 16 * index, 1))
        whole[index] = total
    shape = (rows, 128)
    row, lane = row_of(shape), lane_of(shape)
    column = lax.rem(lane, 64)

    def plane_at(index, plane):
        return whole[index, pl.ds(plane, rows, stride=group), :]

    def around(get, plane):
        middle = get(plane)
        below = get(plane - 1) if plane else roll(get(group - 1), 64, 1)
        above = get(plane + 1) if plane < group - 1 else roll(get(0), 64, 1)
        return [below, above] + sides(middle)

    for plane in range(group):
        beta = plane_at(2, plane)
        masks = [
            (lane >= 64) if plane == 0 else None,
            (lane < 64) if plane == group - 1 else None,
            row > 0,
            row < rows - 1,
            column > 0,
            column < 63,
        ]
        near = around(lambda at: plane_at(2, at), plane)
        near = [other if mask is None else jnp.where(mask, other, 0.0) for other, mask in zip(near, masks)]
        faces = [scale_of(3) * (beta + other) for other in near]
        diagonal = plane_at(1, plane)
        for face in faces:
            diagonal = diagonal + face
        inverse = 1.0 / diagonal
        for index, (face, mask) in enumerate(zip(faces, masks)):
            face = face * inverse
            weights[index, plane] = face if mask is None else jnp.where(mask, face, 0.0)
        scaled[plane] = plane_at(0, plane) * inverse

    steps = chebyshev(BOTTOM, bottom_low)
    for plane in range(group):
        value = steps[0][1] * scaled[plane]
        update[plane] = value
        values[0, plane] = value
    for step, (carry, gain) in enumerate(steps[1:]):
        now, later = step % 2, (step + 1) % 2
        for plane in range(group):
            middle = values[now, plane]
            got = scaled[plane] - middle
            for index, other in enumerate(around(lambda at: values[now, at], plane)):
                got = got + weights[index, plane] * other
            moved = carry * update[plane] + gain * got
            update[plane] = moved
            values[later, plane] = middle + moved


def finish(at, iterate, weights, scaled, level, update, middle, put):
    count = iterate.shape[0]

    @planes_of(count - 2, level)
    def _(plane):
        value = iterate[plane + 1]
        got = FIRST * defect(
            scaled[at + plane + 1],
            [weights[index, at + plane + 1] for index in range(6)],
            value,
            iterate[plane],
            iterate[plane + 2],
        )
        update[plane] = got
        middle[plane] = value + got

    @planes_of(count - 4, level)
    def _(plane):
        value = middle[plane + 1]
        got = defect(
            scaled[at + plane + 2],
            [weights[index, at + plane + 2] for index in range(6)],
            value,
            middle[plane],
            middle[plane + 2],
        )
        put(plane, value + (CARRY * update[plane + 1] + GAIN * got))


def up(
    pos, gathered, weights2, scaled2, iterate2, weights1, scaled1, iterate1,
    weights0, diagonal0, scaled0, iterate0, outer0, solved, left_over,
    whole3, weights3, scaled3, update3, values3,
    thin3, error2, value2, update2, middle2, out2,
    tall1, value1, update1, middle1, out1,
    tall0, value0, update0, middle0, out0,
):
    bottom(gathered, whole3, weights3, scaled3, update3, values3)
    group, rows = weights3.shape[1], weights3.shape[2]
    at_x, at_y, at_z = 4 * pos[0], 16 * pos[1], pos[2]
    last = (BOTTOM - 1) % 2

    lane = lane_of((8, 128))
    near = lax.rem(lane, 64)
    fits = ((near < 16) | ((near < 20) & (pos[1] < 3)) | ((near >= 60) & (pos[1] > 0))).astype(F32)
    first_row, last_row = (pos[0] > 0).astype(F32), (pos[0] < pos[3] - 1).astype(F32)
    low = row_of((8, 128)) < 4
    own = jnp.where(low, fits, fits * last_row)
    left = jnp.where(low, 0.0, fits * first_row)
    for plane in range(group):
        moved = pltpu.roll(values3[last, plane], lax.rem(rows - at_x, rows), 0)
        both = jnp.concatenate([moved[0:8], moved[rows - 8 :]], axis=0)
        both = pltpu.roll(both, lax.rem(128 - at_y, 128), 1)
        ahead, behind = both[0:8] * own, both[8:16] * left
        for start in (0, 1):
            thin3[plane, pl.ds(start, 8, stride=2), :] = ahead
            thin3[plane, pl.ds(16 + start, 4, stride=2), :] = behind[4:8]

    def to_level2(row, lane):
        side, within = lane // 128, lax.rem(lane, 128)
        place = jnp.where(within < 64, within, within - 128)
        source = jnp.where(side == 0, lax.rem(row, 128), lax.rem(row + 64, 128))
        source = jnp.where(source < 64, source, source - 128)
        return (source == lax.shift_right_arithmetic(place, 1)) & ((within < 40) | (within >= 120))

    spread = dot(thin3[...].reshape(group * 24, 128), matrix((128, 256), to_level2)).reshape(group, 24, 256)
    for plane in range(group):
        for side in range(2):
            error2[side * group + plane + 2] = spread[plane, :, 128 * side : 128 * side + 128]
    for end in (0, 2 * group + 2):
        for plane in range(2):
            error2[end + plane] = jnp.zeros((24, 128), F32)

    for plane in range(10):
        value2[plane] = iterate2[2 * at_z + plane] + error2[at_z + plane // 2]

    def put2(plane, value):
        out2[plane] = value

    finish(2 * at_z, value2, weights2, scaled2, 2, update2, middle2, put2)

    def to_level1(row, lane):
        place = jnp.where(lane < 96, lane, lane - 128)
        source = lax.shift_right_arithmetic(place, 1)
        return (jnp.where(row < 64, row, row - 128) == source) & ((lane < 80) | (lane >= 112))

    wide1 = matrix((128, 128), to_level1)
    for plane in range(6):
        tall1[plane, pl.ds(0, 24, stride=2), :] = out2[plane]
        tall1[plane, pl.ds(1, 24, stride=2), :] = out2[plane]
    spread = dot(tall1[...].reshape(6 * 48, 128), wide1).reshape(6, 48, 128)
    for plane in range(12):
        value1[plane] = iterate1[4 * at_z + plane] + spread[plane // 2]

    def put1(plane, value):
        out1[plane] = value

    finish(4 * at_z, value1, weights1, scaled1, 1, update1, middle1, put1)

    def to_level0(row, lane):
        place = jnp.where(lane < 192, lane, lane - 256)
        source = lax.shift_right_arithmetic(place, 1)
        return (jnp.where(row < 96, row, row - 128) == source) & ((lane < 136) | (lane >= 248))

    wide0 = matrix((128, 256), to_level0)
    for plane in range(8):
        value = out1[plane]
        tall0[plane, pl.ds(0, 24, stride=2), :] = value[0:24]
        tall0[plane, pl.ds(1, 24, stride=2), :] = value[0:24]
        tall0[plane, pl.ds(40, 4, stride=2), :] = value[44:48]
        tall0[plane, pl.ds(41, 4, stride=2), :] = value[44:48]

    @planes_of(8, 1)
    def _(plane):
        value = dot(tall0[plane], wide0)
        out0[2 * plane] = value
        out0[2 * plane + 1] = value

    @planes_of(iterate0.shape[0], 0)
    def _(plane):
        value0[plane + 2] = iterate0[plane] + out0[plane + 3]

    count = value0.shape[0]
    for at, plane in enumerate((0, 1, count - 2, count - 1)):
        value0[plane] = outer0[at] + out0[plane + 1]


    @planes_of(count - 2, 0)
    def _(plane):
        value = value0[plane + 1]
        got = FIRST * defect(
            scaled0[plane],
            [weights0[index, plane] for index in range(6)],
            value,
            value0[plane],
            value0[plane + 2],
        )
        update0[plane] = got
        middle0[plane] = value + got

    @planes_of(count - 4, 0)
    def _(plane):
        value = middle0[plane + 1]
        got = defect(
            scaled0[plane + 1],
            [weights0[index, plane + 1] for index in range(6)],
            value,
            middle0[plane],
            middle0[plane + 2],
        )
        out0[plane] = value + (CARRY * update0[plane + 1] + GAIN * got)

    @planes_of(count - 6, 0)
    def _(plane):
        value = out0[plane + 1]
        solved[plane] = value[0:32, 0:128]
        left_over[plane] = residual0(
            weights0, diagonal0, scaled0, value, out0[plane], out0[plane + 2], plane + 2, 128
        )


def call(body, name, outs, scratch, pos, args, flops=0):
    vmem = pl.BlockSpec(memory_space=pltpu.VMEM)
    smem = [pl.BlockSpec(memory_space=pltpu.SMEM)] if pos is not None else []
    operands = ([pos] if pos is not None else []) + list(args)
    return pl.pallas_call(
        body,
        name=name,
        out_shape=[jax.ShapeDtypeStruct(shape, F32) for shape in outs],
        in_specs=smem + [vmem] * len(args),
        out_specs=[vmem] * len(outs),
        scratch_shapes=[pltpu.VMEM(shape, F32) for shape in scratch],
        cost_estimate=pl.CostEstimate(flops=flops, bytes_accessed=0, transcendentals=0) if flops else None,
        compiler_params=pltpu.CompilerParams(vmem_limit_bytes=32 * 2**20),
    )(*operands)


def exchange(up_values, down_values, axis, ring):
    peers = lax.axis_size(axis)
    up_pairs = [(i, (i + 1) % peers) for i in range(peers if ring else peers - 1)]
    down_pairs = [(j, i) for i, j in up_pairs]
    return lax.ppermute(up_values, axis, up_pairs), lax.ppermute(down_values, axis, down_pairs)


def on_device(right_side, acoef, beta):
    ranks, turns, files = [lax.axis_size(axis) for axis in AXES]
    pos = jnp.stack([lax.axis_index(axis) for axis in AXES] + [jnp.int32(ranks)]).astype(jnp.int32)
    planes = right_side.shape[0]
    arrays = (right_side, acoef, beta)

    last = jnp.stack([value[:, 24:] for value in arrays])
    first = jnp.stack([value[:, :8] for value in arrays])
    xb, xa = exchange(last, first, "gx", True)
    own = jnp.stack(arrays)
    last, first = call(packz, "packz", [(sum(REACH), 40, 128)] * 2, [], pos, (own, xb, xa))
    zb, za = exchange(last, first, "gz", False)
    depth = planes + 2 * DEEP
    tiles = max(tile for _, _, tile, _, _ in slots(depth)) + 1
    whole0, left, right = call(
        pack0, "pack0", [(3, depth, 48, 128)] + [(tiles, 40, 128)] * 2, [], pos, (own, xb, xa, zb, za)
    )
    before0, after0 = exchange(right, left, "gy", False)
    plane0 = (48, 256)
    half = planes // 2
    iterate0, message, weights0, diagonal0, scaled0 = call(
        down0,
        "down0",
        [(depth - 8,) + plane0, (files, 36 * half, 128), (6, depth - 6) + plane0] + [(depth - 6,) + plane0] * 2,
        [(3, depth) + plane0, (2, 3 * half, 32, 128)],
        None,
        (whole0, before0, after0),
    )

    whole1 = lax.all_to_all(message, "gz", 0, 0)
    xb, xa = exchange(whole1, whole1, "gx", True)
    depth1 = files * half
    outer0 = call(
        rest0,
        "rest0",
        [(4,) + plane0],
        [(3, depth) + plane0],
        None,
        (whole0, before0, after0, weights0, scaled0, whole1),
        10**9,
    )[0]
    plane1, plane2 = (48, 128), (24, 128)
    depth2 = depth1 // 2
    group = depth2 // 4
    tall1, tall2 = (depth1 + 8,) + plane1, (depth2 + 8,) + plane2
    message, weights1, scaled1, iterate1, weights2, scaled2, iterate2 = call(
        down1,
        "down1",
        [(ranks, 4 * group, 128), (6,) + tall1, tall1, tall1, (6,) + tall2, tall2, tall2],
        [(3,) + tall1, tall1, (depth1 + 2,) + plane1, (3 * depth2,) + plane1]
        + [(3,) + tall2, tall2, (depth2 + 2,) + plane2, (3 * depth2 // 2, 8, 128)]
        + [(3 * depth2,) + plane2, (6, 4 * group, 128)],
        pos,
        (whole1, xb, xa),
    )

    gathered = lax.all_to_all(message, "gx", 0, 0)
    gathered = gathered.reshape(1, ranks * 4 * group, 128)
    gathered = jnp.broadcast_to(gathered, (turns,) + gathered.shape[1:])
    gathered = lax.all_to_all(gathered, "gy", 0, 0)

    rows3 = 4 * ranks
    plane3 = (rows3, 128)
    solved, left_over = call(
        up,
        "up",
        [right_side.shape, right_side.shape],
        [(3, rows3 * group, 128), (6, group) + plane3, (group,) + plane3, (group,) + plane3, (2, group) + plane3]
        + [(group,) + plane2, (2 * group + 4,) + plane2, (10,) + plane2, (8,) + plane2, (8,) + plane2, (6,) + plane2]
        + [(6,) + plane1, (12,) + plane1, (10,) + plane1, (10,) + plane1, (8,) + plane1]
        + [(8,) + plane1, (depth - 4,) + plane0, (depth - 6,) + plane0, (depth - 6,) + plane0, (depth - 2,) + plane0],
        pos,
        (gathered, weights2, scaled2, iterate2, weights1, scaled1, iterate1)
        + (weights0, diagonal0, scaled0, iterate0, outer0),
    )
    return solved, left_over


def solution(mesh):
    spec = P("gz", "gx", "gy")
    return jax.shard_map(
        on_device, mesh=mesh, in_specs=(spec, spec, spec), out_specs=(spec, spec), check_vma=False
    )
```

```python
import functools

import jax
import jax.numpy as jnp
from jax import lax
from jax.experimental import pallas as pl
from jax.experimental.pallas import tpu as pltpu
from jax.sharding import PartitionSpec as P

LEVELS = 4
SWEEPS = 2
BOTTOM = 16

smooth_low = 0.3
bottom_low = 0.05
upper_bound = 2.0
face_scale = 1.0 / 6.0

F32 = jnp.float32
AXES = ("gx", "gy", "gz")
REACH = (4, 4, 5)
DEEP = 5


def chebyshev(steps, lower):
    centre = (upper_bound + lower) / 2.0
    half_width = (upper_bound - lower) / 2.0
    sigma = centre / half_width
    rho = 1.0 / sigma
    out = [(0.0, 1.0 / centre)]
    for _ in range(1, steps):
        rho_next = 1.0 / (2.0 * sigma - rho)
        out.append((rho_next * rho, 2.0 * rho_next / half_width))
        rho = rho_next
    return out


(_, FIRST), (CARRY, GAIN) = chebyshev(SWEEPS, smooth_low)


def roll(value, shift, axis):
    shift %= value.shape[axis]
    return pltpu.roll(value, shift, axis) if shift else value


def lane_of(shape):
    return lax.broadcasted_iota(jnp.int32, shape, 1)


def row_of(shape):
    return lax.broadcasted_iota(jnp.int32, shape, 0)


def sides(value):
    return [roll(value, 1, 0), roll(value, -1, 0), roll(value, 1, 1), roll(value, -1, 1)]


def scale_of(level):
    return face_scale * 0.25**level * 0.5


def coefficients(beta, below, above, acoef, level):
    weights = [scale_of(level) * (beta + other) for other in [below, above] + sides(beta)]
    diagonal = acoef
    for weight in weights:
        diagonal = diagonal + weight
    inside = beta > 0.0
    inverse = jnp.where(inside, 1.0 / jnp.where(inside, diagonal, 1.0), 0.0)
    return [weight * inverse for weight in weights], diagonal, inverse


def defect(scaled, weights, value, below, above):
    result = scaled - value
    for weight, other in zip(weights, [below, above] + sides(value)):
        result = result + weight * other
    return result


def dot(left, right):
    right = right.astype(jnp.bfloat16)
    high = left.astype(jnp.bfloat16)
    rest = left - high.astype(F32)
    middle = rest.astype(jnp.bfloat16)
    low = (rest - middle.astype(F32)).astype(jnp.bfloat16)
    total = jnp.dot(low, right, preferred_element_type=F32)
    total = total + jnp.dot(middle, right, preferred_element_type=F32)
    return total + jnp.dot(high, right, preferred_element_type=F32)


def matrix(shape, rule, value=1.0):
    return jnp.where(rule(row_of(shape), lane_of(shape)), value, 0.0).astype(F32)


def copies(ref, value):
    for index in range(ref.shape[0]):
        ref[index] = value


def away(plane, depth):
    return max(DEEP - plane, plane - (depth - 1 - DEEP), 0)


def slots(depth):
    wide, narrow = [], []
    for index, reach in enumerate(REACH):
        for plane in range(depth):
            if away(plane, depth) < reach:
                (wide if away(plane, depth) <= reach - 2 else narrow).append((index, plane))
    out = [(index, plane, at // 4, 32 * (at % 4), 32) for at, (index, plane) in enumerate(wide)]
    first = -(-len(wide) // 4)
    return out + [(index, plane, first + at // 16, 8 * (at % 16), 8) for at, (index, plane) in enumerate(narrow)]


def masked(pos, xb, xa, index):
    before = jnp.where(pos[0] > 0, xb[index], 0.0)
    return before, jnp.where(pos[0] < pos[3] - 1, xa[index], 0.0)


def packz(pos, own, xb, xa, last, first):
    planes, at = own.shape[1], 0
    four = lax.broadcasted_iota(jnp.int32, xb.shape[1:], 1) < 4
    for index, reach in enumerate(REACH):
        before, after = masked(pos, xb, xa, index)
        ends = jnp.where(four, after, before)
        last[at : at + reach, 0:32, :] = own[index, planes - reach :]
        last[at : at + reach, 32:40, :] = ends[planes - reach :]
        first[at : at + reach, 0:32, :] = own[index, :reach]
        first[at : at + reach, 32:40, :] = ends[:reach]
        at += reach


def pack0(pos, own, xb, xa, zb, za, whole, left, right):
    planes = own.shape[1]
    depth = planes + 2 * DEEP
    at = 0
    for index, reach in enumerate(REACH):
        for plane in range(DEEP - reach):
            for end in (plane, depth - 1 - plane):
                whole[index, end] = jnp.zeros((48, 128), F32)
        for ref, start in ((zb, DEEP - reach), (za, DEEP + planes)):
            whole[index, start : start + reach, 0:40, :] = ref[at : at + reach]
            whole[index, start : start + reach, 40:48, :] = ref[at : at + reach, 32:40, :]
        before, after = masked(pos, xb, xa, index)
        whole[index, DEEP : DEEP + planes, 0:32, :] = own[index]
        whole[index, DEEP : DEEP + planes, 32:40, :] = after
        whole[index, DEEP : DEEP + planes, 40:48, :] = before
        at += reach
    lane = lane_of((40, 128))
    four = row_of((8, 128)) < 4
    low, high = {}, {}
    for index, plane, tile, to, lanes in slots(depth):
        ends = jnp.where(four, whole[index, plane, 32:40, :], whole[index, plane, 40:48, :])
        value = jnp.concatenate([whole[index, plane, 0:32, :], ends], axis=0)
        here = (lane >= to) & (lane < to + lanes)
        zero = jnp.zeros((40, 128), F32)
        low[tile] = jnp.where(here, roll(value, to, 1), low.get(tile, zero))
        high[tile] = jnp.where(here, roll(value, to + lanes, 1), high.get(tile, zero))
    for tile in low:
        left[tile] = low[tile]
        right[tile] = high[tile]


def unpack0(whole, before, after, ext, wanted):
    lane = lane_of((40, 128))
    there = {(index, plane): rest for index, plane, *rest in slots(whole.shape[1])}
    for index, plane in wanted:
        ext[index, plane, :, 0:128] = whole[index, plane]
        if (index, plane) not in there:
            ext[index, plane, :, 128:256] = jnp.zeros((48, 128), F32)
            continue
        tile, to, lanes = there[index, plane]
        ahead = jnp.where(lane < lanes, roll(after[tile], -to, 1), 0.0)
        value = jnp.where(lane >= 128 - lanes, roll(before[tile], -lanes - to, 1), ahead)
        ext[index, plane, 0:40, 128:256] = value
        ext[index, plane, 40:48, 128:256] = value[32:40]


def planes_of(count, level, start=0):
    most = (12, 32, 16)[level]
    return pl.loop(start, start + count, unroll=max(n for n in range(1, most + 1) if count % n == 0))


def coefficients0(ext, plane):
    got, middle, inverse = coefficients(ext[2, plane], ext[2, plane - 1], ext[2, plane + 1], ext[1, plane], 0)
    return got, middle, ext[0, plane] * inverse


def first_sweeps(weights, scaled, below, middle, above):
    value = FIRST * middle
    return value + (CARRY * value + GAIN * defect(scaled, weights, value, FIRST * below, FIRST * above))


def residual0(weights, diagonal, scaled, value, below, above, at, lanes):
    cut = lambda array: array[0:32, 0:lanes]
    result = scaled[at, 0:32, 0:lanes] - cut(value)
    for index, other in enumerate([below, above] + sides(value)):
        result = result + weights[index, at, 0:32, 0:lanes] * cut(other)
    return diagonal[at, 0:32, 0:lanes] * result


def down0(whole, before, after, iterate, message, weights, diagonal, scaled, ext, sums):
    depth = whole.shape[1]
    wanted = [(index, plane) for index in range(2) for plane in range(3, depth - 3)]
    unpack0(whole, before, after, ext, wanted + [(2, plane) for plane in range(2, depth - 2)])

    @planes_of(diagonal.shape[0], 0)
    def _(plane):
        got, diagonal[plane], scaled[plane] = coefficients0(ext, plane + 3)
        for index in range(6):
            weights[index, plane] = got[index]

    @planes_of(iterate.shape[0], 0)
    def _(plane):
        faces = [weights[index, plane + 1] for index in range(6)]
        iterate[plane] = first_sweeps(faces, scaled[plane + 1], scaled[plane], scaled[plane + 1], scaled[plane + 2])

    planes = whole.shape[1] - 2 * DEEP

    def left_over(plane):
        return residual0(
            weights, diagonal, scaled, iterate[plane + 1], iterate[plane], iterate[plane + 2], plane + 2, 256
        )

    half = planes // 2

    @planes_of(half, 0)
    def _(plane):
        pairs = [left_over(2 * plane) + left_over(2 * plane + 1)]
        for index in (1, 2):
            low = ext[index, DEEP + 2 * plane, 0:32, :]
            pairs.append(low + ext[index, DEEP + 2 * plane + 1, 0:32, :])
        for index, value in enumerate(pairs):
            sums[0, index * half + plane] = value[:, 0:128]
            sums[1, index * half + plane] = value[:, 128:256]

    def rows_of(side, places):
        tall = [
            sums[side, place, pl.ds(0, 16, stride=2), :] + sums[side, place, pl.ds(1, 16, stride=2), :]
            for place in places
        ]
        return jnp.concatenate(tall, axis=0)

    even = matrix((128, 128), lambda row, lane: lane == row // 2, 0.125)
    odd = matrix((128, 128), lambda row, lane: lane == row // 2 + 64, 0.125)
    middle = dot(rows_of(0, range(0, 3 * half, 2)), even) + dot(rows_of(0, range(1, 3 * half, 2)), odd)
    ends = None
    for plane in range(half):

        def rule(row, lane, to=32 * plane):
            ahead = (row < 32) & (lane == to + row // 2)
            return ahead | ((row >= 96) & (lane == to + 16 + (row - 96) // 2))

        got = dot(rows_of(1, range(plane, 3 * half, half)), matrix((128, 128), rule, 0.125))
        ends = got if ends is None else ends + got
    copies(message, jnp.concatenate([middle, ends], axis=0))


def rest0(whole, before, after, weights, scaled, later, outer, ext):
    depth = whole.shape[1]
    ends = ((1, 2), (depth - 2, depth - 3))
    wanted = [(index, plane) for index in range(2) for end in ends for plane in end]
    unpack0(whole, before, after, ext, wanted + [(2, p) for p in (0, 1, 2, 3, depth - 4, depth - 3, depth - 2, depth - 1)])
    count = scaled.shape[0]
    for side, (far, near) in enumerate(ends):
        at, beside = (0, 1) if side == 0 else (count - 1, count - 2)
        farthest = coefficients0(ext, far)[2]
        faces, _, middle = coefficients0(ext, near)
        around = (farthest, scaled[at]) if side == 0 else (scaled[at], farthest)
        outer[3 * side] = first_sweeps(faces, middle, around[0], middle, around[1])
        faces = [weights[index, at] for index in range(6)]
        around = (middle, scaled[beside]) if side == 0 else (scaled[beside], middle)
        outer[1 + side] = first_sweeps(faces, scaled[at], around[0], scaled[at], around[1])


def unpack1(ref, there, put):
    lane = lane_of((16, 128))
    per = ref.shape[1] // 36

    @pl.loop(0, ref.shape[0], unroll=ref.shape[0])
    def _(source):
        for index in range(3):
            ends = ref[source, 96 + 16 * index : 112 + 16 * index, :]
            for plane in range(per):
                at = (2 * index + plane // 2) * 16
                value = roll(ref[source, at : at + 16, :], 64 * (plane % 2), 1)
                value = jnp.where(lane < 80, jnp.where(lane < 64, value, roll(ends, 64 - 32 * plane, 1)), 0.0)
                value = jnp.where(lane >= 112, roll(ends, 96 - 32 * plane, 1), value)
                if there is not None:
                    value = jnp.where(there, value, 0.0)
                put(index, source * per + plane, value)


def pass_all(weights, scaled, value, out, count, combine, level):
    @planes_of(count, level)
    def _(plane):
        middle = value[plane + 1]
        got = defect(
            scaled[plane + 4],
            [weights[index, plane + 4] for index in range(6)],
            middle,
            value[plane],
            value[plane + 2],
        )
        out(plane, combine(middle, got))


def prepare(ext, weights, diagonal, scaled, level):
    shape = scaled.shape[1:]
    count = scaled.shape[0] - 8
    for end in (0, count + 4):
        for plane in range(4):
            scaled[end + plane] = jnp.zeros(shape, F32)
            for index in range(6):
                weights[index, end + plane] = jnp.zeros(shape, F32)

    @planes_of(count, level, 4)
    def _(at):
        got, middle, inverse = coefficients(ext[2, at], ext[2, at - 1], ext[2, at + 1], ext[1, at], level)
        for index in range(6):
            weights[index, at] = got[index]
        diagonal[at] = middle
        scaled[at] = ext[0, at] * inverse


def down1(
    pos, own, xb, xa, earlier, message, weights1, scaled1, iterate1, weights2, scaled2, iterate2,
    ext1, diagonal1, start1, sums1, ext2, diagonal2, start2, sums2, thin, thick,
):
    depth = scaled1.shape[0] - 8
    for index in range(3):
        for end in (0, depth + 4):
            for plane in range(4):
                ext1[index, end + plane] = jnp.zeros((48, 128), F32)

    for start, ref, there in ((0, own, None), (16, xa, pos[0] < pos[3] - 1), (32, xb, pos[0] > 0)):

        def put(index, plane, value, start=start):
            ext1[index, plane + 4, start : start + 16, :] = value

        unpack1(ref, there, put)
    prepare(ext1, weights1, diagonal1, scaled1, 1)
    start1[0] = jnp.zeros((48, 128), F32)
    start1[depth + 1] = jnp.zeros((48, 128), F32)

    @planes_of(depth, 1)
    def _(plane):
        start1[plane + 1] = FIRST * scaled1[plane + 4]

    for end in (0, depth + 4):
        for plane in range(4):
            iterate1[end + plane] = jnp.zeros((48, 128), F32)

    def put1(plane, value):
        iterate1[plane + 4] = value

    pass_all(weights1, scaled1, start1, put1, depth, lambda value, got: value + (CARRY * value + GAIN * got), 1)

    half = depth // 2

    @planes_of(half, 1)
    def _(pair):
        total = None
        for plane in (2 * pair, 2 * pair + 1):
            got = diagonal1[plane + 4] * defect(
                scaled1[plane + 4],
                [weights1[index, plane + 4] for index in range(6)],
                iterate1[plane + 4],
                iterate1[plane + 3],
                iterate1[plane + 5],
            )
            total = got if total is None else total + got
        sums1[pair] = total
        for index in (1, 2):
            sums1[index * half + pair] = ext1[index, 2 * pair + 4] + ext1[index, 2 * pair + 5]

    @planes_of(3 * half, 1)
    def _(plane):
        thin[plane] = sums1[plane, pl.ds(0, 24, stride=2), :] + sums1[plane, pl.ds(1, 24, stride=2), :]

    def to_level2(row, lane):
        place = jnp.where(lane < 64, lane, lane - 128)
        source = lax.shift_right_arithmetic(jnp.where(row < 96, row, row - 128), 1)
        return (source == place) & ((row < 80) | (row >= 112))

    level2 = matrix((128, 128), to_level2, 0.125)
    for index in range(3):
        values = thin[index * half : (index + 1) * half].reshape(half * 24, 128)
        ext2[index, 4 : 4 + half] = dot(values, level2).reshape(half, 24, 128)
        for end in (0, half + 4):
            for plane in range(4):
                ext2[index, end + plane] = jnp.zeros((24, 128), F32)

    prepare(ext2, weights2, diagonal2, scaled2, 2)
    start2[0] = jnp.zeros((24, 128), F32)
    start2[half + 1] = jnp.zeros((24, 128), F32)

    @pl.loop(0, half)
    def _(plane):
        start2[plane + 1] = FIRST * scaled2[plane + 4]

    for end in (0, half + 4):
        for plane in range(4):
            iterate2[end + plane] = jnp.zeros((24, 128), F32)

    def put2(plane, value):
        iterate2[plane + 4] = value

    pass_all(weights2, scaled2, start2, put2, half, lambda value, got: value + (CARRY * value + GAIN * got), 2)

    quarter = half // 2
    group = quarter // 2
    place2 = []
    for at in range(6):
        to = 64 * (at % 2) + 16 * lax.rem(pos[1] + at // 2, 4)
        place2.append(matrix((128, 128), lambda row, lane, to=to: (row < 32) & (lane == row // 2 + to), 0.125))
    for index in range(3):
        for plane in range(quarter):
            if index == 0:
                total = None
                for at in (2 * plane, 2 * plane + 1):
                    got = diagonal2[at + 4] * defect(
                        scaled2[at + 4],
                        [weights2[face, at + 4] for face in range(6)],
                        iterate2[at + 4],
                        iterate2[at + 3],
                        iterate2[at + 5],
                    )
                    total = got if total is None else total + got
                total = total[0:8]
            else:
                total = ext2[index, 2 * plane + 4, 0:8, :] + ext2[index, 2 * plane + 5, 0:8, :]
            at = index * quarter + plane
            sums2[at] = total
            side, within = divmod(plane, group)
            thick[index * 2 + side, pl.ds(within, 4, stride=group), :] = (
                sums2[at, pl.ds(0, 4, stride=2), :] + sums2[at, pl.ds(1, 4, stride=2), :]
            )
    result = dot(thick[0], place2[0])
    for at in range(1, 6):
        result = result + dot(thick[at], place2[at])
    copies(message, result)


def bottom(gathered, whole, weights, scaled, update, values):
    group = weights.shape[1]
    rows = weights.shape[2]
    place = lax.rem(lane_of(gathered.shape[1:]) // 16, 4)
    for index in range(3):
        total = gathered[0]
        for source in range(1, 4):
            total = jnp.where(place == (source + index) % 4, gathered[source], total)
        if index:
            total = jnp.where(place + index < 4, roll(total, -16 * index, 1), roll(total, 64 - 16 * index, 1))
        whole[index] = total
    shape = (rows, 128)
    row, lane = row_of(shape), lane_of(shape)
    column = lax.rem(lane, 64)

    def plane_at(index, plane):
        return whole[index, pl.ds(plane, rows, stride=group), :]

    def around(get, plane):
        middle = get(plane)
        below = get(plane - 1) if plane else roll(get(group - 1), 64, 1)
        above = get(plane + 1) if plane < group - 1 else roll(get(0), 64, 1)
        return [below, above] + sides(middle)

    for plane in range(group):
        beta = plane_at(2, plane)
        masks = [
            (lane >= 64) if plane == 0 else None,
            (lane < 64) if plane == group - 1 else None,
            row > 0,
            row < rows - 1,
            column > 0,
            column < 63,
        ]
        near = around(lambda at: plane_at(2, at), plane)
        near = [other if mask is None else jnp.where(mask, other, 0.0) for other, mask in zip(near, masks)]
        faces = [scale_of(3) * (beta + other) for other in near]
        diagonal = plane_at(1, plane)
        for face in faces:
            diagonal = diagonal + face
        inverse = 1.0 / diagonal
        for index, (face, mask) in enumerate(zip(faces, masks)):
            face = face * inverse
            weights[index, plane] = face if mask is None else jnp.where(mask, face, 0.0)
        scaled[plane] = plane_at(0, plane) * inverse

    steps = chebyshev(BOTTOM, bottom_low)
    for plane in range(group):
        value = steps[0][1] * scaled[plane]
        update[plane] = value
        values[0, plane] = value
    for step, (carry, gain) in enumerate(steps[1:]):
        now, later = step % 2, (step + 1) % 2
        for plane in range(group):
            middle = values[now, plane]
            got = scaled[plane] - middle
            for index, other in enumerate(around(lambda at: values[now, at], plane)):
                got = got + weights[index, plane] * other
            moved = carry * update[plane] + gain * got
            update[plane] = moved
            values[later, plane] = middle + moved


def finish(at, iterate, weights, scaled, level, update, middle, put):
    count = iterate.shape[0]

    @planes_of(count - 2, level)
    def _(plane):
        value = iterate[plane + 1]
        got = FIRST * defect(
            scaled[at + plane + 1],
            [weights[index, at + plane + 1] for index in range(6)],
            value,
            iterate[plane],
            iterate[plane + 2],
        )
        update[plane] = got
        middle[plane] = value + got

    @planes_of(count - 4, level)
    def _(plane):
        value = middle[plane + 1]
        got = defect(
            scaled[at + plane + 2],
            [weights[index, at + plane + 2] for index in range(6)],
            value,
            middle[plane],
            middle[plane + 2],
        )
        put(plane, value + (CARRY * update[plane + 1] + GAIN * got))


def up(
    pos, gathered, weights2, scaled2, iterate2, weights1, scaled1, iterate1,
    weights0, diagonal0, scaled0, iterate0, outer0, solved, left_over,
    whole3, weights3, scaled3, update3, values3,
    thin3, error2, value2, update2, middle2, out2,
    tall1, value1, update1, middle1, out1,
    tall0, value0, update0, middle0, out0,
):
    bottom(gathered, whole3, weights3, scaled3, update3, values3)
    group, rows = weights3.shape[1], weights3.shape[2]
    at_x, at_y, at_z = 4 * pos[0], 16 * pos[1], pos[2]
    last = (BOTTOM - 1) % 2

    lane = lane_of((8, 128))
    near = lax.rem(lane, 64)
    fits = ((near < 16) | ((near < 20) & (pos[1] < 3)) | ((near >= 60) & (pos[1] > 0))).astype(F32)
    first_row, last_row = (pos[0] > 0).astype(F32), (pos[0] < pos[3] - 1).astype(F32)
    low = row_of((8, 128)) < 4
    own = jnp.where(low, fits, fits * last_row)
    left = jnp.where(low, 0.0, fits * first_row)
    for plane in range(group):
        moved = pltpu.roll(values3[last, plane], lax.rem(rows - at_x, rows), 0)
        both = jnp.concatenate([moved[0:8], moved[rows - 8 :]], axis=0)
        both = pltpu.roll(both, lax.rem(128 - at_y, 128), 1)
        ahead, behind = both[0:8] * own, both[8:16] * left
        for start in (0, 1):
            thin3[plane, pl.ds(start, 8, stride=2), :] = ahead
            thin3[plane, pl.ds(16 + start, 4, stride=2), :] = behind[4:8]

    def to_level2(row, lane):
        side, within = lane // 128, lax.rem(lane, 128)
        place = jnp.where(within < 64, within, within - 128)
        source = jnp.where(side == 0, lax.rem(row, 128), lax.rem(row + 64, 128))
        source = jnp.where(source < 64, source, source - 128)
        return (source == lax.shift_right_arithmetic(place, 1)) & ((within < 40) | (within >= 120))

    spread = dot(thin3[...].reshape(group * 24, 128), matrix((128, 256), to_level2)).reshape(group, 24, 256)
    for plane in range(group):
        for side in range(2):
            error2[side * group + plane + 2] = spread[plane, :, 128 * side : 128 * side + 128]
    for end in (0, 2 * group + 2):
        for plane in range(2):
            error2[end + plane] = jnp.zeros((24, 128), F32)

    for plane in range(10):
        value2[plane] = iterate2[2 * at_z + plane] + error2[at_z + plane // 2]

    def put2(plane, value):
        out2[plane] = value

    finish(2 * at_z, value2, weights2, scaled2, 2, update2, middle2, put2)

    def to_level1(row, lane):
        place = jnp.where(lane < 96, lane, lane - 128)
        source = lax.shift_right_arithmetic(place, 1)
        return (jnp.where(row < 64, row, row - 128) == source) & ((lane < 80) | (lane >= 112))

    wide1 = matrix((128, 128), to_level1)
    for plane in range(6):
        tall1[plane, pl.ds(0, 24, stride=2), :] = out2[plane]
        tall1[plane, pl.ds(1, 24, stride=2), :] = out2[plane]
    spread = dot(tall1[...].reshape(6 * 48, 128), wide1).reshape(6, 48, 128)
    for plane in range(12):
        value1[plane] = iterate1[4 * at_z + plane] + spread[plane // 2]

    def put1(plane, value):
        out1[plane] = value

    finish(4 * at_z, value1, weights1, scaled1, 1, update1, middle1, put1)

    def to_level0(row, lane):
        place = jnp.where(lane < 192, lane, lane - 256)
        source = lax.shift_right_arithmetic(place, 1)
        return (jnp.where(row < 96, row, row - 128) == source) & ((lane < 136) | (lane >= 248))

    wide0 = matrix((128, 256), to_level0)
    for plane in range(8):
        value = out1[plane]
        tall0[plane, pl.ds(0, 24, stride=2), :] = value[0:24]
        tall0[plane, pl.ds(1, 24, stride=2), :] = value[0:24]
        tall0[plane, pl.ds(40, 4, stride=2), :] = value[44:48]
        tall0[plane, pl.ds(41, 4, stride=2), :] = value[44:48]

    @planes_of(8, 1)
    def _(plane):
        value = dot(tall0[plane], wide0)
        out0[2 * plane] = value
        out0[2 * plane + 1] = value

    @planes_of(iterate0.shape[0], 0)
    def _(plane):
        value0[plane + 2] = iterate0[plane] + out0[plane + 3]

    count = value0.shape[0]
    for at, plane in enumerate((0, 1, count - 2, count - 1)):
        value0[plane] = outer0[at] + out0[plane + 1]


    @planes_of(count - 2, 0)
    def _(plane):
        value = value0[plane + 1]
        got = FIRST * defect(
            scaled0[plane],
            [weights0[index, plane] for index in range(6)],
            value,
            value0[plane],
            value0[plane + 2],
        )
        update0[plane] = got
        middle0[plane] = value + got

    @planes_of(count - 4, 0)
    def _(plane):
        value = middle0[plane + 1]
        got = defect(
            scaled0[plane + 1],
            [weights0[index, plane + 1] for index in range(6)],
            value,
            middle0[plane],
            middle0[plane + 2],
        )
        out0[plane] = value + (CARRY * update0[plane + 1] + GAIN * got)

    @planes_of(count - 6, 0)
    def _(plane):
        value = out0[plane + 1]
        solved[plane] = value[0:32, 0:128]
        left_over[plane] = residual0(
            weights0, diagonal0, scaled0, value, out0[plane], out0[plane + 2], plane + 2, 128
        )


def call(body, name, outs, scratch, pos, args):
    vmem = pl.BlockSpec(memory_space=pltpu.VMEM)
    smem = [pl.BlockSpec(memory_space=pltpu.SMEM)] if pos is not None else []
    operands = ([pos] if pos is not None else []) + list(args)
    return pl.pallas_call(
        body,
        name=name,
        out_shape=[jax.ShapeDtypeStruct(shape, F32) for shape in outs],
        in_specs=smem + [vmem] * len(args),
        out_specs=[vmem] * len(outs),
        scratch_shapes=[pltpu.VMEM(shape, F32) for shape in scratch],
        compiler_params=pltpu.CompilerParams(vmem_limit_bytes=32 * 2**20),
    )(*operands)


def exchange(up_values, down_values, axis, ring):
    peers = lax.axis_size(axis)
    up_pairs = [(i, (i + 1) % peers) for i in range(peers if ring else peers - 1)]
    down_pairs = [(j, i) for i, j in up_pairs]
    return lax.ppermute(up_values, axis, up_pairs), lax.ppermute(down_values, axis, down_pairs)


def on_device(right_side, acoef, beta):
    ranks, turns, files = [lax.axis_size(axis) for axis in AXES]
    pos = jnp.stack([lax.axis_index(axis) for axis in AXES] + [jnp.int32(ranks)]).astype(jnp.int32)
    planes = right_side.shape[0]
    arrays = (right_side, acoef, beta)

    last = jnp.stack([value[:, 24:] for value in arrays])
    first = jnp.stack([value[:, :8] for value in arrays])
    xb, xa = exchange(last, first, "gx", True)
    own = jnp.stack(arrays)
    last, first = call(packz, "packz", [(sum(REACH), 40, 128)] * 2, [], pos, (own, xb, xa))
    zb, za = exchange(last, first, "gz", False)
    depth = planes + 2 * DEEP
    tiles = max(tile for _, _, tile, _, _ in slots(depth)) + 1
    whole0, left, right = call(
        pack0, "pack0", [(3, depth, 48, 128)] + [(tiles, 40, 128)] * 2, [], pos, (own, xb, xa, zb, za)
    )
    before0, after0 = exchange(right, left, "gy", False)
    plane0 = (48, 256)
    half = planes // 2
    iterate0, message, weights0, diagonal0, scaled0 = call(
        down0,
        "down0",
        [(depth - 8,) + plane0, (files, 36 * half, 128), (6, depth - 6) + plane0] + [(depth - 6,) + plane0] * 2,
        [(3, depth) + plane0, (2, 3 * half, 32, 128)],
        None,
        (whole0, before0, after0),
    )

    whole1 = lax.all_to_all(message, "gz", 0, 0)
    xb, xa = exchange(whole1, whole1, "gx", True)
    depth1 = files * half
    outer0 = call(
        rest0,
        "rest0",
        [(4,) + plane0],
        [(3, depth) + plane0],
        None,
        (whole0, before0, after0, weights0, scaled0, whole1),
    )[0]
    plane1, plane2 = (48, 128), (24, 128)
    depth2 = depth1 // 2
    group = depth2 // 4
    tall1, tall2 = (depth1 + 8,) + plane1, (depth2 + 8,) + plane2
    message, weights1, scaled1, iterate1, weights2, scaled2, iterate2 = call(
        down1,
        "down1",
        [(ranks, 4 * group, 128), (6,) + tall1, tall1, tall1, (6,) + tall2, tall2, tall2],
        [(3,) + tall1, tall1, (depth1 + 2,) + plane1, (3 * depth2,) + plane1]
        + [(3,) + tall2, tall2, (depth2 + 2,) + plane2, (3 * depth2 // 2, 8, 128)]
        + [(3 * depth2,) + plane2, (6, 4 * group, 128)],
        pos,
        (whole1, xb, xa, outer0),
    )

    gathered = lax.all_to_all(message, "gx", 0, 0)
    gathered = gathered.reshape(1, ranks * 4 * group, 128)
    gathered = jnp.broadcast_to(gathered, (turns,) + gathered.shape[1:])
    gathered = lax.all_to_all(gathered, "gy", 0, 0)

    rows3 = 4 * ranks
    plane3 = (rows3, 128)
    solved, left_over = call(
        up,
        "up",
        [right_side.shape, right_side.shape],
        [(3, rows3 * group, 128), (6, group) + plane3, (group,) + plane3, (group,) + plane3, (2, group) + plane3]
        + [(group,) + plane2, (2 * group + 4,) + plane2, (10,) + plane2, (8,) + plane2, (8,) + plane2, (6,) + plane2]
        + [(6,) + plane1, (12,) + plane1, (10,) + plane1, (10,) + plane1, (8,) + plane1]
        + [(8,) + plane1, (depth - 4,) + plane0, (depth - 6,) + plane0, (depth - 6,) + plane0, (depth - 2,) + plane0],
        pos,
        (gathered, weights2, scaled2, iterate2, weights1, scaled1, iterate1)
        + (weights0, diagonal0, scaled0, iterate0, outer0),
    )
    return solved, left_over


def solution(mesh):
    spec = P("gz", "gx", "gy")
    return jax.shard_map(
        on_device, mesh=mesh, in_specs=(spec, spec, spec), out_specs=(spec, spec), check_vma=False
    )
```

```python
import functools

import jax
import jax.numpy as jnp
from jax import lax
from jax.experimental import pallas as pl
from jax.experimental.pallas import tpu as pltpu
from jax.sharding import PartitionSpec as P

LEVELS = 4
SWEEPS = 2
BOTTOM = 16

smooth_low = 0.3
bottom_low = 0.05
upper_bound = 2.0
face_scale = 1.0 / 6.0

F32 = jnp.float32
AXES = ("gx", "gy", "gz")
REACH = (4, 4, 5)
DEEP = 5


def chebyshev(steps, lower):
    centre = (upper_bound + lower) / 2.0
    half_width = (upper_bound - lower) / 2.0
    sigma = centre / half_width
    rho = 1.0 / sigma
    out = [(0.0, 1.0 / centre)]
    for _ in range(1, steps):
        rho_next = 1.0 / (2.0 * sigma - rho)
        out.append((rho_next * rho, 2.0 * rho_next / half_width))
        rho = rho_next
    return out


(_, FIRST), (CARRY, GAIN) = chebyshev(SWEEPS, smooth_low)


def roll(value, shift, axis):
    shift %= value.shape[axis]
    return pltpu.roll(value, shift, axis) if shift else value


def lane_of(shape):
    return lax.broadcasted_iota(jnp.int32, shape, 1)


def row_of(shape):
    return lax.broadcasted_iota(jnp.int32, shape, 0)


def sides(value):
    return [roll(value, 1, 0), roll(value, -1, 0), roll(value, 1, 1), roll(value, -1, 1)]


def scale_of(level):
    return face_scale * 0.25**level * 0.5


def coefficients(beta, below, above, acoef, level):
    weights = [scale_of(level) * (beta + other) for other in [below, above] + sides(beta)]
    diagonal = acoef
    for weight in weights:
        diagonal = diagonal + weight
    inside = beta > 0.0
    inverse = jnp.where(inside, 1.0 / jnp.where(inside, diagonal, 1.0), 0.0)
    return [weight * inverse for weight in weights], diagonal, inverse


def defect(scaled, weights, value, below, above):
    result = scaled - value
    for weight, other in zip(weights, [below, above] + sides(value)):
        result = result + weight * other
    return result


def dot(left, right):
    right = right.astype(jnp.bfloat16)
    high = left.astype(jnp.bfloat16)
    rest = left - high.astype(F32)
    middle = rest.astype(jnp.bfloat16)
    low = (rest - middle.astype(F32)).astype(jnp.bfloat16)
    total = jnp.dot(low, right, preferred_element_type=F32)
    total = total + jnp.dot(middle, right, preferred_element_type=F32)
    return total + jnp.dot(high, right, preferred_element_type=F32)


def matrix(shape, rule, value=1.0):
    return jnp.where(rule(row_of(shape), lane_of(shape)), value, 0.0).astype(F32)


def copies(ref, value):
    for index in range(ref.shape[0]):
        ref[index] = value


def away(plane, depth):
    return max(DEEP - plane, plane - (depth - 1 - DEEP), 0)


def slots(depth):
    wide, narrow = [], []
    for index, reach in enumerate(REACH):
        for plane in range(depth):
            if away(plane, depth) < reach:
                (wide if away(plane, depth) <= reach - 2 else narrow).append((index, plane))
    out = [(index, plane, at // 4, 32 * (at % 4), 32) for at, (index, plane) in enumerate(wide)]
    first = -(-len(wide) // 4)
    return out + [(index, plane, first + at // 16, 8 * (at % 16), 8) for at, (index, plane) in enumerate(narrow)]


def masked(pos, xb, xa, index):
    before = jnp.where(pos[0] > 0, xb[index], 0.0)
    return before, jnp.where(pos[0] < pos[3] - 1, xa[index], 0.0)


def packx(own, last, first):
    last[...] = own[:, :, 24:]
    first[...] = own[:, :, :8]


def packz(pos, own, xb, xa, last, first):
    planes, at = own.shape[1], 0
    four = lax.broadcasted_iota(jnp.int32, xb.shape[1:], 1) < 4
    for index, reach in enumerate(REACH):
        before, after = masked(pos, xb, xa, index)
        ends = jnp.where(four, after, before)
        last[at : at + reach, 0:32, :] = own[index, planes - reach :]
        last[at : at + reach, 32:40, :] = ends[planes - reach :]
        first[at : at + reach, 0:32, :] = own[index, :reach]
        first[at : at + reach, 32:40, :] = ends[:reach]
        at += reach


def pack0(pos, own, xb, xa, zb, za, whole, left, right):
    planes = own.shape[1]
    depth = planes + 2 * DEEP
    at = 0
    for index, reach in enumerate(REACH):
        for plane in range(DEEP - reach):
            for end in (plane, depth - 1 - plane):
                whole[index, end] = jnp.zeros((48, 128), F32)
        for ref, start in ((zb, DEEP - reach), (za, DEEP + planes)):
            whole[index, start : start + reach, 0:40, :] = ref[at : at + reach]
            whole[index, start : start + reach, 40:48, :] = ref[at : at + reach, 32:40, :]
        before, after = masked(pos, xb, xa, index)
        whole[index, DEEP : DEEP + planes, 0:32, :] = own[index]
        whole[index, DEEP : DEEP + planes, 32:40, :] = after
        whole[index, DEEP : DEEP + planes, 40:48, :] = before
        at += reach
    lane = lane_of((40, 128))
    four = row_of((8, 128)) < 4
    low, high = {}, {}
    for index, plane, tile, to, lanes in slots(depth):
        ends = jnp.where(four, whole[index, plane, 32:40, :], whole[index, plane, 40:48, :])
        value = jnp.concatenate([whole[index, plane, 0:32, :], ends], axis=0)
        here = (lane >= to) & (lane < to + lanes)
        zero = jnp.zeros((40, 128), F32)
        low[tile] = jnp.where(here, roll(value, to, 1), low.get(tile, zero))
        high[tile] = jnp.where(here, roll(value, to + lanes, 1), high.get(tile, zero))
    for tile in low:
        left[tile] = low[tile]
        right[tile] = high[tile]


def unpack0(whole, before, after, ext, wanted):
    lane = lane_of((40, 128))
    there = {(index, plane): rest for index, plane, *rest in slots(whole.shape[1])}
    for index, plane in wanted:
        ext[index, plane, :, 0:128] = whole[index, plane]
        if (index, plane) not in there:
            ext[index, plane, :, 128:256] = jnp.zeros((48, 128), F32)
            continue
        tile, to, lanes = there[index, plane]
        ahead = jnp.where(lane < lanes, roll(after[tile], -to, 1), 0.0)
        value = jnp.where(lane >= 128 - lanes, roll(before[tile], -lanes - to, 1), ahead)
        ext[index, plane, 0:40, 128:256] = value
        ext[index, plane, 40:48, 128:256] = value[32:40]


def planes_of(count, level, start=0):
    most = (12, 32, 16)[level]
    return pl.loop(start, start + count, unroll=max(n for n in range(1, most + 1) if count % n == 0))


def coefficients0(ext, plane):
    got, middle, inverse = coefficients(ext[2, plane], ext[2, plane - 1], ext[2, plane + 1], ext[1, plane], 0)
    return got, middle, ext[0, plane] * inverse


def first_sweeps(weights, scaled, below, middle, above):
    value = FIRST * middle
    return value + (CARRY * value + GAIN * defect(scaled, weights, value, FIRST * below, FIRST * above))


def residual0(weights, diagonal, scaled, value, below, above, at, lanes):
    cut = lambda array: array[0:32, 0:lanes]
    result = scaled[at, 0:32, 0:lanes] - cut(value)
    for index, other in enumerate([below, above] + sides(value)):
        result = result + weights[index, at, 0:32, 0:lanes] * cut(other)
    return diagonal[at, 0:32, 0:lanes] * result


def down0(whole, before, after, iterate, message, weights, diagonal, scaled, ext, sums):
    depth = whole.shape[1]
    wanted = [(index, plane) for index in range(2) for plane in range(3, depth - 3)]
    unpack0(whole, before, after, ext, wanted + [(2, plane) for plane in range(2, depth - 2)])

    @planes_of(diagonal.shape[0], 0)
    def _(plane):
        got, diagonal[plane], scaled[plane] = coefficients0(ext, plane + 3)
        for index in range(6):
            weights[index, plane] = got[index]

    @planes_of(iterate.shape[0], 0)
    def _(plane):
        faces = [weights[index, plane + 1] for index in range(6)]
        iterate[plane] = first_sweeps(faces, scaled[plane + 1], scaled[plane], scaled[plane + 1], scaled[plane + 2])

    planes = whole.shape[1] - 2 * DEEP

    def left_over(plane):
        return residual0(
            weights, diagonal, scaled, iterate[plane + 1], iterate[plane], iterate[plane + 2], plane + 2, 256
        )

    half = planes // 2

    @planes_of(half, 0)
    def _(plane):
        pairs = [left_over(2 * plane) + left_over(2 * plane + 1)]
        for index in (1, 2):
            low = ext[index, DEEP + 2 * plane, 0:32, :]
            pairs.append(low + ext[index, DEEP + 2 * plane + 1, 0:32, :])
        for index, value in enumerate(pairs):
            sums[0, index * half + plane] = value[:, 0:128]
            sums[1, index * half + plane] = value[:, 128:256]

    def rows_of(side, places):
        tall = [
            sums[side, place, pl.ds(0, 16, stride=2), :] + sums[side, place, pl.ds(1, 16, stride=2), :]
            for place in places
        ]
        return jnp.concatenate(tall, axis=0)

    even = matrix((128, 128), lambda row, lane: lane == row // 2, 0.125)
    odd = matrix((128, 128), lambda row, lane: lane == row // 2 + 64, 0.125)
    middle = dot(rows_of(0, range(0, 3 * half, 2)), even) + dot(rows_of(0, range(1, 3 * half, 2)), odd)
    ends = None
    for plane in range(half):

        def rule(row, lane, to=32 * plane):
            ahead = (row < 32) & (lane == to + row // 2)
            return ahead | ((row >= 96) & (lane == to + 16 + (row - 96) // 2))

        got = dot(rows_of(1, range(plane, 3 * half, half)), matrix((128, 128), rule, 0.125))
        ends = got if ends is None else ends + got
    copies(message, jnp.concatenate([middle, ends], axis=0))


def rest0(whole, before, after, weights, scaled, later, outer, ext):
    depth = whole.shape[1]
    ends = ((1, 2), (depth - 2, depth - 3))
    wanted = [(index, plane) for index in range(2) for end in ends for plane in end]
    unpack0(whole, before, after, ext, wanted + [(2, p) for p in (0, 1, 2, 3, depth - 4, depth - 3, depth - 2, depth - 1)])
    count = scaled.shape[0]
    for side, (far, near) in enumerate(ends):
        at, beside = (0, 1) if side == 0 else (count - 1, count - 2)
        farthest = coefficients0(ext, far)[2]
        faces, _, middle = coefficients0(ext, near)
        around = (farthest, scaled[at]) if side == 0 else (scaled[at], farthest)
        outer[3 * side] = first_sweeps(faces, middle, around[0], middle, around[1])
        faces = [weights[index, at] for index in range(6)]
        around = (middle, scaled[beside]) if side == 0 else (scaled[beside], middle)
        outer[1 + side] = first_sweeps(faces, scaled[at], around[0], scaled[at], around[1])


def unpack1(ref, there, put):
    lane = lane_of((16, 128))
    per = ref.shape[1] // 36

    @pl.loop(0, ref.shape[0], unroll=ref.shape[0])
    def _(source):
        for index in range(3):
            ends = ref[source, 96 + 16 * index : 112 + 16 * index, :]
            for plane in range(per):
                at = (2 * index + plane // 2) * 16
                value = roll(ref[source, at : at + 16, :], 64 * (plane % 2), 1)
                value = jnp.where(lane < 80, jnp.where(lane < 64, value, roll(ends, 64 - 32 * plane, 1)), 0.0)
                value = jnp.where(lane >= 112, roll(ends, 96 - 32 * plane, 1), value)
                if there is not None:
                    value = jnp.where(there, value, 0.0)
                put(index, source * per + plane, value)


def pass_all(weights, scaled, value, out, count, combine, level):
    @planes_of(count, level)
    def _(plane):
        middle = value[plane + 1]
        got = defect(
            scaled[plane + 4],
            [weights[index, plane + 4] for index in range(6)],
            middle,
            value[plane],
            value[plane + 2],
        )
        out(plane, combine(middle, got))


def prepare(ext, weights, diagonal, scaled, level):
    shape = scaled.shape[1:]
    count = scaled.shape[0] - 8
    for end in (0, count + 4):
        for plane in range(4):
            scaled[end + plane] = jnp.zeros(shape, F32)
            for index in range(6):
                weights[index, end + plane] = jnp.zeros(shape, F32)

    @planes_of(count, level, 4)
    def _(at):
        got, middle, inverse = coefficients(ext[2, at], ext[2, at - 1], ext[2, at + 1], ext[1, at], level)
        for index in range(6):
            weights[index, at] = got[index]
        diagonal[at] = middle
        scaled[at] = ext[0, at] * inverse


def down1(
    pos, own, xb, xa, earlier, message, weights1, scaled1, iterate1, weights2, scaled2, iterate2,
    ext1, diagonal1, start1, sums1, ext2, diagonal2, start2, sums2, thin, thick,
):
    depth = scaled1.shape[0] - 8
    for index in range(3):
        for end in (0, depth + 4):
            for plane in range(4):
                ext1[index, end + plane] = jnp.zeros((48, 128), F32)

    for start, ref, there in ((0, own, None), (16, xa, pos[0] < pos[3] - 1), (32, xb, pos[0] > 0)):

        def put(index, plane, value, start=start):
            ext1[index, plane + 4, start : start + 16, :] = value

        unpack1(ref, there, put)
    prepare(ext1, weights1, diagonal1, scaled1, 1)
    start1[0] = jnp.zeros((48, 128), F32)
    start1[depth + 1] = jnp.zeros((48, 128), F32)

    @planes_of(depth, 1)
    def _(plane):
        start1[plane + 1] = FIRST * scaled1[plane + 4]

    for end in (0, depth + 4):
        for plane in range(4):
            iterate1[end + plane] = jnp.zeros((48, 128), F32)

    def put1(plane, value):
        iterate1[plane + 4] = value

    pass_all(weights1, scaled1, start1, put1, depth, lambda value, got: value + (CARRY * value + GAIN * got), 1)

    half = depth // 2

    @planes_of(half, 1)
    def _(pair):
        total = None
        for plane in (2 * pair, 2 * pair + 1):
            got = diagonal1[plane + 4] * defect(
                scaled1[plane + 4],
                [weights1[index, plane + 4] for index in range(6)],
                iterate1[plane + 4],
                iterate1[plane + 3],
                iterate1[plane + 5],
            )
            total = got if total is None else total + got
        sums1[pair] = total
        for index in (1, 2):
            sums1[index * half + pair] = ext1[index, 2 * pair + 4] + ext1[index, 2 * pair + 5]

    @planes_of(3 * half, 1)
    def _(plane):
        thin[plane] = sums1[plane, pl.ds(0, 24, stride=2), :] + sums1[plane, pl.ds(1, 24, stride=2), :]

    def to_level2(row, lane):
        place = jnp.where(lane < 64, lane, lane - 128)
        source = lax.shift_right_arithmetic(jnp.where(row < 96, row, row - 128), 1)
        return (source == place) & ((row < 80) | (row >= 112))

    level2 = matrix((128, 128), to_level2, 0.125)
    for index in range(3):
        values = thin[index * half : (index + 1) * half].reshape(half * 24, 128)
        ext2[index, 4 : 4 + half] = dot(values, level2).reshape(half, 24, 128)
        for end in (0, half + 4):
            for plane in range(4):
                ext2[index, end + plane] = jnp.zeros((24, 128), F32)

    prepare(ext2, weights2, diagonal2, scaled2, 2)
    start2[0] = jnp.zeros((24, 128), F32)
    start2[half + 1] = jnp.zeros((24, 128), F32)

    @pl.loop(0, half)
    def _(plane):
        start2[plane + 1] = FIRST * scaled2[plane + 4]

    for end in (0, half + 4):
        for plane in range(4):
            iterate2[end + plane] = jnp.zeros((24, 128), F32)

    def put2(plane, value):
        iterate2[plane + 4] = value

    pass_all(weights2, scaled2, start2, put2, half, lambda value, got: value + (CARRY * value + GAIN * got), 2)

    quarter = half // 2
    group = quarter // 2
    place2 = []
    for plane in range(quarter):
        to = 64 * (plane // group) + 16 * lax.rem(pos[1] + plane % group, 4)
        place2.append(matrix((128, 128), lambda row, lane, to=to: (row < 32) & (lane == row // 2 + to), 0.125))
        thick[plane] = jnp.zeros((16, 128), F32)
    for index in range(3):
        for plane in range(quarter):
            if index == 0:
                total = None
                for at in (2 * plane, 2 * plane + 1):
                    got = diagonal2[at + 4] * defect(
                        scaled2[at + 4],
                        [weights2[face, at + 4] for face in range(6)],
                        iterate2[at + 4],
                        iterate2[at + 3],
                        iterate2[at + 5],
                    )
                    total = got if total is None else total + got
                total = total[0:8]
            else:
                total = ext2[index, 2 * plane + 4, 0:8, :] + ext2[index, 2 * plane + 5, 0:8, :]
            at = index * quarter + plane
            sums2[at] = total
            thick[plane, pl.ds(index, 4, stride=3), :] = (
                sums2[at, pl.ds(0, 4, stride=2), :] + sums2[at, pl.ds(1, 4, stride=2), :]
            )
    result = dot(thick[0], place2[0])
    for plane in range(1, quarter):
        result = result + dot(thick[plane], place2[plane])
    copies(message, result)


def packy(pieces, message):
    for at in range(pieces.shape[0]):
        copies(message.at[:, 12 * at : 12 * at + 12, :], pieces[at, 0:12, :])


def bottom(gathered, whole, weights, scaled, update, values):
    group = weights.shape[1]
    rows = weights.shape[2]
    shape = (rows, 128)
    row, lane = row_of(shape), lane_of(shape)
    column = lax.rem(lane, 64)
    quarter = column // 16
    for index in range(3):
        pieces = [gathered[source, pl.ds(index, rows, stride=3), :] for source in range(4)]
        for plane in range(group):
            total = pieces[0]
            for source in range(1, 4):
                total = jnp.where(quarter == (source + plane) % 4, pieces[source], total)
            if plane:
                near, far = roll(total, -16 * plane, 1), roll(total, 64 - 16 * plane, 1)
                total = jnp.where(quarter + plane < 4, near, far)
            whole[index, plane] = total

    def plane_at(index, plane):
        return whole[index, plane]

    def around(get, plane):
        middle = get(plane)
        below = get(plane - 1) if plane else roll(get(group - 1), 64, 1)
        above = get(plane + 1) if plane < group - 1 else roll(get(0), 64, 1)
        return [below, above] + sides(middle)

    for plane in range(group):
        beta = plane_at(2, plane)
        masks = [
            (lane >= 64) if plane == 0 else None,
            (lane < 64) if plane == group - 1 else None,
            row > 0,
            row < rows - 1,
            column > 0,
            column < 63,
        ]
        near = around(lambda at: plane_at(2, at), plane)
        near = [other if mask is None else jnp.where(mask, other, 0.0) for other, mask in zip(near, masks)]
        faces = [scale_of(3) * (beta + other) for other in near]
        diagonal = plane_at(1, plane)
        for face in faces:
            diagonal = diagonal + face
        inverse = 1.0 / diagonal
        for index, (face, mask) in enumerate(zip(faces, masks)):
            face = face * inverse
            weights[index, plane] = face if mask is None else jnp.where(mask, face, 0.0)
        scaled[plane] = plane_at(0, plane) * inverse

    steps = chebyshev(BOTTOM, bottom_low)
    for plane in range(group):
        value = steps[0][1] * scaled[plane]
        update[plane] = value
        values[0, plane] = value
    for step, (carry, gain) in enumerate(steps[1:]):
        now, later = step % 2, (step + 1) % 2
        for plane in range(group):
            middle = values[now, plane]
            got = scaled[plane] - middle
            for index, other in enumerate(around(lambda at: values[now, at], plane)):
                got = got + weights[index, plane] * other
            moved = carry * update[plane] + gain * got
            update[plane] = moved
            values[later, plane] = middle + moved


def finish(at, iterate, weights, scaled, level, update, middle, put):
    count = iterate.shape[0]

    @planes_of(count - 2, level)
    def _(plane):
        value = iterate[plane + 1]
        got = FIRST * defect(
            scaled[at + plane + 1],
            [weights[index, at + plane + 1] for index in range(6)],
            value,
            iterate[plane],
            iterate[plane + 2],
        )
        update[plane] = got
        middle[plane] = value + got

    @planes_of(count - 4, level)
    def _(plane):
        value = middle[plane + 1]
        got = defect(
            scaled[at + plane + 2],
            [weights[index, at + plane + 2] for index in range(6)],
            value,
            middle[plane],
            middle[plane + 2],
        )
        put(plane, value + (CARRY * update[plane + 1] + GAIN * got))


def up(
    pos, gathered, weights2, scaled2, iterate2, weights1, scaled1, iterate1,
    weights0, diagonal0, scaled0, iterate0, outer0, solved, left_over,
    whole3, weights3, scaled3, update3, values3,
    thin3, error2, value2, update2, middle2, out2,
    tall1, value1, update1, middle1, out1,
    tall0, value0, update0, middle0, out0,
):
    bottom(gathered, whole3, weights3, scaled3, update3, values3)
    group, rows = weights3.shape[1], weights3.shape[2]
    at_x, at_y, at_z = 4 * pos[0], 16 * pos[1], pos[2]
    last = (BOTTOM - 1) % 2

    lane = lane_of((8, 128))
    near = lax.rem(lane, 64)
    fits = ((near < 16) | ((near < 20) & (pos[1] < 3)) | ((near >= 60) & (pos[1] > 0))).astype(F32)
    first_row, last_row = (pos[0] > 0).astype(F32), (pos[0] < pos[3] - 1).astype(F32)
    low = row_of((8, 128)) < 4
    own = jnp.where(low, fits, fits * last_row)
    left = jnp.where(low, 0.0, fits * first_row)
    for plane in range(group):
        moved = pltpu.roll(values3[last, plane], lax.rem(rows - at_x, rows), 0)
        both = jnp.concatenate([moved[0:8], moved[rows - 8 :]], axis=0)
        both = pltpu.roll(both, lax.rem(128 - at_y, 128), 1)
        ahead, behind = both[0:8] * own, both[8:16] * left
        for start in (0, 1):
            thin3[plane, pl.ds(start, 8, stride=2), :] = ahead
            thin3[plane, pl.ds(16 + start, 4, stride=2), :] = behind[4:8]

    def to_level2(row, lane):
        side, within = lane // 128, lax.rem(lane, 128)
        place = jnp.where(within < 64, within, within - 128)
        source = jnp.where(side == 0, lax.rem(row, 128), lax.rem(row + 64, 128))
        source = jnp.where(source < 64, source, source - 128)
        return (source == lax.shift_right_arithmetic(place, 1)) & ((within < 40) | (within >= 120))

    spread = dot(thin3[...].reshape(group * 24, 128), matrix((128, 256), to_level2)).reshape(group, 24, 256)
    for plane in range(group):
        for side in range(2):
            error2[side * group + plane + 2] = spread[plane, :, 128 * side : 128 * side + 128]
    for end in (0, 2 * group + 2):
        for plane in range(2):
            error2[end + plane] = jnp.zeros((24, 128), F32)

    for plane in range(10):
        value2[plane] = iterate2[2 * at_z + plane] + error2[at_z + plane // 2]

    def put2(plane, value):
        out2[plane] = value

    finish(2 * at_z, value2, weights2, scaled2, 2, update2, middle2, put2)

    def to_level1(row, lane):
        place = jnp.where(lane < 96, lane, lane - 128)
        source = lax.shift_right_arithmetic(place, 1)
        return (jnp.where(row < 64, row, row - 128) == source) & ((lane < 80) | (lane >= 112))

    wide1 = matrix((128, 128), to_level1)
    for plane in range(6):
        tall1[plane, pl.ds(0, 24, stride=2), :] = out2[plane]
        tall1[plane, pl.ds(1, 24, stride=2), :] = out2[plane]
    spread = dot(tall1[...].reshape(6 * 48, 128), wide1).reshape(6, 48, 128)
    for plane in range(12):
        value1[plane] = iterate1[4 * at_z + plane] + spread[plane // 2]

    def put1(plane, value):
        out1[plane] = value

    finish(4 * at_z, value1, weights1, scaled1, 1, update1, middle1, put1)

    def to_level0(row, lane):
        place = jnp.where(lane < 192, lane, lane - 256)
        source = lax.shift_right_arithmetic(place, 1)
        return (jnp.where(row < 96, row, row - 128) == source) & ((lane < 136) | (lane >= 248))

    wide0 = matrix((128, 256), to_level0)
    for plane in range(8):
        value = out1[plane]
        tall0[plane, pl.ds(0, 24, stride=2), :] = value[0:24]
        tall0[plane, pl.ds(1, 24, stride=2), :] = value[0:24]
        tall0[plane, pl.ds(40, 4, stride=2), :] = value[44:48]
        tall0[plane, pl.ds(41, 4, stride=2), :] = value[44:48]

    @planes_of(8, 1)
    def _(plane):
        value = dot(tall0[plane], wide0)
        out0[2 * plane] = value
        out0[2 * plane + 1] = value

    @planes_of(iterate0.shape[0], 0)
    def _(plane):
        value0[plane + 2] = iterate0[plane] + out0[plane + 3]

    count = value0.shape[0]
    for at, plane in enumerate((0, 1, count - 2, count - 1)):
        value0[plane] = outer0[at] + out0[plane + 1]


    @planes_of(count - 2, 0)
    def _(plane):
        value = value0[plane + 1]
        got = FIRST * defect(
            scaled0[plane],
            [weights0[index, plane] for index in range(6)],
            value,
            value0[plane],
            value0[plane + 2],
        )
        update0[plane] = got
        middle0[plane] = value + got

    @planes_of(count - 4, 0)
    def _(plane):
        value = middle0[plane + 1]
        got = defect(
            scaled0[plane + 1],
            [weights0[index, plane + 1] for index in range(6)],
            value,
            middle0[plane],
            middle0[plane + 2],
        )
        out0[plane] = value + (CARRY * update0[plane + 1] + GAIN * got)

    @planes_of(count - 6, 0)
    def _(plane):
        value = out0[plane + 1]
        solved[plane] = value[0:32, 0:128]
        left_over[plane] = residual0(
            weights0, diagonal0, scaled0, value, out0[plane], out0[plane + 2], plane + 2, 128
        )


def call(body, name, outs, scratch, pos, args):
    vmem = pl.BlockSpec(memory_space=pltpu.VMEM)
    smem = [pl.BlockSpec(memory_space=pltpu.SMEM)] if pos is not None else []
    operands = ([pos] if pos is not None else []) + list(args)
    return pl.pallas_call(
        body,
        name=name,
        out_shape=[jax.ShapeDtypeStruct(shape, F32) for shape in outs],
        in_specs=smem + [vmem] * len(args),
        out_specs=[vmem] * len(outs),
        scratch_shapes=[pltpu.VMEM(shape, F32) for shape in scratch],
        compiler_params=pltpu.CompilerParams(vmem_limit_bytes=32 * 2**20),
    )(*operands)


def exchange(up_values, down_values, axis, ring):
    peers = lax.axis_size(axis)
    up_pairs = [(i, (i + 1) % peers) for i in range(peers if ring else peers - 1)]
    down_pairs = [(j, i) for i, j in up_pairs]
    return lax.ppermute(up_values, axis, up_pairs), lax.ppermute(down_values, axis, down_pairs)


def on_device(right_side, acoef, beta):
    ranks, turns, files = [lax.axis_size(axis) for axis in AXES]
    pos = jnp.stack([lax.axis_index(axis) for axis in AXES] + [jnp.int32(ranks)]).astype(jnp.int32)
    planes = right_side.shape[0]
    arrays = (right_side, acoef, beta)

    own = jnp.stack(arrays)
    last, first = call(packx, "packx", [(3, planes, 8, 128)] * 2, [], None, (own,))
    xb, xa = exchange(last, first, "gx", True)
    last, first = call(packz, "packz", [(sum(REACH), 40, 128)] * 2, [], pos, (own, xb, xa))
    zb, za = exchange(last, first, "gz", False)
    depth = planes + 2 * DEEP
    tiles = max(tile for _, _, tile, _, _ in slots(depth)) + 1
    whole0, left, right = call(
        pack0, "pack0", [(3, depth, 48, 128)] + [(tiles, 40, 128)] * 2, [], pos, (own, xb, xa, zb, za)
    )
    before0, after0 = exchange(right, left, "gy", False)
    plane0 = (48, 256)
    half = planes // 2
    iterate0, message, weights0, diagonal0, scaled0 = call(
        down0,
        "down0",
        [(depth - 8,) + plane0, (files, 36 * half, 128), (6, depth - 6) + plane0] + [(depth - 6,) + plane0] * 2,
        [(3, depth) + plane0, (2, 3 * half, 32, 128)],
        None,
        (whole0, before0, after0),
    )

    whole1 = lax.all_to_all(message, "gz", 0, 0)
    xb, xa = exchange(whole1, whole1, "gx", True)
    depth1 = files * half
    outer0 = call(
        rest0,
        "rest0",
        [(4,) + plane0],
        [(3, depth) + plane0],
        None,
        (whole0, before0, after0, weights0, scaled0, whole1),
    )[0]
    plane1, plane2 = (48, 128), (24, 128)
    depth2 = depth1 // 2
    group = depth2 // 4
    tall1, tall2 = (depth1 + 8,) + plane1, (depth2 + 8,) + plane2
    message, weights1, scaled1, iterate1, weights2, scaled2, iterate2 = call(
        down1,
        "down1",
        [(ranks, 16, 128), (6,) + tall1, tall1, tall1, (6,) + tall2, tall2, tall2],
        [(3,) + tall1, tall1, (depth1 + 2,) + plane1, (3 * depth2,) + plane1]
        + [(3,) + tall2, tall2, (depth2 + 2,) + plane2, (3 * depth2 // 2, 8, 128)]
        + [(3 * depth2,) + plane2, (2 * group, 16, 128)],
        pos,
        (whole1, xb, xa, outer0),
    )

    gathered = lax.all_to_all(message, "gx", 0, 0)
    gathered = call(packy, "packy", [(turns, 12 * ranks, 128)], [], None, (gathered,))[0]
    gathered = lax.all_to_all(gathered, "gy", 0, 0)

    rows3 = 4 * ranks
    plane3 = (rows3, 128)
    solved, left_over = call(
        up,
        "up",
        [right_side.shape, right_side.shape],
        [(3, group) + plane3, (6, group) + plane3, (group,) + plane3, (group,) + plane3, (2, group) + plane3]
        + [(group,) + plane2, (2 * group + 4,) + plane2, (10,) + plane2, (8,) + plane2, (8,) + plane2, (6,) + plane2]
        + [(6,) + plane1, (12,) + plane1, (10,) + plane1, (10,) + plane1, (8,) + plane1]
        + [(8,) + plane1, (depth - 4,) + plane0, (depth - 6,) + plane0, (depth - 6,) + plane0, (depth - 2,) + plane0],
        pos,
        (gathered, weights2, scaled2, iterate2, weights1, scaled1, iterate1)
        + (weights0, diagonal0, scaled0, iterate0, outer0),
    )
    return solved, left_over


def solution(mesh):
    spec = P("gz", "gx", "gy")
    return jax.shard_map(
        on_device, mesh=mesh, in_specs=(spec, spec, spec), out_specs=(spec, spec), check_vma=False
    )
```

```python
import functools

import jax
import jax.numpy as jnp
from jax import lax
from jax.experimental import pallas as pl
from jax.experimental.pallas import tpu as pltpu
from jax.sharding import PartitionSpec as P

LEVELS = 4
SWEEPS = 2
BOTTOM = 16

smooth_low = 0.3
bottom_low = 0.05
upper_bound = 2.0
face_scale = 1.0 / 6.0

F32 = jnp.float32
AXES = ("gx", "gy", "gz")
REACH = (4, 4, 5)
DEEP = 5


def chebyshev(steps, lower):
    centre = (upper_bound + lower) / 2.0
    half_width = (upper_bound - lower) / 2.0
    sigma = centre / half_width
    rho = 1.0 / sigma
    out = [(0.0, 1.0 / centre)]
    for _ in range(1, steps):
        rho_next = 1.0 / (2.0 * sigma - rho)
        out.append((rho_next * rho, 2.0 * rho_next / half_width))
        rho = rho_next
    return out


(_, FIRST), (CARRY, GAIN) = chebyshev(SWEEPS, smooth_low)


def roll(value, shift, axis):
    shift %= value.shape[axis]
    return pltpu.roll(value, shift, axis) if shift else value


def lane_of(shape):
    return lax.broadcasted_iota(jnp.int32, shape, 1)


def row_of(shape):
    return lax.broadcasted_iota(jnp.int32, shape, 0)


def sides(value):
    return [roll(value, 1, 0), roll(value, -1, 0), roll(value, 1, 1), roll(value, -1, 1)]


def scale_of(level):
    return face_scale * 0.25**level * 0.5


def coefficients(beta, below, above, acoef, level):
    weights = [scale_of(level) * (beta + other) for other in [below, above] + sides(beta)]
    diagonal = acoef
    for weight in weights:
        diagonal = diagonal + weight
    inside = beta > 0.0
    inverse = jnp.where(inside, 1.0 / jnp.where(inside, diagonal, 1.0), 0.0)
    return [weight * inverse for weight in weights], diagonal, inverse


def defect(scaled, weights, value, below, above):
    result = scaled - value
    for weight, other in zip(weights, [below, above] + sides(value)):
        result = result + weight * other
    return result


def dot(left, right):
    right = right.astype(jnp.bfloat16)
    high = left.astype(jnp.bfloat16)
    rest = left - high.astype(F32)
    middle = rest.astype(jnp.bfloat16)
    low = (rest - middle.astype(F32)).astype(jnp.bfloat16)
    total = jnp.dot(low, right, preferred_element_type=F32)
    total = total + jnp.dot(middle, right, preferred_element_type=F32)
    return total + jnp.dot(high, right, preferred_element_type=F32)


def matrix(shape, rule, value=1.0):
    return jnp.where(rule(row_of(shape), lane_of(shape)), value, 0.0).astype(F32)


def copies(ref, value):
    for index in range(ref.shape[0]):
        ref[index] = value


def away(plane, depth):
    return max(DEEP - plane, plane - (depth - 1 - DEEP), 0)


def slots(depth):
    wide, narrow = [], []
    for index, reach in enumerate(REACH):
        for plane in range(depth):
            if away(plane, depth) < reach:
                (wide if away(plane, depth) <= reach - 2 else narrow).append((index, plane))
    out = [(index, plane, at // 4, 32 * (at % 4), 32) for at, (index, plane) in enumerate(wide)]
    first = -(-len(wide) // 4)
    return out + [(index, plane, first + at // 16, 8 * (at % 16), 8) for at, (index, plane) in enumerate(narrow)]


def masked(pos, xb, xa, index):
    before = jnp.where(pos[0] > 0, xb[index], 0.0)
    return before, jnp.where(pos[0] < pos[3] - 1, xa[index], 0.0)


def packx(own, last, first):
    last[...] = own[:, :, 24:]
    first[...] = own[:, :, :8]


def packz(pos, own, xb, xa, last, first):
    planes, at = own.shape[1], 0
    four = lax.broadcasted_iota(jnp.int32, xb.shape[1:], 1) < 4
    for index, reach in enumerate(REACH):
        before, after = masked(pos, xb, xa, index)
        ends = jnp.where(four, after, before)
        last[at : at + reach, 0:32, :] = own[index, planes - reach :]
        last[at : at + reach, 32:40, :] = ends[planes - reach :]
        first[at : at + reach, 0:32, :] = own[index, :reach]
        first[at : at + reach, 32:40, :] = ends[:reach]
        at += reach


def pack0(pos, own, xb, xa, zb, za, whole, left, right):
    planes = own.shape[1]
    depth = planes + 2 * DEEP
    at = 0
    for index, reach in enumerate(REACH):
        for plane in range(DEEP - reach):
            for end in (plane, depth - 1 - plane):
                whole[index, end] = jnp.zeros((48, 128), F32)
        for ref, start in ((zb, DEEP - reach), (za, DEEP + planes)):
            whole[index, start : start + reach, 0:40, :] = ref[at : at + reach]
            whole[index, start : start + reach, 40:48, :] = ref[at : at + reach, 32:40, :]
        before, after = masked(pos, xb, xa, index)
        whole[index, DEEP : DEEP + planes, 0:32, :] = own[index]
        whole[index, DEEP : DEEP + planes, 32:40, :] = after
        whole[index, DEEP : DEEP + planes, 40:48, :] = before
        at += reach
    lane = lane_of((40, 128))
    four = row_of((8, 128)) < 4
    low, high = {}, {}
    for index, plane, tile, to, lanes in slots(depth):
        ends = jnp.where(four, whole[index, plane, 32:40, :], whole[index, plane, 40:48, :])
        value = jnp.concatenate([whole[index, plane, 0:32, :], ends], axis=0)
        moved, back = roll(value, to, 1), (to - lanes) % 128
        zero = jnp.zeros((40, 128), F32)
        low[tile] = jnp.where((lane >= to) & (lane < to + lanes), moved, low.get(tile, zero))
        high[tile] = jnp.where((lane >= back) & (lane < back + lanes), moved, high.get(tile, zero))
    for tile in low:
        left[tile] = low[tile]
        right[tile] = high[tile]


def unpack0(whole, before, after, ext, wanted):
    lane = lane_of((40, 128))
    there = {(index, plane): rest for index, plane, *rest in slots(whole.shape[1])}
    for index, plane in wanted:
        ext[index, plane, :, 0:128] = whole[index, plane]
        if (index, plane) not in there:
            ext[index, plane, :, 128:256] = jnp.zeros((48, 128), F32)
            continue
        tile, to, lanes = there[index, plane]
        value = roll(jnp.where((lane >= to) & (lane < to + lanes), after[tile], before[tile]), -to, 1)
        value = jnp.where((lane < lanes) | (lane >= 128 - lanes), value, 0.0)
        ext[index, plane, 0:40, 128:256] = value
        ext[index, plane, 40:48, 128:256] = value[32:40]


def planes_of(count, level, start=0):
    most = (12, 32, 16)[level]
    return pl.loop(start, start + count, unroll=max(n for n in range(1, most + 1) if count % n == 0))


def coefficients0(ext, plane):
    got, middle, inverse = coefficients(ext[2, plane], ext[2, plane - 1], ext[2, plane + 1], ext[1, plane], 0)
    return got, middle, ext[0, plane] * inverse


def first_sweeps(weights, scaled, below, middle, above):
    value = FIRST * middle
    return value + (CARRY * value + GAIN * defect(scaled, weights, value, FIRST * below, FIRST * above))


def residual0(weights, diagonal, scaled, value, below, above, at, lanes):
    cut = lambda array: array[0:32, 0:lanes]
    result = scaled[at, 0:32, 0:lanes] - cut(value)
    for index, other in enumerate([below, above] + sides(value)):
        result = result + weights[index, at, 0:32, 0:lanes] * cut(other)
    return diagonal[at, 0:32, 0:lanes] * result


def down0(whole, before, after, iterate, message, weights, diagonal, scaled, ext, sums):
    depth = whole.shape[1]
    wanted = [(index, plane) for index in range(2) for plane in range(3, depth - 3)]
    unpack0(whole, before, after, ext, wanted + [(2, plane) for plane in range(2, depth - 2)])

    @planes_of(diagonal.shape[0], 0)
    def _(plane):
        got, diagonal[plane], scaled[plane] = coefficients0(ext, plane + 3)
        for index in range(6):
            weights[index, plane] = got[index]

    @planes_of(iterate.shape[0], 0)
    def _(plane):
        faces = [weights[index, plane + 1] for index in range(6)]
        iterate[plane] = first_sweeps(faces, scaled[plane + 1], scaled[plane], scaled[plane + 1], scaled[plane + 2])

    planes = whole.shape[1] - 2 * DEEP

    def left_over(plane):
        return residual0(
            weights, diagonal, scaled, iterate[plane + 1], iterate[plane], iterate[plane + 2], plane + 2, 256
        )

    half = planes // 2

    @planes_of(half, 0)
    def _(plane):
        pairs = [left_over(2 * plane) + left_over(2 * plane + 1)]
        for index in (1, 2):
            low = ext[index, DEEP + 2 * plane, 0:32, :]
            pairs.append(low + ext[index, DEEP + 2 * plane + 1, 0:32, :])
        for index, value in enumerate(pairs):
            sums[0, index * half + plane] = value[:, 0:128]
            sums[1, index * half + plane] = value[:, 128:256]

    def rows_of(side, places):
        tall = [
            sums[side, place, pl.ds(0, 16, stride=2), :] + sums[side, place, pl.ds(1, 16, stride=2), :]
            for place in places
        ]
        return jnp.concatenate(tall, axis=0)

    even = matrix((128, 128), lambda row, lane: lane == row // 2, 0.125)
    odd = matrix((128, 128), lambda row, lane: lane == row // 2 + 64, 0.125)
    middle = dot(rows_of(0, range(0, 3 * half, 2)), even) + dot(rows_of(0, range(1, 3 * half, 2)), odd)
    ends = None
    for plane in range(half):

        def rule(row, lane, ahead=-32 * plane % 128, behind=(48 - 32 * plane) % 128):
            return ((row < 32) & (lane == ahead + row // 2)) | ((row >= 96) & (lane == behind + (row - 96) // 2))

        got = dot(rows_of(1, range(plane, 3 * half, half)), matrix((128, 128), rule, 0.125))
        ends = got if ends is None else ends + got
    copies(message, jnp.concatenate([middle, ends], axis=0))


def rest0(whole, before, after, weights, scaled, later, outer, ext):
    depth = whole.shape[1]
    ends = ((1, 2), (depth - 2, depth - 3))
    wanted = [(index, plane) for index in range(2) for end in ends for plane in end]
    unpack0(whole, before, after, ext, wanted + [(2, p) for p in (0, 1, 2, 3, depth - 4, depth - 3, depth - 2, depth - 1)])
    count = scaled.shape[0]
    for side, (far, near) in enumerate(ends):
        at, beside = (0, 1) if side == 0 else (count - 1, count - 2)
        farthest = coefficients0(ext, far)[2]
        faces, _, middle = coefficients0(ext, near)
        around = (farthest, scaled[at]) if side == 0 else (scaled[at], farthest)
        outer[3 * side] = first_sweeps(faces, middle, around[0], middle, around[1])
        faces = [weights[index, at] for index in range(6)]
        around = (middle, scaled[beside]) if side == 0 else (scaled[beside], middle)
        outer[1 + side] = first_sweeps(faces, scaled[at], around[0], scaled[at], around[1])


def unpack1(ref, there, put):
    lane = lane_of((16, 128))
    per = ref.shape[1] // 36

    @pl.loop(0, ref.shape[0], unroll=ref.shape[0])
    def _(source):
        for index in range(3):
            ends = ref[source, 96 + 16 * index : 112 + 16 * index, :]
            for plane in range(per):
                at = (2 * index + plane // 2) * 16
                value = roll(ref[source, at : at + 16, :], 64 * (plane % 2), 1)
                halo = jnp.where((lane < 80) | (lane >= 112), roll(ends, 64 + 32 * plane, 1), 0.0)
                value = jnp.where(lane < 64, value, halo)
                if there is not None:
                    value = jnp.where(there, value, 0.0)
                put(index, source * per + plane, value)


def pass_all(weights, scaled, value, out, count, combine, level):
    @planes_of(count, level)
    def _(plane):
        middle = value[plane + 1]
        got = defect(
            scaled[plane + 4],
            [weights[index, plane + 4] for index in range(6)],
            middle,
            value[plane],
            value[plane + 2],
        )
        out(plane, combine(middle, got))


def prepare(ext, weights, diagonal, scaled, level):
    shape = scaled.shape[1:]
    count = scaled.shape[0] - 8
    for end in (0, count + 4):
        for plane in range(4):
            scaled[end + plane] = jnp.zeros(shape, F32)
            for index in range(6):
                weights[index, end + plane] = jnp.zeros(shape, F32)

    @planes_of(count, level, 4)
    def _(at):
        got, middle, inverse = coefficients(ext[2, at], ext[2, at - 1], ext[2, at + 1], ext[1, at], level)
        for index in range(6):
            weights[index, at] = got[index]
        diagonal[at] = middle
        scaled[at] = ext[0, at] * inverse


def down1(
    pos, own, xb, xa, earlier, message, weights1, scaled1, iterate1, weights2, scaled2, iterate2,
    ext1, diagonal1, start1, sums1, ext2, diagonal2, start2, sums2, thin, thick,
):
    depth = scaled1.shape[0] - 8
    for index in range(3):
        for end in (0, depth + 4):
            for plane in range(4):
                ext1[index, end + plane] = jnp.zeros((48, 128), F32)

    for start, ref, there in ((0, own, None), (16, xa, pos[0] < pos[3] - 1), (32, xb, pos[0] > 0)):

        def put(index, plane, value, start=start):
            ext1[index, plane + 4, start : start + 16, :] = value

        unpack1(ref, there, put)
    prepare(ext1, weights1, diagonal1, scaled1, 1)
    start1[0] = jnp.zeros((48, 128), F32)
    start1[depth + 1] = jnp.zeros((48, 128), F32)

    @planes_of(depth, 1)
    def _(plane):
        start1[plane + 1] = FIRST * scaled1[plane + 4]

    for end in (0, depth + 4):
        for plane in range(4):
            iterate1[end + plane] = jnp.zeros((48, 128), F32)

    def put1(plane, value):
        iterate1[plane + 4] = value

    pass_all(weights1, scaled1, start1, put1, depth, lambda value, got: value + (CARRY * value + GAIN * got), 1)

    half = depth // 2

    @planes_of(half, 1)
    def _(pair):
        total = None
        for plane in (2 * pair, 2 * pair + 1):
            got = diagonal1[plane + 4] * defect(
                scaled1[plane + 4],
                [weights1[index, plane + 4] for index in range(6)],
                iterate1[plane + 4],
                iterate1[plane + 3],
                iterate1[plane + 5],
            )
            total = got if total is None else total + got
        sums1[pair] = total
        for index in (1, 2):
            sums1[index * half + pair] = ext1[index, 2 * pair + 4] + ext1[index, 2 * pair + 5]

    @planes_of(3 * half, 1)
    def _(plane):
        thin[plane] = sums1[plane, pl.ds(0, 24, stride=2), :] + sums1[plane, pl.ds(1, 24, stride=2), :]

    def to_level2(row, lane):
        place = jnp.where(lane < 64, lane, lane - 128)
        source = lax.shift_right_arithmetic(jnp.where(row < 96, row, row - 128), 1)
        return (source == place) & ((row < 80) | (row >= 112))

    level2 = matrix((128, 128), to_level2, 0.125)
    for index in range(3):
        values = thin[index * half : (index + 1) * half].reshape(half * 24, 128)
        ext2[index, 4 : 4 + half] = dot(values, level2).reshape(half, 24, 128)
        for end in (0, half + 4):
            for plane in range(4):
                ext2[index, end + plane] = jnp.zeros((24, 128), F32)

    prepare(ext2, weights2, diagonal2, scaled2, 2)
    start2[0] = jnp.zeros((24, 128), F32)
    start2[half + 1] = jnp.zeros((24, 128), F32)

    @pl.loop(0, half)
    def _(plane):
        start2[plane + 1] = FIRST * scaled2[plane + 4]

    for end in (0, half + 4):
        for plane in range(4):
            iterate2[end + plane] = jnp.zeros((24, 128), F32)

    def put2(plane, value):
        iterate2[plane + 4] = value

    pass_all(weights2, scaled2, start2, put2, half, lambda value, got: value + (CARRY * value + GAIN * got), 2)

    quarter = half // 2
    group = quarter // 2
    place2 = []
    for plane in range(quarter):
        to = 64 * (plane // group) + 16 * lax.rem(pos[1] + plane % group, 4)
        place2.append(matrix((128, 128), lambda row, lane, to=to: (row < 32) & (lane == row // 2 + to), 0.125))
        thick[plane] = jnp.zeros((16, 128), F32)
    for index in range(3):
        for plane in range(quarter):
            if index == 0:
                total = None
                for at in (2 * plane, 2 * plane + 1):
                    got = diagonal2[at + 4] * defect(
                        scaled2[at + 4],
                        [weights2[face, at + 4] for face in range(6)],
                        iterate2[at + 4],
                        iterate2[at + 3],
                        iterate2[at + 5],
                    )
                    total = got if total is None else total + got
                total = total[0:8]
            else:
                total = ext2[index, 2 * plane + 4, 0:8, :] + ext2[index, 2 * plane + 5, 0:8, :]
            at = index * quarter + plane
            sums2[at] = total
            thick[plane, pl.ds(index, 4, stride=3), :] = (
                sums2[at, pl.ds(0, 4, stride=2), :] + sums2[at, pl.ds(1, 4, stride=2), :]
            )
    result = dot(thick[0], place2[0])
    for plane in range(1, quarter):
        result = result + dot(thick[plane], place2[plane])
    copies(message, result)


def packy(pieces, message):
    for at in range(pieces.shape[0]):
        copies(message.at[:, 12 * at : 12 * at + 12, :], pieces[at, 0:12, :])


def bottom(gathered, whole, weights, scaled, update, values):
    group = weights.shape[1]
    rows = weights.shape[2]
    shape = (rows, 128)
    row, lane = row_of(shape), lane_of(shape)
    column = lax.rem(lane, 64)
    quarter = column // 16
    for index in range(3):
        pieces = [gathered[source, pl.ds(index, rows, stride=3), :] for source in range(4)]
        for plane in range(group):
            total = pieces[0]
            for source in range(1, 4):
                total = jnp.where(quarter == (source + plane) % 4, pieces[source], total)
            if plane:
                near, far = roll(total, -16 * plane, 1), roll(total, 64 - 16 * plane, 1)
                total = jnp.where(quarter + plane < 4, near, far)
            whole[index, plane] = total

    def plane_at(index, plane):
        return whole[index, plane]

    def around(get, plane):
        middle = get(plane)
        below = get(plane - 1) if plane else roll(get(group - 1), 64, 1)
        above = get(plane + 1) if plane < group - 1 else roll(get(0), 64, 1)
        return [below, above] + sides(middle)

    for plane in range(group):
        beta = plane_at(2, plane)
        masks = [
            (lane >= 64) if plane == 0 else None,
            (lane < 64) if plane == group - 1 else None,
            row > 0,
            row < rows - 1,
            column > 0,
            column < 63,
        ]
        near = around(lambda at: plane_at(2, at), plane)
        near = [other if mask is None else jnp.where(mask, other, 0.0) for other, mask in zip(near, masks)]
        faces = [scale_of(3) * (beta + other) for other in near]
        diagonal = plane_at(1, plane)
        for face in faces:
            diagonal = diagonal + face
        inverse = 1.0 / diagonal
        for index, (face, mask) in enumerate(zip(faces, masks)):
            face = face * inverse
            weights[index, plane] = face if mask is None else jnp.where(mask, face, 0.0)
        scaled[plane] = plane_at(0, plane) * inverse

    steps = chebyshev(BOTTOM, bottom_low)
    for plane in range(group):
        value = steps[0][1] * scaled[plane]
        update[plane] = value
        values[0, plane] = value
    for step, (carry, gain) in enumerate(steps[1:]):
        now, later = step % 2, (step + 1) % 2
        for plane in range(group):
            middle = values[now, plane]
            got = scaled[plane] - middle
            for index, other in enumerate(around(lambda at: values[now, at], plane)):
                got = got + weights[index, plane] * other
            moved = carry * update[plane] + gain * got
            update[plane] = moved
            values[later, plane] = middle + moved


def finish(at, iterate, weights, scaled, level, update, middle, put):
    count = iterate.shape[0]

    @planes_of(count - 2, level)
    def _(plane):
        value = iterate[plane + 1]
        got = FIRST * defect(
            scaled[at + plane + 1],
            [weights[index, at + plane + 1] for index in range(6)],
            value,
            iterate[plane],
            iterate[plane + 2],
        )
        update[plane] = got
        middle[plane] = value + got

    @planes_of(count - 4, level)
    def _(plane):
        value = middle[plane + 1]
        got = defect(
            scaled[at + plane + 2],
            [weights[index, at + plane + 2] for index in range(6)],
            value,
            middle[plane],
            middle[plane + 2],
        )
        put(plane, value + (CARRY * update[plane + 1] + GAIN * got))


def up(
    pos, gathered, weights2, scaled2, iterate2, weights1, scaled1, iterate1,
    weights0, diagonal0, scaled0, iterate0, outer0, solved, left_over,
    whole3, weights3, scaled3, update3, values3,
    thin3, error2, value2, update2, middle2, out2,
    tall1, value1, update1, middle1, out1,
    tall0, value0, update0, middle0, out0,
):
    bottom(gathered, whole3, weights3, scaled3, update3, values3)
    group, rows = weights3.shape[1], weights3.shape[2]
    at_x, at_y, at_z = 4 * pos[0], 16 * pos[1], pos[2]
    last = (BOTTOM - 1) % 2

    lane = lane_of((8, 128))
    near = lax.rem(lane, 64)
    fits = ((near < 16) | ((near < 20) & (pos[1] < 3)) | ((near >= 60) & (pos[1] > 0))).astype(F32)
    first_row, last_row = (pos[0] > 0).astype(F32), (pos[0] < pos[3] - 1).astype(F32)
    low = row_of((8, 128)) < 4
    own = jnp.where(low, fits, fits * last_row)
    left = jnp.where(low, 0.0, fits * first_row)
    for plane in range(group):
        moved = pltpu.roll(values3[last, plane], lax.rem(rows - at_x, rows), 0)
        both = jnp.concatenate([moved[0:8], moved[rows - 8 :]], axis=0)
        both = pltpu.roll(both, lax.rem(128 - at_y, 128), 1)
        ahead, behind = both[0:8] * own, both[8:16] * left
        for start in (0, 1):
            thin3[plane, pl.ds(start, 8, stride=2), :] = ahead
            thin3[plane, pl.ds(16 + start, 4, stride=2), :] = behind[4:8]

    def to_level2(row, lane):
        side, within = lane // 128, lax.rem(lane, 128)
        place = jnp.where(within < 64, within, within - 128)
        source = jnp.where(side == 0, lax.rem(row, 128), lax.rem(row + 64, 128))
        source = jnp.where(source < 64, source, source - 128)
        return (source == lax.shift_right_arithmetic(place, 1)) & ((within < 40) | (within >= 120))

    spread = dot(thin3[...].reshape(group * 24, 128), matrix((128, 256), to_level2)).reshape(group, 24, 256)
    for plane in range(group):
        for side in range(2):
            error2[side * group + plane + 2] = spread[plane, :, 128 * side : 128 * side + 128]
    for end in (0, 2 * group + 2):
        for plane in range(2):
            error2[end + plane] = jnp.zeros((24, 128), F32)

    for plane in range(10):
        value2[plane] = iterate2[2 * at_z + plane] + error2[at_z + plane // 2]

    def put2(plane, value):
        out2[plane] = value

    finish(2 * at_z, value2, weights2, scaled2, 2, update2, middle2, put2)

    def to_level1(row, lane):
        place = jnp.where(lane < 96, lane, lane - 128)
        source = lax.shift_right_arithmetic(place, 1)
        return (jnp.where(row < 64, row, row - 128) == source) & ((lane < 80) | (lane >= 112))

    wide1 = matrix((128, 128), to_level1)
    for plane in range(6):
        tall1[plane, pl.ds(0, 24, stride=2), :] = out2[plane]
        tall1[plane, pl.ds(1, 24, stride=2), :] = out2[plane]
    spread = dot(tall1[...].reshape(6 * 48, 128), wide1).reshape(6, 48, 128)
    for plane in range(12):
        value1[plane] = iterate1[4 * at_z + plane] + spread[plane // 2]

    def put1(plane, value):
        out1[plane] = value

    finish(4 * at_z, value1, weights1, scaled1, 1, update1, middle1, put1)

    def to_level0(row, lane):
        place = jnp.where(lane < 192, lane, lane - 256)
        source = lax.shift_right_arithmetic(place, 1)
        return (jnp.where(row < 96, row, row - 128) == source) & ((lane < 136) | (lane >= 248))

    wide0 = matrix((128, 256), to_level0)
    for plane in range(8):
        value = out1[plane]
        tall0[plane, pl.ds(0, 24, stride=2), :] = value[0:24]
        tall0[plane, pl.ds(1, 24, stride=2), :] = value[0:24]
        tall0[plane, pl.ds(40, 4, stride=2), :] = value[44:48]
        tall0[plane, pl.ds(41, 4, stride=2), :] = value[44:48]

    @planes_of(8, 1)
    def _(plane):
        value = dot(tall0[plane], wide0)
        out0[2 * plane] = value
        out0[2 * plane + 1] = value

    @planes_of(iterate0.shape[0], 0)
    def _(plane):
        value0[plane + 2] = iterate0[plane] + out0[plane + 3]

    count = value0.shape[0]
    for at, plane in enumerate((0, 1, count - 2, count - 1)):
        value0[plane] = outer0[at] + out0[plane + 1]


    @planes_of(count - 2, 0)
    def _(plane):
        value = value0[plane + 1]
        got = FIRST * defect(
            scaled0[plane],
            [weights0[index, plane] for index in range(6)],
            value,
            value0[plane],
            value0[plane + 2],
        )
        update0[plane] = got
        middle0[plane] = value + got

    @planes_of(count - 4, 0)
    def _(plane):
        value = middle0[plane + 1]
        got = defect(
            scaled0[plane + 1],
            [weights0[index, plane + 1] for index in range(6)],
            value,
            middle0[plane],
            middle0[plane + 2],
        )
        out0[plane] = value + (CARRY * update0[plane + 1] + GAIN * got)

    @planes_of(count - 6, 0)
    def _(plane):
        value = out0[plane + 1]
        solved[plane] = value[0:32, 0:128]
        left_over[plane] = residual0(
            weights0, diagonal0, scaled0, value, out0[plane], out0[plane + 2], plane + 2, 128
        )


def call(body, name, outs, scratch, pos, args):
    vmem = pl.BlockSpec(memory_space=pltpu.VMEM)
    smem = [pl.BlockSpec(memory_space=pltpu.SMEM)] if pos is not None else []
    operands = ([pos] if pos is not None else []) + list(args)
    return pl.pallas_call(
        body,
        name=name,
        out_shape=[jax.ShapeDtypeStruct(shape, F32) for shape in outs],
        in_specs=smem + [vmem] * len(args),
        out_specs=[vmem] * len(outs),
        scratch_shapes=[pltpu.VMEM(shape, F32) for shape in scratch],
        compiler_params=pltpu.CompilerParams(vmem_limit_bytes=32 * 2**20),
    )(*operands)


def exchange(up_values, down_values, axis, ring):
    peers = lax.axis_size(axis)
    up_pairs = [(i, (i + 1) % peers) for i in range(peers if ring else peers - 1)]
    down_pairs = [(j, i) for i, j in up_pairs]
    return lax.ppermute(up_values, axis, up_pairs), lax.ppermute(down_values, axis, down_pairs)


def on_device(right_side, acoef, beta):
    ranks, turns, files = [lax.axis_size(axis) for axis in AXES]
    pos = jnp.stack([lax.axis_index(axis) for axis in AXES] + [jnp.int32(ranks)]).astype(jnp.int32)
    planes = right_side.shape[0]
    arrays = (right_side, acoef, beta)

    own = jnp.stack(arrays)
    last, first = call(packx, "packx", [(3, planes, 8, 128)] * 2, [], None, (own,))
    xb, xa = exchange(last, first, "gx", True)
    last, first = call(packz, "packz", [(sum(REACH), 40, 128)] * 2, [], pos, (own, xb, xa))
    zb, za = exchange(last, first, "gz", False)
    depth = planes + 2 * DEEP
    tiles = max(tile for _, _, tile, _, _ in slots(depth)) + 1
    whole0, left, right = call(
        pack0, "pack0", [(3, depth, 48, 128)] + [(tiles, 40, 128)] * 2, [], pos, (own, xb, xa, zb, za)
    )
    before0, after0 = exchange(right, left, "gy", False)
    plane0 = (48, 256)
    half = planes // 2
    iterate0, message, weights0, diagonal0, scaled0 = call(
        down0,
        "down0",
        [(depth - 8,) + plane0, (files, 36 * half, 128), (6, depth - 6) + plane0] + [(depth - 6,) + plane0] * 2,
        [(3, depth) + plane0, (2, 3 * half, 32, 128)],
        None,
        (whole0, before0, after0),
    )

    whole1 = lax.all_to_all(message, "gz", 0, 0)
    xb, xa = exchange(whole1, whole1, "gx", True)
    depth1 = files * half
    outer0 = call(
        rest0,
        "rest0",
        [(4,) + plane0],
        [(3, depth) + plane0],
        None,
        (whole0, before0, after0, weights0, scaled0, whole1),
    )[0]
    plane1, plane2 = (48, 128), (24, 128)
    depth2 = depth1 // 2
    group = depth2 // 4
    tall1, tall2 = (depth1 + 8,) + plane1, (depth2 + 8,) + plane2
    message, weights1, scaled1, iterate1, weights2, scaled2, iterate2 = call(
        down1,
        "down1",
        [(ranks, 16, 128), (6,) + tall1, tall1, tall1, (6,) + tall2, tall2, tall2],
        [(3,) + tall1, tall1, (depth1 + 2,) + plane1, (3 * depth2,) + plane1]
        + [(3,) + tall2, tall2, (depth2 + 2,) + plane2, (3 * depth2 // 2, 8, 128)]
        + [(3 * depth2,) + plane2, (2 * group, 16, 128)],
        pos,
        (whole1, xb, xa, outer0),
    )

    gathered = lax.all_to_all(message, "gx", 0, 0)
    gathered = call(packy, "packy", [(turns, 12 * ranks, 128)], [], None, (gathered,))[0]
    gathered = lax.all_to_all(gathered, "gy", 0, 0)

    rows3 = 4 * ranks
    plane3 = (rows3, 128)
    solved, left_over = call(
        up,
        "up",
        [right_side.shape, right_side.shape],
        [(3, group) + plane3, (6, group) + plane3, (group,) + plane3, (group,) + plane3, (2, group) + plane3]
        + [(group,) + plane2, (2 * group + 4,) + plane2, (10,) + plane2, (8,) + plane2, (8,) + plane2, (6,) + plane2]
        + [(6,) + plane1, (12,) + plane1, (10,) + plane1, (10,) + plane1, (8,) + plane1]
        + [(8,) + plane1, (depth - 4,) + plane0, (depth - 6,) + plane0, (depth - 6,) + plane0, (depth - 2,) + plane0],
        pos,
        (gathered, weights2, scaled2, iterate2, weights1, scaled1, iterate1)
        + (weights0, diagonal0, scaled0, iterate0, outer0),
    )
    return solved, left_over


def solution(mesh):
    spec = P("gz", "gx", "gy")
    return jax.shard_map(
        on_device, mesh=mesh, in_specs=(spec, spec, spec), out_specs=(spec, spec), check_vma=False
    )
```

```python
import functools

import jax
import jax.numpy as jnp
from jax import lax
from jax.experimental import pallas as pl
from jax.experimental.pallas import tpu as pltpu
from jax.sharding import PartitionSpec as P

LEVELS = 4
SWEEPS = 2
BOTTOM = 16

smooth_low = 0.3
bottom_low = 0.05
upper_bound = 2.0
face_scale = 1.0 / 6.0

F32 = jnp.float32
AXES = ("gx", "gy", "gz")
REACH = (4, 4, 5)
DEEP = 5


def chebyshev(steps, lower):
    centre = (upper_bound + lower) / 2.0
    half_width = (upper_bound - lower) / 2.0
    sigma = centre / half_width
    rho = 1.0 / sigma
    out = [(0.0, 1.0 / centre)]
    for _ in range(1, steps):
        rho_next = 1.0 / (2.0 * sigma - rho)
        out.append((rho_next * rho, 2.0 * rho_next / half_width))
        rho = rho_next
    return out


(_, FIRST), (CARRY, GAIN) = chebyshev(SWEEPS, smooth_low)


def roll(value, shift, axis):
    shift %= value.shape[axis]
    return pltpu.roll(value, shift, axis) if shift else value


def lane_of(shape):
    return lax.broadcasted_iota(jnp.int32, shape, 1)


def row_of(shape):
    return lax.broadcasted_iota(jnp.int32, shape, 0)


def sides(value):
    return [roll(value, 1, 0), roll(value, -1, 0), roll(value, 1, 1), roll(value, -1, 1)]


def scale_of(level):
    return face_scale * 0.25**level * 0.5


def coefficients(beta, below, above, acoef, level):
    weights = [scale_of(level) * (beta + other) for other in [below, above] + sides(beta)]
    diagonal = acoef
    for weight in weights:
        diagonal = diagonal + weight
    inside = beta > 0.0
    inverse = jnp.where(inside, 1.0 / jnp.where(inside, diagonal, 1.0), 0.0)
    return [weight * inverse for weight in weights], diagonal, inverse


def defect(scaled, weights, value, below, above):
    result = scaled - value
    for weight, other in zip(weights, [below, above] + sides(value)):
        result = result + weight * other
    return result


def dot(left, right):
    right = right.astype(jnp.bfloat16)
    high = left.astype(jnp.bfloat16)
    rest = left - high.astype(F32)
    middle = rest.astype(jnp.bfloat16)
    low = (rest - middle.astype(F32)).astype(jnp.bfloat16)
    total = jnp.dot(low, right, preferred_element_type=F32)
    total = total + jnp.dot(middle, right, preferred_element_type=F32)
    return total + jnp.dot(high, right, preferred_element_type=F32)


def matrix(shape, rule, value=1.0):
    return jnp.where(rule(row_of(shape), lane_of(shape)), value, 0.0).astype(F32)


def copies(ref, value):
    for index in range(ref.shape[0]):
        ref[index] = value


def away(plane, depth):
    return max(DEEP - plane, plane - (depth - 1 - DEEP), 0)


def slots(depth):
    wide, narrow = [], []
    for index, reach in enumerate(REACH):
        for plane in range(depth):
            if away(plane, depth) < reach:
                (wide if away(plane, depth) <= reach - 2 else narrow).append((index, plane))
    out = [(index, plane, at // 4, 32 * (at % 4), 32) for at, (index, plane) in enumerate(wide)]
    first = -(-len(wide) // 4)
    return out + [(index, plane, first + at // 16, 8 * (at % 16), 8) for at, (index, plane) in enumerate(narrow)]


def masked(pos, xb, xa, index):
    before = jnp.where(pos[0] > 0, xb[index], 0.0)
    return before, jnp.where(pos[0] < pos[3] - 1, xa[index], 0.0)


def packx(own, last, first):
    last[...] = own[:, :, 24:]
    first[...] = own[:, :, :8]


def packz(pos, own, xb, xa, last, first):
    planes, at = own.shape[1], 0
    four = lax.broadcasted_iota(jnp.int32, xb.shape[1:], 1) < 4
    for index, reach in enumerate(REACH):
        before, after = masked(pos, xb, xa, index)
        ends = jnp.where(four, after, before)
        last[at : at + reach, 0:32, :] = own[index, planes - reach :]
        last[at : at + reach, 32:40, :] = ends[planes - reach :]
        first[at : at + reach, 0:32, :] = own[index, :reach]
        first[at : at + reach, 32:40, :] = ends[:reach]
        at += reach


def pack0(pos, own, xb, xa, zb, za, whole, left, right):
    planes = own.shape[1]
    depth = planes + 2 * DEEP
    at = 0
    for index, reach in enumerate(REACH):
        for plane in range(DEEP - reach):
            for end in (plane, depth - 1 - plane):
                whole[index, end] = jnp.zeros((48, 128), F32)
        for ref, start in ((zb, DEEP - reach), (za, DEEP + planes)):
            whole[index, start : start + reach, 0:40, :] = ref[at : at + reach]
            whole[index, start : start + reach, 40:48, :] = ref[at : at + reach, 32:40, :]
        before, after = masked(pos, xb, xa, index)
        whole[index, DEEP : DEEP + planes, 0:32, :] = own[index]
        whole[index, DEEP : DEEP + planes, 32:40, :] = after
        whole[index, DEEP : DEEP + planes, 40:48, :] = before
        at += reach
    lane = lane_of((40, 128))
    four = row_of((8, 128)) < 4
    low, high = {}, {}
    for index, plane, tile, to, lanes in slots(depth):
        ends = jnp.where(four, whole[index, plane, 32:40, :], whole[index, plane, 40:48, :])
        value = jnp.concatenate([whole[index, plane, 0:32, :], ends], axis=0)
        moved, back = roll(value, to, 1), (to - lanes) % 128
        zero = jnp.zeros((40, 128), F32)
        low[tile] = jnp.where((lane >= to) & (lane < to + lanes), moved, low.get(tile, zero))
        high[tile] = jnp.where((lane >= back) & (lane < back + lanes), moved, high.get(tile, zero))
    for tile in low:
        left[tile] = low[tile]
        right[tile] = high[tile]


def unpack0(whole, before, after, ext, wanted):
    lane = lane_of((40, 128))
    there = {(index, plane): rest for index, plane, *rest in slots(whole.shape[1])}
    for index, plane in wanted:
        ext[index, plane, :, 0:128] = whole[index, plane]
        if (index, plane) not in there:
            ext[index, plane, :, 128:256] = jnp.zeros((48, 128), F32)
            continue
        tile, to, lanes = there[index, plane]
        value = roll(jnp.where((lane >= to) & (lane < to + lanes), after[tile], before[tile]), -to, 1)
        value = jnp.where((lane < lanes) | (lane >= 128 - lanes), value, 0.0)
        ext[index, plane, 0:40, 128:256] = value
        ext[index, plane, 40:48, 128:256] = value[32:40]


def planes_of(count, level, start=0):
    most = (12, 32, 16)[level]
    return pl.loop(start, start + count, unroll=max(n for n in range(1, most + 1) if count % n == 0))


def coefficients0(ext, plane):
    got, middle, inverse = coefficients(ext[2, plane], ext[2, plane - 1], ext[2, plane + 1], ext[1, plane], 0)
    return got, middle, ext[0, plane] * inverse


def first_sweeps(weights, scaled, below, middle, above):
    value = FIRST * middle
    return value + (CARRY * value + GAIN * defect(scaled, weights, value, FIRST * below, FIRST * above))


def residual0(weights, diagonal, scaled, value, below, above, at, lanes):
    cut = lambda array: array[0:32, 0:lanes]
    result = scaled[at, 0:32, 0:lanes] - cut(value)
    for index, other in enumerate([below, above] + sides(value)):
        result = result + weights[index, at, 0:32, 0:lanes] * cut(other)
    return diagonal[at, 0:32, 0:lanes] * result


def down0(whole, before, after, iterate, message, weights, diagonal, scaled, ext, sums):
    depth = whole.shape[1]
    wanted = [(index, plane) for index in range(2) for plane in range(3, depth - 3)]
    unpack0(whole, before, after, ext, wanted + [(2, plane) for plane in range(2, depth - 2)])

    @planes_of(diagonal.shape[0], 0)
    def _(plane):
        got, diagonal[plane], scaled[plane] = coefficients0(ext, plane + 3)
        for index in range(6):
            weights[index, plane] = got[index]

    @planes_of(iterate.shape[0], 0)
    def _(plane):
        faces = [weights[index, plane + 1] for index in range(6)]
        iterate[plane] = first_sweeps(faces, scaled[plane + 1], scaled[plane], scaled[plane + 1], scaled[plane + 2])

    planes = whole.shape[1] - 2 * DEEP

    def left_over(plane):
        return residual0(
            weights, diagonal, scaled, iterate[plane + 1], iterate[plane], iterate[plane + 2], plane + 2, 256
        )

    half = planes // 2

    @planes_of(half, 0)
    def _(plane):
        pairs = [left_over(2 * plane) + left_over(2 * plane + 1)]
        for index in (1, 2):
            low = ext[index, DEEP + 2 * plane, 0:32, :]
            pairs.append(low + ext[index, DEEP + 2 * plane + 1, 0:32, :])
        for index, value in enumerate(pairs):
            sums[0, index * half + plane] = value[:, 0:128]
            sums[1, index * half + plane] = value[:, 128:256]

    def rows_of(side, places):
        tall = [
            sums[side, place, pl.ds(0, 16, stride=2), :] + sums[side, place, pl.ds(1, 16, stride=2), :]
            for place in places
        ]
        return jnp.concatenate(tall, axis=0)

    even = matrix((128, 128), lambda row, lane: lane == row // 2, 0.125)
    odd = matrix((128, 128), lambda row, lane: lane == row // 2 + 64, 0.125)
    middle = dot(rows_of(0, range(0, 3 * half, 2)), even) + dot(rows_of(0, range(1, 3 * half, 2)), odd)
    ends = None
    for plane in range(half):

        def rule(row, lane, ahead=-32 * plane % 128, behind=(48 - 32 * plane) % 128):
            return ((row < 32) & (lane == ahead + row // 2)) | ((row >= 96) & (lane == behind + (row - 96) // 2))

        got = dot(rows_of(1, range(plane, 3 * half, half)), matrix((128, 128), rule, 0.125))
        ends = got if ends is None else ends + got
    copies(message, jnp.concatenate([middle, ends], axis=0))


def rest0(whole, before, after, weights, scaled, later, outer, ext):
    depth = whole.shape[1]
    ends = ((1, 2), (depth - 2, depth - 3))
    wanted = [(index, plane) for index in range(2) for end in ends for plane in end]
    unpack0(whole, before, after, ext, wanted + [(2, p) for p in (0, 1, 2, 3, depth - 4, depth - 3, depth - 2, depth - 1)])
    count = scaled.shape[0]
    for side, (far, near) in enumerate(ends):
        at, beside = (0, 1) if side == 0 else (count - 1, count - 2)
        farthest = coefficients0(ext, far)[2]
        faces, _, middle = coefficients0(ext, near)
        around = (farthest, scaled[at]) if side == 0 else (scaled[at], farthest)
        outer[3 * side] = first_sweeps(faces, middle, around[0], middle, around[1])
        faces = [weights[index, at] for index in range(6)]
        around = (middle, scaled[beside]) if side == 0 else (scaled[beside], middle)
        outer[1 + side] = first_sweeps(faces, scaled[at], around[0], scaled[at], around[1])


def unpack1(ref, there, put):
    lane = lane_of((16, 128))
    per = ref.shape[1] // 36

    @pl.loop(0, ref.shape[0], unroll=ref.shape[0])
    def _(source):
        for index in range(3):
            ends = ref[source, 96 + 16 * index : 112 + 16 * index, :]
            for plane in range(per):
                at = (2 * index + plane // 2) * 16
                value = roll(ref[source, at : at + 16, :], 64 * (plane % 2), 1)
                halo = jnp.where((lane < 80) | (lane >= 112), roll(ends, 64 + 32 * plane, 1), 0.0)
                value = jnp.where(lane < 64, value, halo)
                if there is not None:
                    value = jnp.where(there, value, 0.0)
                put(index, source * per + plane, value)


def pass_all(weights, scaled, value, out, count, combine, level):
    @planes_of(count, level)
    def _(plane):
        middle = value[plane + 1]
        got = defect(
            scaled[plane + 4],
            [weights[index, plane + 4] for index in range(6)],
            middle,
            value[plane],
            value[plane + 2],
        )
        out(plane, combine(middle, got))


def prepare(ext, weights, diagonal, scaled, level):
    shape = scaled.shape[1:]
    count = scaled.shape[0] - 8
    for end in (0, count + 4):
        for plane in range(4):
            scaled[end + plane] = jnp.zeros(shape, F32)
            for index in range(6):
                weights[index, end + plane] = jnp.zeros(shape, F32)

    @planes_of(count, level, 4)
    def _(at):
        got, middle, inverse = coefficients(ext[2, at], ext[2, at - 1], ext[2, at + 1], ext[1, at], level)
        for index in range(6):
            weights[index, at] = got[index]
        diagonal[at] = middle
        scaled[at] = ext[0, at] * inverse


def down1(
    pos, own, xb, xa, earlier, message, weights1, scaled1, iterate1, weights2, scaled2, iterate2,
    ext1, diagonal1, start1, sums1, ext2, diagonal2, start2, sums2, thin, thick,
):
    depth = scaled1.shape[0] - 8
    for index in range(3):
        for end in (0, depth + 4):
            for plane in range(4):
                ext1[index, end + plane] = jnp.zeros((48, 128), F32)

    for start, ref, there in ((0, own, None), (16, xa, pos[0] < pos[3] - 1), (32, xb, pos[0] > 0)):

        def put(index, plane, value, start=start):
            ext1[index, plane + 4, start : start + 16, :] = value

        unpack1(ref, there, put)
    prepare(ext1, weights1, diagonal1, scaled1, 1)
    start1[0] = jnp.zeros((48, 128), F32)
    start1[depth + 1] = jnp.zeros((48, 128), F32)

    @planes_of(depth, 1)
    def _(plane):
        start1[plane + 1] = FIRST * scaled1[plane + 4]

    for end in (0, depth + 4):
        for plane in range(4):
            iterate1[end + plane] = jnp.zeros((48, 128), F32)

    def put1(plane, value):
        iterate1[plane + 4] = value

    pass_all(weights1, scaled1, start1, put1, depth, lambda value, got: value + (CARRY * value + GAIN * got), 1)

    half = depth // 2

    @planes_of(half, 1)
    def _(pair):
        total = None
        for plane in (2 * pair, 2 * pair + 1):
            got = diagonal1[plane + 4] * defect(
                scaled1[plane + 4],
                [weights1[index, plane + 4] for index in range(6)],
                iterate1[plane + 4],
                iterate1[plane + 3],
                iterate1[plane + 5],
            )
            total = got if total is None else total + got
        sums1[pair] = total
        for index in (1, 2):
            sums1[index * half + pair] = ext1[index, 2 * pair + 4] + ext1[index, 2 * pair + 5]

    @planes_of(3 * half, 1)
    def _(plane):
        thin[plane] = sums1[plane, pl.ds(0, 24, stride=2), :] + sums1[plane, pl.ds(1, 24, stride=2), :]

    def to_level2(row, lane):
        place = jnp.where(lane < 64, lane, lane - 128)
        source = lax.shift_right_arithmetic(jnp.where(row < 96, row, row - 128), 1)
        return (source == place) & ((row < 80) | (row >= 112))

    level2 = matrix((128, 128), to_level2, 0.125)
    for index in range(3):
        values = thin[index * half : (index + 1) * half].reshape(half * 24, 128)
        ext2[index, 4 : 4 + half] = dot(values, level2).reshape(half, 24, 128)
        for end in (0, half + 4):
            for plane in range(4):
                ext2[index, end + plane] = jnp.zeros((24, 128), F32)

    prepare(ext2, weights2, diagonal2, scaled2, 2)
    start2[0] = jnp.zeros((24, 128), F32)
    start2[half + 1] = jnp.zeros((24, 128), F32)

    @pl.loop(0, half)
    def _(plane):
        start2[plane + 1] = FIRST * scaled2[plane + 4]

    for end in (0, half + 4):
        for plane in range(4):
            iterate2[end + plane] = jnp.zeros((24, 128), F32)

    def put2(plane, value):
        iterate2[plane + 4] = value

    pass_all(weights2, scaled2, start2, put2, half, lambda value, got: value + (CARRY * value + GAIN * got), 2)

    quarter = half // 2
    group = quarter // 2
    place2 = []
    for plane in range(quarter):
        to = 64 * (plane // group) + 16 * lax.rem(pos[1] + plane % group, 4)
        place2.append(matrix((128, 128), lambda row, lane, to=to: (row < 32) & (lane == row // 2 + to), 0.125))
        thick[plane] = jnp.zeros((16, 128), F32)
    for index in range(3):
        for plane in range(quarter):
            if index == 0:
                total = None
                for at in (2 * plane, 2 * plane + 1):
                    got = diagonal2[at + 4] * defect(
                        scaled2[at + 4],
                        [weights2[face, at + 4] for face in range(6)],
                        iterate2[at + 4],
                        iterate2[at + 3],
                        iterate2[at + 5],
                    )
                    total = got if total is None else total + got
                total = total[0:8]
            else:
                total = ext2[index, 2 * plane + 4, 0:8, :] + ext2[index, 2 * plane + 5, 0:8, :]
            at = index * quarter + plane
            sums2[at] = total
            thick[plane, pl.ds(index, 4, stride=3), :] = (
                sums2[at, pl.ds(0, 4, stride=2), :] + sums2[at, pl.ds(1, 4, stride=2), :]
            )
    result = dot(thick[0], place2[0])
    for plane in range(1, quarter):
        result = result + dot(thick[plane], place2[plane])
    copies(message, result[0:12])


def packy(pieces, message):
    for at in range(pieces.shape[0]):
        copies(message.at[:, 12 * at : 12 * at + 12, :], pieces[at, 0:12, :])


def bottom(gathered, whole, weights, scaled, update, values):
    group = weights.shape[1]
    rows = weights.shape[2]
    shape = (rows, 128)
    row, lane = row_of(shape), lane_of(shape)
    column = lax.rem(lane, 64)
    quarter = column // 16
    for index in range(3):
        pieces = [gathered[source, pl.ds(index, rows, stride=3), :] for source in range(4)]
        for plane in range(group):
            total = pieces[0]
            for source in range(1, 4):
                total = jnp.where(quarter == (source + plane) % 4, pieces[source], total)
            if plane:
                near, far = roll(total, -16 * plane, 1), roll(total, 64 - 16 * plane, 1)
                total = jnp.where(quarter + plane < 4, near, far)
            whole[index, plane] = total

    def plane_at(index, plane):
        return whole[index, plane]

    def around(get, plane):
        middle = get(plane)
        below = get(plane - 1) if plane else roll(get(group - 1), 64, 1)
        above = get(plane + 1) if plane < group - 1 else roll(get(0), 64, 1)
        return [below, above] + sides(middle)

    for plane in range(group):
        beta = plane_at(2, plane)
        masks = [
            (lane >= 64) if plane == 0 else None,
            (lane < 64) if plane == group - 1 else None,
            row > 0,
            row < rows - 1,
            column > 0,
            column < 63,
        ]
        near = around(lambda at: plane_at(2, at), plane)
        near = [other if mask is None else jnp.where(mask, other, 0.0) for other, mask in zip(near, masks)]
        faces = [scale_of(3) * (beta + other) for other in near]
        diagonal = plane_at(1, plane)
        for face in faces:
            diagonal = diagonal + face
        inverse = 1.0 / diagonal
        for index, (face, mask) in enumerate(zip(faces, masks)):
            face = face * inverse
            weights[index, plane] = face if mask is None else jnp.where(mask, face, 0.0)
        scaled[plane] = plane_at(0, plane) * inverse

    steps = chebyshev(BOTTOM, bottom_low)
    for plane in range(group):
        value = steps[0][1] * scaled[plane]
        update[plane] = value
        values[0, plane] = value
    for step, (carry, gain) in enumerate(steps[1:]):
        now, later = step % 2, (step + 1) % 2
        for plane in range(group):
            middle = values[now, plane]
            got = scaled[plane] - middle
            for index, other in enumerate(around(lambda at: values[now, at], plane)):
                got = got + weights[index, plane] * other
            moved = carry * update[plane] + gain * got
            update[plane] = moved
            values[later, plane] = middle + moved


def finish(at, iterate, weights, scaled, level, update, middle, put):
    count = iterate.shape[0]

    @planes_of(count - 2, level)
    def _(plane):
        value = iterate[plane + 1]
        got = FIRST * defect(
            scaled[at + plane + 1],
            [weights[index, at + plane + 1] for index in range(6)],
            value,
            iterate[plane],
            iterate[plane + 2],
        )
        update[plane] = got
        middle[plane] = value + got

    @planes_of(count - 4, level)
    def _(plane):
        value = middle[plane + 1]
        got = defect(
            scaled[at + plane + 2],
            [weights[index, at + plane + 2] for index in range(6)],
            value,
            middle[plane],
            middle[plane + 2],
        )
        put(plane, value + (CARRY * update[plane + 1] + GAIN * got))


def up(
    pos, gathered, weights2, scaled2, iterate2, weights1, scaled1, iterate1,
    weights0, diagonal0, scaled0, iterate0, outer0, solved, left_over,
    whole3, weights3, scaled3, update3, values3,
    thin3, error2, value2, update2, middle2, out2,
    tall1, value1, update1, middle1, out1,
    tall0, value0, update0, middle0, out0,
):
    bottom(gathered, whole3, weights3, scaled3, update3, values3)
    group, rows = weights3.shape[1], weights3.shape[2]
    at_x, at_y, at_z = 4 * pos[0], 16 * pos[1], pos[2]
    last = (BOTTOM - 1) % 2

    lane = lane_of((8, 128))
    near = lax.rem(lane, 64)
    fits = ((near < 16) | ((near < 20) & (pos[1] < 3)) | ((near >= 60) & (pos[1] > 0))).astype(F32)
    first_row, last_row = (pos[0] > 0).astype(F32), (pos[0] < pos[3] - 1).astype(F32)
    low = row_of((8, 128)) < 4
    own = jnp.where(low, fits, fits * last_row)
    left = jnp.where(low, 0.0, fits * first_row)
    for plane in range(group):
        moved = pltpu.roll(values3[last, plane], lax.rem(rows - at_x, rows), 0)
        both = jnp.concatenate([moved[0:8], moved[rows - 8 :]], axis=0)
        both = pltpu.roll(both, lax.rem(128 - at_y, 128), 1)
        ahead, behind = both[0:8] * own, both[8:16] * left
        for start in (0, 1):
            thin3[plane, pl.ds(start, 8, stride=2), :] = ahead
            thin3[plane, pl.ds(16 + start, 4, stride=2), :] = behind[4:8]

    def to_level2(row, lane):
        side, within = lane // 128, lax.rem(lane, 128)
        place = jnp.where(within < 64, within, within - 128)
        source = jnp.where(side == 0, lax.rem(row, 128), lax.rem(row + 64, 128))
        source = jnp.where(source < 64, source, source - 128)
        return (source == lax.shift_right_arithmetic(place, 1)) & ((within < 40) | (within >= 120))

    spread = dot(thin3[...].reshape(group * 24, 128), matrix((128, 256), to_level2)).reshape(group, 24, 256)
    for plane in range(group):
        for side in range(2):
            error2[side * group + plane + 2] = spread[plane, :, 128 * side : 128 * side + 128]
    for end in (0, 2 * group + 2):
        for plane in range(2):
            error2[end + plane] = jnp.zeros((24, 128), F32)

    for plane in range(10):
        value2[plane] = iterate2[2 * at_z + plane] + error2[at_z + plane // 2]

    def put2(plane, value):
        out2[plane] = value

    finish(2 * at_z, value2, weights2, scaled2, 2, update2, middle2, put2)

    def to_level1(row, lane):
        place = jnp.where(lane < 96, lane, lane - 128)
        source = lax.shift_right_arithmetic(place, 1)
        return (jnp.where(row < 64, row, row - 128) == source) & ((lane < 80) | (lane >= 112))

    wide1 = matrix((128, 128), to_level1)
    for plane in range(6):
        tall1[plane, pl.ds(0, 24, stride=2), :] = out2[plane]
        tall1[plane, pl.ds(1, 24, stride=2), :] = out2[plane]
    spread = dot(tall1[...].reshape(6 * 48, 128), wide1).reshape(6, 48, 128)
    for plane in range(12):
        value1[plane] = iterate1[4 * at_z + plane] + spread[plane // 2]

    def put1(plane, value):
        out1[plane] = value

    finish(4 * at_z, value1, weights1, scaled1, 1, update1, middle1, put1)

    def to_level0(row, lane):
        place = jnp.where(lane < 192, lane, lane - 256)
        source = lax.shift_right_arithmetic(place, 1)
        return (jnp.where(row < 96, row, row - 128) == source) & ((lane < 136) | (lane >= 248))

    wide0 = matrix((128, 256), to_level0)
    for plane in range(8):
        value = out1[plane]
        tall0[plane, pl.ds(0, 24, stride=2), :] = value[0:24]
        tall0[plane, pl.ds(1, 24, stride=2), :] = value[0:24]
        tall0[plane, pl.ds(40, 4, stride=2), :] = value[44:48]
        tall0[plane, pl.ds(41, 4, stride=2), :] = value[44:48]

    @planes_of(8, 1)
    def _(plane):
        value = dot(tall0[plane], wide0)
        out0[2 * plane] = value
        out0[2 * plane + 1] = value

    @planes_of(iterate0.shape[0], 0)
    def _(plane):
        value0[plane + 2] = iterate0[plane] + out0[plane + 3]

    count = value0.shape[0]
    for at, plane in enumerate((0, 1, count - 2, count - 1)):
        value0[plane] = outer0[at] + out0[plane + 1]


    @planes_of(count - 2, 0)
    def _(plane):
        value = value0[plane + 1]
        got = FIRST * defect(
            scaled0[plane],
            [weights0[index, plane] for index in range(6)],
            value,
            value0[plane],
            value0[plane + 2],
        )
        update0[plane] = got
        middle0[plane] = value + got

    @planes_of(count - 4, 0)
    def _(plane):
        value = middle0[plane + 1]
        got = defect(
            scaled0[plane + 1],
            [weights0[index, plane + 1] for index in range(6)],
            value,
            middle0[plane],
            middle0[plane + 2],
        )
        out0[plane] = value + (CARRY * update0[plane + 1] + GAIN * got)

    @planes_of(count - 6, 0)
    def _(plane):
        value = out0[plane + 1]
        solved[plane] = value[0:32, 0:128]
        left_over[plane] = residual0(
            weights0, diagonal0, scaled0, value, out0[plane], out0[plane + 2], plane + 2, 128
        )


def call(body, name, outs, scratch, pos, args):
    vmem = pl.BlockSpec(memory_space=pltpu.VMEM)
    smem = [pl.BlockSpec(memory_space=pltpu.SMEM)] if pos is not None else []
    operands = ([pos] if pos is not None else []) + list(args)
    return pl.pallas_call(
        body,
        name=name,
        out_shape=[jax.ShapeDtypeStruct(shape, F32) for shape in outs],
        in_specs=smem + [vmem] * len(args),
        out_specs=[vmem] * len(outs),
        scratch_shapes=[pltpu.VMEM(shape, F32) for shape in scratch],
        compiler_params=pltpu.CompilerParams(vmem_limit_bytes=32 * 2**20),
    )(*operands)


def exchange(up_values, down_values, axis, ring):
    peers = lax.axis_size(axis)
    up_pairs = [(i, (i + 1) % peers) for i in range(peers if ring else peers - 1)]
    down_pairs = [(j, i) for i, j in up_pairs]
    return lax.ppermute(up_values, axis, up_pairs), lax.ppermute(down_values, axis, down_pairs)


def on_device(right_side, acoef, beta):
    ranks, turns, files = [lax.axis_size(axis) for axis in AXES]
    pos = jnp.stack([lax.axis_index(axis) for axis in AXES] + [jnp.int32(ranks)]).astype(jnp.int32)
    planes = right_side.shape[0]
    arrays = (right_side, acoef, beta)

    own = jnp.stack(arrays)
    last, first = call(packx, "packx", [(3, planes, 8, 128)] * 2, [], None, (own,))
    xb, xa = exchange(last, first, "gx", True)
    last, first = call(packz, "packz", [(sum(REACH), 40, 128)] * 2, [], pos, (own, xb, xa))
    zb, za = exchange(last, first, "gz", False)
    depth = planes + 2 * DEEP
    tiles = max(tile for _, _, tile, _, _ in slots(depth)) + 1
    whole0, left, right = call(
        pack0, "pack0", [(3, depth, 48, 128)] + [(tiles, 40, 128)] * 2, [], pos, (own, xb, xa, zb, za)
    )
    before0, after0 = exchange(right, left, "gy", False)
    plane0 = (48, 256)
    half = planes // 2
    iterate0, message, weights0, diagonal0, scaled0 = call(
        down0,
        "down0",
        [(depth - 8,) + plane0, (files, 36 * half, 128), (6, depth - 6) + plane0] + [(depth - 6,) + plane0] * 2,
        [(3, depth) + plane0, (2, 3 * half, 32, 128)],
        None,
        (whole0, before0, after0),
    )

    whole1 = lax.all_to_all(message, "gz", 0, 0)
    xb, xa = exchange(whole1, whole1, "gx", True)
    depth1 = files * half
    outer0 = call(
        rest0,
        "rest0",
        [(4,) + plane0],
        [(3, depth) + plane0],
        None,
        (whole0, before0, after0, weights0, scaled0, whole1),
    )[0]
    plane1, plane2 = (48, 128), (24, 128)
    depth2 = depth1 // 2
    group = depth2 // 4
    tall1, tall2 = (depth1 + 8,) + plane1, (depth2 + 8,) + plane2
    message, weights1, scaled1, iterate1, weights2, scaled2, iterate2 = call(
        down1,
        "down1",
        [(ranks, 12, 128), (6,) + tall1, tall1, tall1, (6,) + tall2, tall2, tall2],
        [(3,) + tall1, tall1, (depth1 + 2,) + plane1, (3 * depth2,) + plane1]
        + [(3,) + tall2, tall2, (depth2 + 2,) + plane2, (3 * depth2 // 2, 8, 128)]
        + [(3 * depth2,) + plane2, (2 * group, 16, 128)],
        pos,
        (whole1, xb, xa, outer0),
    )

    gathered = lax.all_to_all(message, "gx", 0, 0)
    gathered = call(packy, "packy", [(turns, 12 * ranks, 128)], [], None, (gathered,))[0]
    gathered = lax.all_to_all(gathered, "gy", 0, 0)

    rows3 = 4 * ranks
    plane3 = (rows3, 128)
    solved, left_over = call(
        up,
        "up",
        [right_side.shape, right_side.shape],
        [(3, group) + plane3, (6, group) + plane3, (group,) + plane3, (group,) + plane3, (2, group) + plane3]
        + [(group,) + plane2, (2 * group + 4,) + plane2, (10,) + plane2, (8,) + plane2, (8,) + plane2, (6,) + plane2]
        + [(6,) + plane1, (12,) + plane1, (10,) + plane1, (10,) + plane1, (8,) + plane1]
        + [(8,) + plane1, (depth - 4,) + plane0, (depth - 6,) + plane0, (depth - 6,) + plane0, (depth - 2,) + plane0],
        pos,
        (gathered, weights2, scaled2, iterate2, weights1, scaled1, iterate1)
        + (weights0, diagonal0, scaled0, iterate0, outer0),
    )
    return solved, left_over


def solution(mesh):
    spec = P("gz", "gx", "gy")
    return jax.shard_map(
        on_device, mesh=mesh, in_specs=(spec, spec, spec), out_specs=(spec, spec), check_vma=False
    )
```
